128 devices in a mesh: dp: 64 (over z_lo, y, x, core), chan: 2 (over z_hi).
Axes of the slice: x: 4, y: 4, z: 4 (z_hi: 2, z_lo: 2; z = z_hi * 2 + z_lo), core: 2. Of those that a mesh axis runs over, the one named last changes fastest.
Arguments:
- tokens: bfloat16 [32768, 768], P('dp', 'chan'), may hold values from -6 to 6
- lengths: int32 [64], P('dp'), may hold values from 1 to 512, 20480 in all
- norm_gain: float32 [2, 2, 768], P(None, None, 'chan'), may hold values from 0.1 to 1.9
- norm_bias: float32 [2, 2, 768], P(None, None, 'chan'), may hold values from -3 to 3
- in_weight: bfloat16 [2, 768, 3, 768], P(None, None, None, 'chan'), may hold values from -0.21875 to 0.21875
- in_bias: float32 [2, 3, 768], P(None, None, 'chan'), may hold values from -3 to 3
- short_weight: float32 [2, 3, 3, 768], P(None, None, None, 'chan'), may hold values from -3 to 3
- short_bias: float32 [2, 3, 768], P(None, None, 'chan'), may hold values from -3 to 3
- filter_first: float32 [2, 33, 64], replicated, may hold values from -1 to 1
- filter_inner: float32 [2, 2, 64, 64], replicated, may hold values from -1 to 1
- filter_biases: float32 [2, 3, 64], replicated, may hold values from -3.140625 to 3.140625
- filter_out: float32 [2, 64, 768], P(None, None, 'chan'), may hold values from -0.125 to 0.125
- filter_skip: float32 [2, 768], P(None, 'chan'), may hold values from -4 to 4
- out_weight: bfloat16 [2, 768, 768], P(None, 'chan'), may hold values from -0.21875 to 0.21875
- out_bias: float32 [2, 768], P(None, 'chan'), may hold values from -3 to 3
- up_weight: bfloat16 [2, 768, 3072], P(None, None, 'chan'), may hold values from -0.21875 to 0.21875
- up_bias: float32 [2, 3072], P(None, 'chan'), may hold values from -3 to 3
- down_weight: bfloat16 [2, 3072, 768], P(None, 'chan'), may hold values from -0.15625 to 0.15625
- down_bias: float32 [2, 768], P(None, 'chan'), may hold values from -3 to 3
- cotangent: bfloat16 [32768, 768], P('dp', 'chan'), may hold values from -6 to 6
Outputs:
- result: bfloat16 [32768, 768], P('dp', 'chan')
- grad_tokens: float32 [32768, 768], P('dp', 'chan')
- grad_norm_gain: float32 [2, 2, 768], P(None, None, 'chan')
- grad_norm_bias: float32 [2, 2, 768], P(None, None, 'chan')
- grad_in_weight: float32 [2, 768, 3, 768], P(None, None, None, 'chan')
- grad_in_bias: float32 [2, 3, 768], P(None, None, 'chan')
- grad_short_weight: float32 [2, 3, 3, 768], P(None, None, None, 'chan')
- grad_short_bias: float32 [2, 3, 768], P(None, None, 'chan')
- grad_filter_first: float32 [2, 33, 64], replicated
- grad_filter_inner: float32 [2, 2, 64, 64], replicated
- grad_filter_biases: float32 [2, 3, 64], replicated
- grad_filter_out: float32 [2, 64, 768], P(None, None, 'chan')
- grad_filter_skip: float32 [2, 768], P(None, 'chan')
- grad_out_weight: float32 [2, 768, 768], P(None, 'chan')
- grad_out_bias: float32 [2, 768], P(None, 'chan')
- grad_up_weight: float32 [2, 768, 3072], P(None, None, 'chan')
- grad_up_bias: float32 [2, 3072], P(None, 'chan')
- grad_down_weight: float32 [2, 3072, 768], P(None, 'chan')
- grad_down_bias: float32 [2, 768], P(None, 'chan')
The draws below stay inside these ranges and needn't reach their ends.
Inputs may be any that keep to these rules, and one draw needn't show every extreme that they name: `lengths`: valid tokens of a sequence fill the first slots of its 512 slots, and some sequence fills all of them.
All inputs are finite; a program needn't handle non-finite values. No bound on the sum of `lengths` on one device may be relied on, other than what follows from the above.
Results may differ from the reference program's by a relative error of at most 0.018.
Values may be sent and summed in bfloat16 or wider, within the bound.
No kernel may reach another device: no remote copies, remote signals or barrier semaphores. Data moves between devices by JAX's collectives and lax.ppermute only.
A program may use at most 256 MiB of HBM per device.

```python
import math
import jax
import jax.numpy as jnp
import numpy as np
from jax import lax

D = 768
FF = 3072
ORDER = 64
EMB = 33
LAYERS = 2
LEN = 512
SEQUENCES = 64
TOKENS = 32768


def block_scale(stream_key, dims, cuts, least, high):
    factor_of = 1.0
    for axis_at, blocks in cuts:
        draws = jax.random.uniform(jax.random.fold_in(jax.random.fold_in(stream_key, 6), axis_at), (blocks,), jnp.float32, least / len(cuts), high / len(cuts))
        factor_of = factor_of * jnp.repeat(jnp.exp(draws), dims[axis_at] // blocks).reshape((-1,) + (1,) * (len(dims) - 1 - axis_at))
    return factor_of


def split_up(number_of, total, reach, slope):
    portions = [(1 << 20) // math.isqrt(standing ** slope) + 1 for standing in range(2, number_of + 1)]
    surplus, counts = total - reach - (number_of - 1), [1] * (number_of - 1)
    while surplus > 0:
        free = [i for i in range(number_of - 1) if counts[i] < reach]
        pool, left = sum([portions[i] for i in free]), surplus
        for i in free:
            extra = min(reach - counts[i], max(1, left * portions[i] // pool), surplus)
            counts[i] = counts[i] + extra
            surplus = surplus - extra
    return np.array([reach] + counts)


def ragged_sizes(key, count, total, bound, slope):
    if count == 2:
        one = jax.random.randint(key, (), max(1, total - bound), min(bound, total - 1) + 1)
        return jnp.stack([one, total - one])
    sizes = jnp.asarray(split_up(count, total, bound, slope), jnp.int32)
    pairs = (count - 1) // 2
    source_of, receiver = sizes[1:1 + 2 * pairs:2], sizes[2:2 + 2 * pairs:2]
    slack = jnp.minimum(source_of - 1, bound - receiver)
    passed = jax.random.randint(jax.random.fold_in(key, 1), (pairs,), 0, 1 << 20) % (slack + 1)
    sizes = sizes.at[1:1 + 2 * pairs:2].set(source_of - passed).at[2:2 + 2 * pairs:2].set(receiver + passed)
    return sizes[jax.random.permutation(jax.random.fold_in(key, 2), count)]


def scatter_about(own_key, shape, scale, most, cuts=(), kind=jnp.bfloat16):
    result = jax.random.normal(own_key, shape, jnp.float32) * scale
    if len(cuts) > 0:
        result = block_scale(own_key, shape, cuts, -0.22, 0.18) * result
    return jnp.clip(result, min=-most, max=most).astype(kind)


def setup_inputs(seed: int = 0) -> dict:
    key_list = jax.random.split(jax.random.key(seed), 21)
    tokens = scatter_about(key_list[0], (TOKENS, D), 1.0, 6.0, ((0, 64), (1, 2)))
    lengths = ragged_sizes(key_list[1], SEQUENCES, SEQUENCES * LEN * 5 // 8, LEN, 1).astype(jnp.int32)
    norm_gain = jnp.clip(1.0 + 0.18 * jax.random.normal(key_list[2], (LAYERS, 2, D), jnp.float32), 0.1, 1.9)
    norm_bias = scatter_about(key_list[3], (LAYERS, 2, D), 0.5, 3.0, ((2, 2),), jnp.float32)
    in_weight = scatter_about(key_list[4], (LAYERS, D, 3, D), D ** -0.5, 0.21875, ((3, 2),))
    in_bias = scatter_about(key_list[5], (LAYERS, 3, D), 0.5, 3.0, ((2, 2),), jnp.float32)
    short_weight = scatter_about(key_list[6], (LAYERS, 3, 3, D), 0.6, 3.0, ((3, 2),), jnp.float32)
    short_bias = scatter_about(key_list[7], (LAYERS, 3, D), 0.5, 3.0, ((2, 2),), jnp.float32)
    filter_first = scatter_about(key_list[8], (LAYERS, EMB, ORDER), EMB ** -0.5, 1.0, (), jnp.float32)
    filter_inner = scatter_about(key_list[9], (LAYERS, 2, ORDER, ORDER), (ORDER // 2) ** -0.5, 1.0, (), jnp.float32)
    filter_biases = jnp.clip(jax.random.uniform(key_list[10], (LAYERS, 3, ORDER), jnp.float32, -3.140625, 3.140625), -3.140625, 3.140625)
    filter_out = scatter_about(key_list[11], (LAYERS, ORDER, D), (ORDER * 32) ** -0.5, 0.125, ((2, 2),), jnp.float32)
    filter_skip = scatter_about(key_list[12], (LAYERS, D), 1.0, 4.0, ((1, 2),), jnp.float32)
    out_weight = scatter_about(key_list[13], (LAYERS, D, D), D ** -0.5, 0.21875, ((1, 2),))
    out_bias = scatter_about(key_list[14], (LAYERS, D), 0.5, 3.0, ((1, 2),), jnp.float32)
    up_weight = scatter_about(key_list[15], (LAYERS, D, FF), D ** -0.5, 0.21875, ((2, 2),))
    up_bias = scatter_about(key_list[16], (LAYERS, FF), 0.5, 3.0, ((1, 2),), jnp.float32)
    down_weight = scatter_about(key_list[17], (LAYERS, FF, D), (FF // 2) ** -0.5, 0.15625, ((1, 2),))
    down_bias = scatter_about(key_list[18], (LAYERS, D), 0.5, 3.0, ((1, 2),), jnp.float32)
    cotangent = scatter_about(key_list[19], (TOKENS, D), 1.0, 6.0, ((0, 64), (1, 2)))
    return {"tokens": tokens, "lengths": lengths, "norm_gain": norm_gain, "norm_bias": norm_bias, "in_weight": in_weight, "in_bias": in_bias, "short_weight": short_weight, "short_bias": short_bias, "filter_first": filter_first, "filter_inner": filter_inner, "filter_biases": filter_biases, "filter_out": filter_out, "filter_skip": filter_skip, "out_weight": out_weight, "out_bias": out_bias, "up_weight": up_weight, "up_bias": up_bias, "down_weight": down_weight, "down_bias": down_bias, "cotangent": cotangent}


@jax.custom_vjp
def low(v):
    return lax.optimization_barrier(v.astype(jnp.bfloat16)).astype(jnp.float32)

@jax.custom_vjp
def low_back(v):
    return v

def low_keep(v):
    return (low(v), None)

def low_pass(kept, grad):
    return (grad,)

def back_keep(v):
    return (v, None)

def back_low(kept, grad):
    return (low(grad),)
low.defvjp(low_keep, low_pass)
low_back.defvjp(back_keep, back_low)
HIGH = lax.Precision.HIGHEST

def product(left, right):
    return jnp.matmul(left, right, precision=HIGH)

def norm_rows(stream, gain, shift):
    mean = lax.optimization_barrier(jnp.mean(stream, -1, keepdims=True))
    spread = lax.optimization_barrier(jnp.mean(stream * stream, -1, keepdims=True)) - mean * mean
    return (stream - mean) * lax.rsqrt(spread + 1e-05) * gain + shift

def positions(length, emb):
    bands = (emb - 1) // 2
    steps = jnp.arange(length, dtype=jnp.float32)
    times = steps / (length - 1)
    freqs = 0.0001 + (bands - 1 - 0.0001) * jnp.arange(bands, dtype=jnp.float32) / (bands - 1)
    angle = 2 * math.pi * steps[:, None] * freqs[None, :] / length
    feats = jnp.concatenate([times[:, None], jnp.cos(angle), -jnp.sin(angle)], 1)
    return (feats, times)

def decay_rates(channel, width):
    slow = math.log(0.01) / 1.5
    fast = math.log(0.01) / 0.3
    return jnp.abs(slow + (fast - slow) * channel.astype(jnp.float32) / (width - 1))

def long_conv(signal, kernel, skip):
    length = signal.shape[1]
    size = 2 * length
    spectrum = jnp.fft.rfft(signal, n=size, axis=1) * jnp.fft.rfft(kernel, n=size, axis=0)[None]
    return jnp.fft.irfft(spectrum, n=size, axis=1)[:, :length] + skip * signal

def hyena_block(stream, mask, params, feats, times, rates):
    gain, shift, in_w, in_b, short_w, short_b, first_w, inner_w, filt_b, out_fw, skip, out_w, out_b, up_w, up_b, down_w, down_b = params
    seqs, length = mask.shape
    normed = low(norm_rows(stream, gain[0], shift[0]))
    mixed = low_back(product(normed, in_w.reshape(D, 3 * D)) + in_b.reshape(3 * D))
    mixed = mixed.reshape(seqs, length, 3, D)
    padded = jnp.pad(mixed, ((0, 0), (2, 0), (0, 0), (0, 0)))
    conv = short_w[0] * padded[:, :length] + short_w[1] * padded[:, 1:length + 1] + short_w[2] * padded[:, 2:] + short_b
    hidden = jnp.sin(product(feats, first_w) + filt_b[0])
    hidden = jnp.sin(product(hidden, inner_w[0]) + filt_b[1])
    hidden = jnp.sin(product(hidden, inner_w[1]) + filt_b[2])
    kernel = product(hidden, out_fw) * (jnp.exp(-times[:, None] * rates[None, :]) + 0.05)
    value = conv[:, :, 2] * conv[:, :, 1]
    value = long_conv(value, kernel, skip)
    gated = low(value * conv[:, :, 0])
    branch = low_back(product(gated, out_w) + out_b)
    stream = stream + mask[..., None] * branch
    normed_two = low(norm_rows(stream, gain[1], shift[1]))
    inner = low_back(product(normed_two, up_w) + up_b)
    branch_two = low_back(product(low(jax.nn.gelu(inner)), down_w) + down_b)
    return stream + mask[..., None] * branch_two

def reference(tokens, lengths, norm_gain, norm_bias, in_weight, in_bias, short_weight, short_bias, filter_first, filter_inner, filter_biases, filter_out, filter_skip, out_weight, out_bias, up_weight, up_bias, down_weight, down_bias, cotangent):
    mask = (jnp.arange(LEN, dtype=jnp.int32)[None, :] < lengths[:, None]).astype(jnp.float32)
    feats, times = positions(LEN, EMB)
    rates = decay_rates(jnp.arange(D, dtype=jnp.int32), D)
    params = tuple((p.astype(jnp.float32) for p in (norm_gain, norm_bias, in_weight, in_bias, short_weight, short_bias, filter_first, filter_inner, filter_biases, filter_out, filter_skip, out_weight, out_bias, up_weight, up_bias, down_weight, down_bias)))
    start = tokens.astype(jnp.float32).reshape(SEQUENCES, LEN, D)

    def forward(first, weights):
        stream = first
        for layer in range(LAYERS):
            stream = hyena_block(stream, mask, [p[layer] for p in weights], feats, times, rates)
        return stream
    final, pullback = jax.vjp(forward, start, params)
    grad_start, grads = pullback(cotangent.astype(jnp.float32).reshape(SEQUENCES, LEN, D))
    return (final.reshape(TOKENS, D).astype(jnp.bfloat16), grad_start.reshape(TOKENS, D), grads[0], grads[1], grads[2], grads[3], grads[4], grads[5], grads[6], grads[7], grads[8], grads[9], grads[10], grads[11], grads[12], grads[13], grads[14], grads[15], grads[16])
```

```python
import functools
import math

import jax
import jax.numpy as jnp
import ml_dtypes
import numpy as np
from jax import lax
from jax.experimental import pallas as pl
from jax.experimental.pallas import tpu as pltpu
from jax.sharding import Mesh
from jax.sharding import PartitionSpec as P

D = 768
T = 512
H = T // 2
C = 384
FH = 1536
EPSILON = 1e-05
HIGH = lax.Precision.HIGHEST
F32 = jnp.float32
BF = jnp.bfloat16
VMEM_LIMIT = 56 * 2**20

ORDER = np.concatenate([np.arange(0, T, 2), np.arange(1, T, 2)])


def split_table(t):
    hi = t.astype(ml_dtypes.bfloat16)
    lo = (t - hi.astype(np.float64)).astype(ml_dtypes.bfloat16)
    return hi, lo


def wave_tables():
    n = np.arange(H)
    even = 2 * math.pi * (np.outer(n, 2 * n) % (2 * T)) / (2 * T)
    odd = 2 * math.pi * (np.outer(n, 2 * n + 1) % (2 * T)) / (2 * T)
    alt = np.where(n % 2 == 0, 1.0, -1.0)
    out = []
    for ang in (even, odd):
        co, si = np.cos(ang), np.sin(ang)
        si[0] = alt
        hi, lo = split_table(np.concatenate([co, si], 0))
        out.append(np.concatenate([hi, lo, hi], 1))
        hi, lo = split_table(np.concatenate([co.T, si.T], 1))
        out.append(np.concatenate([hi, lo, hi], 1))
    fe, ie, fo, io = out
    return fe, fo, ie, io


FE, FO, IE, IO = wave_tables()


def dot(a, b):
    return lax.dot_general(a, b, (((1,), (0,)), ((), ())), preferred_element_type=F32)


def dot_nt(a, b):
    return lax.dot_general(a, b, (((1,), (1,)), ((), ())), preferred_element_type=F32)


def dot_tn(a, b):
    return lax.dot_general(a, b, (((0,), (0,)), ((), ())), preferred_element_type=F32)


def normalize(x):
    mean = jnp.mean(x, -1, keepdims=True)
    scale = lax.rsqrt(jnp.mean(x * x, -1, keepdims=True) - mean * mean + EPSILON)
    return (x - mean) * scale, scale


def norm_pull(dn, x, gain):
    xhat, scale = normalize(x)
    ds = dn * gain
    first = jnp.mean(ds, -1, keepdims=True)
    second = jnp.mean(ds * xhat, -1, keepdims=True)
    return scale * (ds - first - xhat * second), dn * xhat


def row_mask(start, rows, length):
    r = start + lax.broadcasted_iota(jnp.int32, (rows, 1), 0)
    slot = jnp.where(r < H, 2 * r, 2 * (r - H) + 1)
    return (slot < length).astype(F32)


def down_one(x):
    r = lax.broadcasted_iota(jnp.int32, x.shape, 0)
    return jnp.where(r == 0, 0.0, pltpu.roll(x, 1, 0))


def up_one(x):
    r = lax.broadcasted_iota(jnp.int32, x.shape, 0)
    return jnp.where(r == x.shape[0] - 1, 0.0, pltpu.roll(x, x.shape[0] - 1, 0))


def put_split(ref, value, rows, lanes):
    hi = value.astype(BF)
    lo = (value - hi.astype(F32)).astype(BF)
    step = ref.shape[0] // 3
    ref[pl.ds(rows, value.shape[0]), lanes] = hi
    ref[pl.ds(step + rows, value.shape[0]), lanes] = hi
    ref[pl.ds(2 * step + rows, value.shape[0]), lanes] = lo


def top_row(shape):
    return lax.broadcasted_iota(jnp.int32, shape, 0) == 0


def butterfly(even, odd, lanes):
    ce, se = even[pl.ds(0, H), lanes], even[pl.ds(H, H), lanes]
    co, so = odd[pl.ds(0, H), lanes], odd[pl.ds(H, H), lanes]
    top = top_row(ce.shape)
    return ce + co, ce - co, jnp.where(top, se, se + so), jnp.where(top, so, se - so)


def spectrum_product(a, k, conj):
    a1, a2, b1, b2 = a
    k1, k2, l1, l2 = k
    top = top_row(a1.shape)
    aa, bb, cc, dd = a1 * k1, b1 * l1, a2 * k2, b2 * l2
    if conj:
        y1 = jnp.where(top, aa, aa + bb)
        y2 = jnp.where(top, cc, cc + dd)
        m1 = jnp.where(top, bb + dd, b1 * k1 - a1 * l1)
        m2 = jnp.where(top, b2 * l1 - b1 * l2, b2 * k2 - a2 * l2)
    else:
        y1 = jnp.where(top, aa, aa - bb)
        y2 = jnp.where(top, cc, cc - dd)
        m1 = jnp.where(top, bb - dd, a1 * l1 + b1 * k1)
        m2 = jnp.where(top, b1 * l2 + b2 * l1, a2 * l2 + b2 * k2)
    return y1, y2, m1, m2


def put_inverse(rhs_e, rhs_o, y, lanes):
    y1, y2, m1, m2 = y
    top = top_row(y1.shape)
    unit = 1.0 / T
    w = jnp.where(top, 0.5 * unit, unit)
    put_split(rhs_e, (y1 + y2) * w, 0, lanes)
    put_split(rhs_o, (y1 - y2) * w, 0, lanes)
    put_split(rhs_e, jnp.where(top, m1, m1 + m2) * unit, H, lanes)
    put_split(rhs_o, jnp.where(top, m2, m1 - m2) * unit, H, lanes)


def lanes_of(block):
    return pl.ds(block * 128, 128)


def short_conv(u_ref, sw_ref, sb_ref, block):
    out = []
    for s in range(3):
        at = lanes_of(s * (C // 128) + block)
        ue, uo = u_ref[pl.ds(0, H), at], u_ref[pl.ds(H, H), at]
        t0, t1, t2 = (sw_ref[j : j + 1, at] for j in range(3))
        bias = sb_ref[0:1, at]
        uo_d = down_one(uo)
        we = t2 * ue + t1 * uo_d + t0 * down_one(ue) + bias
        wo = t2 * uo + t1 * ue + t0 * uo_d + bias
        out.append((we, wo))
    return out


def filter_spectrum(k_ref, fe_ref, fo_ref, out_ref, rhs_e, rhs_o, se, so):
    for b in range(C // 128):
        at = lanes_of(b)
        put_split(rhs_e, k_ref[0, pl.ds(0, H), at], 0, at)
        put_split(rhs_o, k_ref[0, pl.ds(H, H), at], 0, at)
    se[...] = dot(fe_ref[...], rhs_e[...])
    so[...] = dot(fo_ref[...], rhs_o[...])
    for b in range(C // 128):
        at = lanes_of(b)
        for i, v in enumerate(butterfly(se, so, at)):
            out_ref[0, i, :, at] = v


def add_branch(x_ref, own_ref, other_ref, vec_ref, row, length, start, rows):
    at = pl.ds(start, rows)
    y = own_ref[at, :].astype(F32) + other_ref[at, :].astype(F32) + vec_ref[row : row + 1, :]
    return x_ref[at, :] + row_mask(start, rows, length) * y


RB = 128


def row_loop(body, init=0):
    def step(i, c):
        return body(pl.multiple_of(i * RB, RB), c)

    return lax.fori_loop(0, T // RB, step, init)


def mixer_forward(joined, *refs):
    if joined:
        len_ref, x_ref, own_ref, other_ref, prev_ref = refs[:5]
        refs = refs[5:]
    else:
        x_ref = refs[0]
        refs = refs[1:]
    (vec_ref, inw_ref, inb_ref, sw_ref, sb_ref, ks_ref, skip_ref, fe_ref, fo_ref, ie_ref, io_ref, outw_ref) = refs[:12]
    refs = refs[12:]
    if joined:
        xo_ref = refs[0]
        refs = refs[1:]
    u_ref, qs_ref, g_ref, p_ref, a_s, w0_s, q_s, rhs_e, rhs_o, se, so, rhs2_e, rhs2_o, z_s = refs

    def first(start, c):
        at = pl.ds(start, RB)
        if joined:
            x = add_branch(x_ref, own_ref, other_ref, prev_ref, 5, len_ref[0], start, RB)
            xo_ref[at, :] = x
        else:
            x = x_ref[at, :]
        xhat, _ = normalize(x)
        a_s[at, :] = (xhat * vec_ref[0:1, :] + vec_ref[1:2, :]).astype(BF)
        return c

    row_loop(first)
    for s in range(3):
        at = pl.ds(s * C, C)
        u_ref[:, at] = dot(a_s[...], inw_ref[s]) + inb_ref[0:1, at]
    for b in range(C // 128):
        at = lanes_of(b)
        (w0e, w0o), (w1e, w1o), (w2e, w2o) = short_conv(u_ref, sw_ref, sb_ref, b)
        w0_s[pl.ds(0, H), at] = w0e
        w0_s[pl.ds(H, H), at] = w0o
        qe, qo = w2e * w1e, w2o * w1o
        q_s[pl.ds(0, H), at] = qe
        q_s[pl.ds(H, H), at] = qo
        put_split(rhs_e, qe, 0, at)
        put_split(rhs_o, qo, 0, at)
    se[...] = dot(fe_ref[...], rhs_e[...])
    so[...] = dot(fo_ref[...], rhs_o[...])
    for b in range(C // 128):
        at = lanes_of(b)
        spec = butterfly(se, so, at)
        for i, v in enumerate(spec):
            qs_ref[i, :, at] = v
        y = spectrum_product(spec, [ks_ref[0, i, :, at] for i in range(4)], False)
        put_inverse(rhs2_e, rhs2_o, y, at)
    se[pl.ds(0, H), :] = dot(ie_ref[...], rhs2_e[...])
    se[pl.ds(H, H), :] = dot(io_ref[...], rhs2_o[...])

    def last(start, c):
        at = pl.ds(start, RB)
        g = se[at, :] + skip_ref[0:1, :] * q_s[at, :]
        g_ref[at, :] = g
        z_s[at, :] = (g * w0_s[at, :]).astype(BF)
        return c

    row_loop(last)
    p_ref[...] = dot(z_s[...], outw_ref[...]).astype(BF)


def gelu_parts(h):
    c0 = math.sqrt(2 / math.pi)
    hh = h * h
    t = jnp.tanh(c0 * (h + 0.044715 * (hh * h)))
    half = 0.5 * (1.0 + t)
    return half, t, hh, c0


def ff_forward(len_ref, x_ref, own_ref, other_ref, vec_ref, up_ref, upb_ref, dn_ref, xo_ref, h_ref, p_ref, b_s, acc):
    j = pl.program_id(0)

    @pl.when(j == 0)
    def _():
        def first(start, c):
            at = pl.ds(start, RB)
            x = add_branch(x_ref, own_ref, other_ref, vec_ref, 4, len_ref[0], start, RB)
            xo_ref[at, :] = x
            xhat, _ = normalize(x)
            b_s[at, :] = (xhat * vec_ref[2:3, :] + vec_ref[3:4, :]).astype(BF)
            return c

        row_loop(first)

    h = dot(b_s[...], up_ref[...]) + upb_ref[...]
    h_ref[...] = h
    half, _, _, _ = gelu_parts(h)
    part = dot((h * half).astype(BF), dn_ref[...])

    @pl.when(j == 0)
    def _():
        acc[...] = part

    @pl.when(j > 0)
    def _():
        acc[...] += part

    @pl.when(j == pl.num_programs(0) - 1)
    def _():
        p_ref[...] = acc[...].astype(BF)


def ff_backward(joined, *refs):
    len_ref, g_ref = refs[:2]
    refs = refs[2:]
    if joined:
        own_ref, other_ref, xn_ref, nvec_ref = refs[:4]
        refs = refs[4:]
    x_ref, h_ref, vec_ref, up_ref, dn_ref = refs[:5]
    refs = refs[5:]
    if joined:
        go_ref, ngrad_ref = refs[:2]
        refs = refs[2:]
    gup_ref, gdn_ref, gupb_ref, gdnb_ref, p_ref, dm_s, b_s, acc = refs
    j = pl.program_id(0)

    @pl.when(j == 0)
    def _():
        def first(start, c):
            at = pl.ds(start, RB)
            g = g_ref[at, :].astype(F32)
            sums, s1, s2 = c
            if joined:
                dn = own_ref[at, :].astype(F32) + other_ref[at, :].astype(F32)
                dx, dg = norm_pull(dn, xn_ref[at, :], nvec_ref[0:1, :])
                g = g + dx
                go_ref[at, :] = g
                s1 = s1 + jnp.sum(dg, 0, keepdims=True)
                s2 = s2 + jnp.sum(dn, 0, keepdims=True)
            dm = (row_mask(start, RB, len_ref[0]) * g).astype(BF)
            dm_s[at, :] = dm
            xhat, _ = normalize(x_ref[at, :])
            b_s[at, :] = (xhat * vec_ref[2:3, :] + vec_ref[3:4, :]).astype(BF)
            return sums + jnp.sum(dm.astype(F32), 0, keepdims=True), s1, s2

        zero = jnp.zeros((1, D), F32)
        sums, s1, s2 = row_loop(first, (zero, zero, zero))
        gdnb_ref[...] = sums
        if joined:
            ngrad_ref[0:1, :] = s1
            ngrad_ref[1:2, :] = s2

    h = h_ref[...]
    half, t, hh, c0 = gelu_parts(h)
    e = (h * half).astype(BF)
    slope = half + 0.5 * c0 * h * (1.0 - t * t) * (1.0 + 3 * 0.044715 * hh)
    dh = (dot_nt(dm_s[...], dn_ref[...]) * slope).astype(BF)
    gupb_ref[...] = jnp.sum(dh.astype(F32), 0, keepdims=True)
    part = dot_nt(dh, up_ref[...])
    gdn_ref[...] = dot_tn(e, dm_s[...]).astype(BF)
    gup_ref[...] = dot_tn(b_s[...], dh).astype(BF)

    @pl.when(j == 0)
    def _():
        acc[...] = part

    @pl.when(j > 0)
    def _():
        acc[...] += part

    @pl.when(j == pl.num_programs(0) - 1)
    def _():
        p_ref[...] = acc[...].astype(BF)


def mixer_backward(
    len_ref, g_in_ref, own_ref, other_ref, x1_ref, x0_ref, u_ref, qs_ref, g_ref, ks_ref, vec_ref, inw_ref, outw_ref,
    sw_ref, sb_ref, skip_ref, fe_ref, fo_ref, ie_ref, io_ref,
    go_ref, ngrad_ref, goutw_ref, goutb_ref, ginw_ref, ginb_ref, gsw_ref, gsb_ref, gskip_ref, dk_ref, p_ref,
    dy_s, a_s, dz_s, z_s, dg_s, w1_s, w2_s, dw0_s, rhs_e, rhs_o, se, so, rhs2_e, rhs2_o, inv_s, du_s,
):
    def first(start, c):
        at = pl.ds(start, RB)
        sums, s1, s2 = c
        dn = own_ref[at, :].astype(F32) + other_ref[at, :].astype(F32)
        dx, dg = norm_pull(dn, x1_ref[at, :], vec_ref[2:3, :])
        g = g_in_ref[at, :].astype(F32) + dx
        go_ref[at, :] = g
        dy = (row_mask(start, RB, len_ref[0]) * g).astype(BF)
        dy_s[at, :] = dy
        xhat, _ = normalize(x0_ref[at, :])
        a_s[at, :] = (xhat * vec_ref[0:1, :] + vec_ref[1:2, :]).astype(BF)
        return (
            sums + jnp.sum(dy.astype(F32), 0, keepdims=True),
            s1 + jnp.sum(dg, 0, keepdims=True),
            s2 + jnp.sum(dn, 0, keepdims=True),
        )

    zero = jnp.zeros((1, D), F32)
    sums, s1, s2 = row_loop(first, (zero, zero, zero))
    goutb_ref[...] = sums
    ngrad_ref[0:1, :] = s1
    ngrad_ref[1:2, :] = s2
    dz_s[...] = dot_nt(dy_s[...], outw_ref[...])
    halves = (pl.ds(0, H), pl.ds(H, H))
    for b in range(C // 128):
        at = lanes_of(b)
        w0, w1, w2 = short_conv(u_ref, sw_ref, sb_ref, b)
        dskip = 0.0
        for i, (rows, rhs) in enumerate(zip(halves, (rhs_e, rhs_o))):
            dz, g = dz_s[rows, at], g_ref[rows, at]
            z_s[rows, at] = (g * w0[i]).astype(BF)
            dw0_s[rows, at] = dz * g
            dg = dz * w0[i]
            dg_s[rows, at] = dg
            dskip = dskip + jnp.sum(dg * (w2[i] * w1[i]), 0, keepdims=True)
            w1_s[rows, at] = w1[i]
            w2_s[rows, at] = w2[i]
            put_split(rhs, dg, 0, at)
        gskip_ref[0:1, at] = dskip
    se[...] = dot(fe_ref[...], rhs_e[...])
    so[...] = dot(fo_ref[...], rhs_o[...])
    for b in range(C // 128):
        at = lanes_of(b)
        spec = butterfly(se, so, at)
        put_inverse(rhs2_e, rhs2_o, spectrum_product(spec, [ks_ref[0, i, :, at] for i in range(4)], True), at)
        put_inverse(rhs2_e, rhs2_o, spectrum_product(spec, [qs_ref[i, :, at] for i in range(4)], True), pl.ds(C + b * 128, 128))
    inv_s[pl.ds(0, H), :] = dot(ie_ref[...], rhs2_e[...])
    inv_s[pl.ds(H, H), :] = dot(io_ref[...], rhs2_o[...])
    dk_ref[...] = inv_s[:, pl.ds(C, C)]
    for b in range(C // 128):
        at = lanes_of(b)
        dw = [[dw0_s[rows, at] for rows in halves], [], []]
        for rows in halves:
            dq = inv_s[rows, at] + skip_ref[0:1, at] * dg_s[rows, at]
            dw[1].append(dq * w2_s[rows, at])
            dw[2].append(dq * w1_s[rows, at])
        for s in range(3):
            to = lanes_of(s * (C // 128) + b)
            ue, uo = u_ref[halves[0], to], u_ref[halves[1], to]
            t0, t1, t2 = (sw_ref[j : j + 1, to] for j in range(3))
            de, do = dw[s]
            de_u, do_u = up_one(de), up_one(do)
            due = (t2 * de + t1 * do + t0 * de_u).astype(BF)
            duo = (t2 * do + t1 * de_u + t0 * do_u).astype(BF)
            du_s[halves[0], to] = due
            du_s[halves[1], to] = duo
            uo_d = down_one(uo)
            gsw_ref[0:1, to] = jnp.sum(de * down_one(ue) + do * uo_d, 0, keepdims=True)
            gsw_ref[1:2, to] = jnp.sum(de * uo_d + do * ue, 0, keepdims=True)
            gsw_ref[2:3, to] = jnp.sum(de * ue + do * uo, 0, keepdims=True)
            gsb_ref[0:1, to] = jnp.sum(de + do, 0, keepdims=True)
            ginb_ref[0:1, to] = jnp.sum(due.astype(F32) + duo.astype(F32), 0, keepdims=True)
    part = dot_nt(du_s[:, pl.ds(0, C)], inw_ref[0])
    for s in range(1, 3):
        part += dot_nt(du_s[:, pl.ds(s * C, C)], inw_ref[s])
    p_ref[...] = part.astype(BF)
    goutw_ref[...] = dot_tn(z_s[...], dy_s[...]).astype(BF)
    for s in range(3):
        ginw_ref[s] = dot_tn(a_s[...], du_s[:, pl.ds(s * C, C)]).astype(BF)


def sds(shape, dtype=F32):
    return jax.ShapeDtypeStruct(shape, dtype)


def params(flops, nbytes):
    return dict(
        compiler_params=pltpu.CompilerParams(vmem_limit_bytes=VMEM_LIMIT),
        cost_estimate=pl.CostEstimate(flops=int(flops), bytes_accessed=int(nbytes), transcendentals=0),
    )


SMEM = pl.BlockSpec(memory_space=pltpu.SMEM)
WHOLE = pl.BlockSpec(memory_space=pltpu.VMEM)


def spectrum_scratch():
    return [pltpu.VMEM((3 * H, C), BF)] * 2 + [pltpu.VMEM((T, C), F32)] * 2


def run_filter_spectrum(kernels):
    layers = kernels.shape[0]
    fixed = lambda shape: pl.BlockSpec(shape, lambda l: (0,) * len(shape))
    return pl.pallas_call(
        filter_spectrum,
        grid=(layers,),
        in_specs=[pl.BlockSpec((1, T, C), lambda l: (l, 0, 0)), fixed(FE.shape), fixed(FO.shape)],
        out_specs=pl.BlockSpec((1, 4, H, C), lambda l: (l, 0, 0, 0)),
        out_shape=sds((layers, 4, H, C)),
        scratch_shapes=spectrum_scratch(),
        name="filter_spectrum",
        **params(2e9, 8e6),
    )(kernels, FE, FO)


def run_mixer_forward(joint, x, vec, inw, inb, sw, sb, ks, skip, outw):
    joined = joint is not None
    args = ([joint[0], x, joint[1], joint[2], joint[3]] if joined else [x]) + [
        vec, inw, inb, sw, sb, ks, skip, FE, FO, IE, IO, outw]
    outs = ([sds((T, D))] if joined else []) + [sds((T, 3 * C)), sds((4, H, C)), sds((T, C)), sds((T, D), BF)]
    return pl.pallas_call(
        functools.partial(mixer_forward, joined),
        in_specs=([SMEM] if joined else []) + [WHOLE] * (len(args) - joined),
        out_specs=[WHOLE] * len(outs),
        out_shape=outs,
        scratch_shapes=[pltpu.VMEM((T, D), BF), pltpu.VMEM((T, C), F32), pltpu.VMEM((T, C), F32)]
        + spectrum_scratch()
        + [pltpu.VMEM((6 * H, C), BF)] * 2
        + [pltpu.VMEM((T, C), BF)],
        name="mixer_forward",
        **params(6e9, 1.2e7),
    )(*args)


FC = 512


def run_ff_forward(length, x, own, other, vec, up, upb, dn):
    fixed = lambda shape: pl.BlockSpec(shape, lambda j: (0,) * len(shape))
    return pl.pallas_call(
        ff_forward,
        grid=(FH // FC,),
        in_specs=[
            SMEM, fixed((T, D)), fixed((T, D)), fixed((T, D)), fixed(vec.shape),
            pl.BlockSpec((D, FC), lambda j: (0, j)),
            pl.BlockSpec((1, FC), lambda j: (0, j)),
            pl.BlockSpec((FC, D), lambda j: (j, 0)),
        ],
        out_specs=[fixed((T, D)), pl.BlockSpec((T, FC), lambda j: (0, j)), fixed((T, D))],
        out_shape=[sds((T, D)), sds((T, FH)), sds((T, D), BF)],
        scratch_shapes=[pltpu.VMEM((T, D), BF), pltpu.VMEM((T, D), F32)],
        name="ff_forward",
        **params(5e9, 1.2e7),
    )(length, x, own, other, vec, up, upb, dn)


def run_ff_backward(length, g, joint, x, h, vec, up, dn):
    joined = joint is not None
    fixed = lambda shape: pl.BlockSpec(shape, lambda j: (0,) * len(shape))
    args = [length, g] + (list(joint) if joined else []) + [x, h, vec, up, dn]
    in_specs = [SMEM, fixed((T, D))]
    if joined:
        in_specs += [fixed((T, D))] * 3 + [fixed(joint[3].shape)]
    in_specs += [
        fixed((T, D)),
        pl.BlockSpec((T, FC), lambda j: (0, j)),
        fixed(vec.shape),
        pl.BlockSpec((D, FC), lambda j: (0, j)),
        pl.BlockSpec((FC, D), lambda j: (j, 0)),
    ]
    out_specs = [fixed((T, D)), fixed((2, D))] if joined else []
    outs = [sds((T, D)), sds((2, D))] if joined else []
    out_specs += [
        pl.BlockSpec((D, FC), lambda j: (0, j)),
        pl.BlockSpec((FC, D), lambda j: (j, 0)),
        pl.BlockSpec((1, FC), lambda j: (0, j)),
        fixed((1, D)),
        fixed((T, D)),
    ]
    outs += [sds((D, FH), BF), sds((FH, D), BF), sds((1, FH)), sds((1, D)), sds((T, D), BF)]
    return pl.pallas_call(
        functools.partial(ff_backward, joined),
        grid=(FH // FC,),
        in_specs=in_specs,
        out_specs=out_specs,
        out_shape=outs,
        scratch_shapes=[pltpu.VMEM((T, D), BF), pltpu.VMEM((T, D), BF), pltpu.VMEM((T, D), F32)],
        name="ff_backward",
        **params(1e10, 2e7),
    )(*args)


def run_mixer_backward(length, g_in, own, other, x1, x0, u, qs, g, ks, vec, inw, outw, sw, sb, skip):
    args = [length, g_in, own, other, x1, x0, u, qs, g, ks, vec, inw, outw, sw, sb, skip, FE, FO, IE, IO]
    outs = [
        sds((T, D)), sds((2, D)), sds((C, D), BF), sds((1, D)), sds((3, D, C), BF), sds((1, 3 * C)),
        sds((3, 3 * C)), sds((1, 3 * C)), sds((1, C)), sds((T, C)), sds((T, D), BF),
    ]
    tc = pltpu.VMEM((T, C), F32)
    return pl.pallas_call(
        mixer_backward,
        in_specs=[SMEM] + [WHOLE] * (len(args) - 1),
        out_specs=[WHOLE] * len(outs),
        out_shape=outs,
        scratch_shapes=[
            pltpu.VMEM((T, D), BF), pltpu.VMEM((T, D), BF), tc, pltpu.VMEM((T, C), BF), tc, tc, tc, tc,
            *spectrum_scratch(),
            pltpu.VMEM((6 * H, 2 * C), BF), pltpu.VMEM((6 * H, 2 * C), BF),
            pltpu.VMEM((T, 2 * C), F32), pltpu.VMEM((T, 3 * C), BF),
        ],
        name="mixer_backward",
        **params(1e10, 2e7),
    )(*args)


def positions(length, emb):
    bands = (emb - 1) // 2
    steps = jnp.asarray(ORDER, jnp.float32)
    times = steps / (length - 1)
    freqs = 0.0001 + (bands - 1 - 0.0001) * jnp.arange(bands, dtype=jnp.float32) / (bands - 1)
    angle = 2 * math.pi * steps[:, None] * freqs[None, :] / length
    feats = jnp.concatenate([times[:, None], jnp.cos(angle), -jnp.sin(angle)], 1)
    return (feats, times)


def decay_rates(channel, width):
    slow = math.log(0.01) / 1.5
    fast = math.log(0.01) / 0.3
    return jnp.abs(slow + (fast - slow) * channel.astype(jnp.float32) / (width - 1))


def filter_net(first_w, inner_w, biases, out_w, feats, decay):
    hidden = jnp.sin(jnp.dot(feats, first_w, precision=HIGH) + biases[0])
    hidden = jnp.sin(jnp.dot(hidden, inner_w[0], precision=HIGH) + biases[1])
    hidden = jnp.sin(jnp.dot(hidden, inner_w[1], precision=HIGH) + biases[2])
    return jnp.dot(hidden, out_w, precision=HIGH) * decay


SWAP = [(0, 1), (1, 0)]
PLANE = ("y", "x")


def swap(x, axis):
    return lax.ppermute(x, axis, SWAP)


def in_order(mine, own, other, axis):
    low = mine == 0
    return jnp.concatenate([jnp.where(low, own, other), jnp.where(low, other, own)], axis)


def total(part, core, axis=0):
    half = part.shape[axis] // 2
    keep = lax.dynamic_slice_in_dim(part, core * half, half, axis)
    give = lax.dynamic_slice_in_dim(part, (1 - core) * half, half, axis)
    mine = (keep.astype(F32) + swap(give, "c").astype(F32)).astype(part.dtype)
    mine = lax.psum_scatter(mine, PLANE, scatter_dimension=0, tiled=True)
    mine = (mine.astype(F32) + swap(mine, "zl").astype(F32)).astype(part.dtype)
    mine = lax.all_gather(mine, PLANE, axis=0, tiled=True)
    return in_order(core, mine, swap(mine, "c"), axis).astype(F32)


def shards(
    tokens, lengths, norm_gain, norm_bias, in_weight, in_bias, short_weight, short_bias, filter_first, filter_inner,
    filter_biases, filter_out, filter_skip, out_weight, out_bias, up_weight, up_bias, down_weight, down_bias, cotangent,
):
    layers = norm_gain.shape[0]
    half_at = lax.axis_index("zh")
    core = lax.axis_index("c")

    tokens_other = swap(tokens, "zh")
    rows = jnp.concatenate(
        [norm_gain[:, 0], norm_bias[:, 0], norm_gain[:, 1], norm_bias[:, 1], out_bias, down_bias], 0
    )
    rows = in_order(half_at, rows, swap(rows, "zh"), 1).reshape(6, layers, D)
    vecs = [jnp.pad(rows[:, l], ((0, 2), (0, 0))) for l in range(layers)]
    cot_other = swap(cotangent, "zh")

    def by_parity(x):
        return x.reshape(H, 2, D).transpose(1, 0, 2).reshape(T, D)

    def by_slot(x):
        return x.reshape(2, H, -1).transpose(1, 0, 2).reshape(T, -1)

    x = by_parity(in_order(half_at, tokens, tokens_other, 1)).astype(F32)

    feats, times = positions(T, filter_first.shape[1])
    channel = half_at * C + jnp.arange(C, dtype=jnp.int32)
    decay = jnp.exp(-times[:, None] * decay_rates(channel, D)[None, :]) + 0.05
    nets, pulls = [], []
    for l in range(layers):
        k, pull = jax.vjp(
            lambda a, b, c, d: filter_net(a, b, c, d, feats, decay),
            filter_first[l], filter_inner[l], filter_biases[l], filter_out[l],
        )
        nets.append(k)
        pulls.append(pull)
    spectra = run_filter_spectrum(jnp.stack(nets))

    inw = in_weight.transpose(0, 2, 1, 3)
    inb = in_bias.reshape(layers, 1, 3 * C)
    sw = short_weight.reshape(layers, 3, 3 * C)
    sb = short_bias.reshape(layers, 1, 3 * C)
    skip = filter_skip.reshape(layers, 1, C)
    upb = up_bias.reshape(layers, 1, FH)
    ks = [spectra[l : l + 1] for l in range(layers)]

    saved = []
    joint = None
    for l in range(layers):
        made = run_mixer_forward(joint, x, vecs[l], inw[l], inb[l], sw[l], sb[l], ks[l], skip[l], out_weight[l])
        if joint is not None:
            x, made = made[0], made[1:]
        u, qs, g, p = made
        x1, h, p2 = run_ff_forward(lengths, x, p, swap(p, "zh"), vecs[l], up_weight[l], upb[l], down_weight[l])
        saved.append((x, u, qs, g, x1, h))
        p2_other = swap(p2, "zh")
        joint = (lengths, p2, p2_other, vecs[l])
        x = x1

    def my_half(x):
        return lax.dynamic_slice_in_dim(x, half_at * C, C, 1)

    slot = jnp.asarray(ORDER, jnp.int32)[:, None]
    mask = (slot < lengths[0]).astype(F32)
    y = my_half(joint[1]).astype(F32) + my_half(joint[2]).astype(F32) + down_bias[layers - 1]
    result = by_slot((my_half(x) + mask * y).astype(BF))

    grad = by_parity(in_order(half_at, cotangent, cot_other, 1))
    joint = None
    big = [None] * layers
    small = [None] * layers
    norms = {}
    for l in reversed(range(layers)):
        x0, u, qs, g, x1, h = saved[l]
        made = run_ff_backward(lengths, grad, joint, x1, h, vecs[l], up_weight[l], down_weight[l])
        if joint is not None:
            grad, norms[l + 1, 0] = made[:2]
            made = made[2:]
        gup, gdn, gupb, gdnb, p = made
        made = run_mixer_backward(
            lengths, grad, p, swap(p, "zh"), x1, x0, u, qs, g, ks[l], vecs[l], inw[l], out_weight[l], sw[l], sb[l], skip[l]
        )
        grad, norms[l, 1], goutw, goutb, ginw, ginb, gsw, gsb, gskip, dk, p = made
        joint = (p, swap(p, "zh"), x0, vecs[l])
        big[l] = [total(gup, core), total(gdn, core), total(goutw, core, 1)]
        big[l].append(total(ginw.reshape(3 * D, C), core).reshape(3, D, C))
        gfilter = pulls[l](dk)
        small[l] = (gupb, gdnb, goutb, ginb, gsw, gsb, gskip, gfilter)

    own, other, x0, vec = joint
    dn = own.astype(F32) + other.astype(F32)
    dx, dg = norm_pull(dn, x0, vec[0:1])
    grad = by_slot(my_half(grad + dx))
    norms[0, 0] = jnp.stack([jnp.sum(dg, 0), jnp.sum(dn, 0)])

    pieces = []
    for l in range(layers):
        gupb, gdnb, goutb, ginb, gsw, gsb, gskip, gfilter = small[l]
        pieces += [
            my_half(norms[l, 0]), my_half(norms[l, 1]), my_half(gdnb), my_half(goutb), gupb.reshape(4, C),
            ginb.reshape(3, C), gsw.reshape(9, C), gsb.reshape(3, C), gskip, gfilter[3],
        ]
    shared = jnp.concatenate([m.reshape(-1) for l in range(layers) for m in small[l][7][:3]])
    n_shared = shared.shape[0]
    shared = jnp.pad(shared, (0, -n_shared % C)).reshape(-1, C)
    pack = jnp.concatenate(pieces, 0)
    n_rows = pack.shape[0]
    pack = jnp.concatenate([pack, shared], 0)
    pack = total(jnp.pad(pack, ((0, -pack.shape[0] % 32), (0, 0))), core)
    shared = pack[n_rows : n_rows + shared.shape[0]]
    shared = (shared + swap(shared, "zh")).reshape(-1)[:n_shared].reshape(layers, -1)
    pack = pack[:n_rows].reshape(layers, -1, C)
    n0 = filter_first[0].size
    n1 = filter_inner[0].size
    g_first = shared[:, :n0].reshape(filter_first.shape)
    g_inner = shared[:, n0 : n0 + n1].reshape(filter_inner.shape)
    g_fbias = shared[:, n0 + n1 :].reshape(filter_biases.shape)

    def stack(i):
        return jnp.stack([big[l][i] for l in range(layers)])

    return (
        result,
        grad,
        pack[:, 0:4:2],
        pack[:, 1:4:2],
        stack(3).transpose(0, 2, 1, 3),
        pack[:, 10:13],
        pack[:, 13:22].reshape(short_weight.shape),
        pack[:, 22:25],
        g_first,
        g_inner,
        g_fbias,
        pack[:, 26:90],
        pack[:, 25],
        stack(2),
        pack[:, 5],
        stack(0),
        pack[:, 6:10].reshape(layers, FH),
        stack(1),
        pack[:, 4],
    )


def solution(mesh):
    names = ("zl", "y", "x", "c", "zh")
    fine = Mesh(mesh.devices.reshape(2, 4, 4, 2, 2), names)
    dp = ("zl", "y", "x", "c")
    rows = P(dp, "zh")
    third, fourth = P(None, None, "zh"), P(None, None, None, "zh")
    second, middle = P(None, "zh"), P(None, "zh", None)
    placed = (
        rows, P(dp), third, third, fourth, third, fourth, third, P(), P(), P(), third, second, middle, second, third,
        second, middle, second, rows,
    )
    return jax.shard_map(
        shards,
        mesh=fine,
        in_specs=placed,
        out_specs=(
            rows, rows, third, third, fourth, third, fourth, third, P(), P(), P(), third, second, middle, second, third,
            second, middle, second,
        ),
        check_vma=False,
    )
```

```python
import functools
import math

import jax
import jax.numpy as jnp
import ml_dtypes
import numpy as np
from jax import lax
from jax.experimental import pallas as pl
from jax.experimental.pallas import tpu as pltpu
from jax.sharding import Mesh
from jax.sharding import PartitionSpec as P

D = 768
T = 512
H = T // 2
C = 384
FH = 1536
NET = 64
EMB = 33
BANDS = 16
PIECE = 96
EPSILON = 1e-05
HIGH = lax.Precision.HIGHEST
F32 = jnp.float32
BF = jnp.bfloat16
VMEM_LIMIT = 56 * 2**20

ORDER = np.concatenate([np.arange(0, T, 2), np.arange(1, T, 2)])


def split_table(t):
    hi = t.astype(ml_dtypes.bfloat16)
    lo = (t - hi.astype(np.float64)).astype(ml_dtypes.bfloat16)
    return hi, lo


def wave_tables():
    n = np.arange(H)
    even = 2 * math.pi * (np.outer(n, 2 * n) % (2 * T)) / (2 * T)
    odd = 2 * math.pi * (np.outer(n, 2 * n + 1) % (2 * T)) / (2 * T)
    alt = np.where(n % 2 == 0, 1.0, -1.0)
    out = []
    for ang in (even, odd):
        co, si = np.cos(ang), np.sin(ang)
        si[0] = alt
        hi, lo = split_table(np.concatenate([co, si], 0))
        out.append(np.concatenate([hi, lo, hi], 1))
        hi, lo = split_table(np.concatenate([co.T, si.T], 1))
        out.append(np.concatenate([hi, lo, hi], 1))
    fe, ie, fo, io = out
    return fe, fo, ie, io


FE, FO, IE, IO = wave_tables()


def slot_features():
    slots = ORDER.astype(np.float64)
    freqs = 0.0001 + (BANDS - 1 - 0.0001) * np.arange(BANDS) / (BANDS - 1)
    angle = 2 * math.pi * slots[:, None] * freqs[None, :] / T
    times = (slots / (T - 1))[:, None]
    feats = np.concatenate([times, np.cos(angle), -np.sin(angle), np.zeros((T, 128 - EMB))], 1)
    return feats.astype(np.float32), np.broadcast_to(times, (T, 128)).astype(np.float32)


FEATS, TIMES = slot_features()


def dot(a, b):
    return lax.dot_general(a, b, (((1,), (0,)), ((), ())), preferred_element_type=F32)


def dot_nt(a, b):
    return lax.dot_general(a, b, (((1,), (1,)), ((), ())), preferred_element_type=F32)


def dot_tn(a, b):
    return lax.dot_general(a, b, (((0,), (0,)), ((), ())), preferred_element_type=F32)


def normalize(x):
    mean = jnp.mean(x, -1, keepdims=True)
    scale = lax.rsqrt(jnp.mean(x * x, -1, keepdims=True) - mean * mean + EPSILON)
    return (x - mean) * scale, scale


def norm_pull(dn, x, gain):
    xhat, scale = normalize(x)
    ds = dn * gain
    first = jnp.mean(ds, -1, keepdims=True)
    second = jnp.mean(ds * xhat, -1, keepdims=True)
    return scale * (ds - first - xhat * second), dn * xhat


def row_mask(start, rows, length):
    r = start + lax.broadcasted_iota(jnp.int32, (rows, 1), 0)
    slot = jnp.where(r < H, 2 * r, 2 * (r - H) + 1)
    return (slot < length).astype(F32)


def down_one(x):
    r = lax.broadcasted_iota(jnp.int32, x.shape, 0)
    return jnp.where(r == 0, 0.0, pltpu.roll(x, 1, 0))


def up_one(x):
    r = lax.broadcasted_iota(jnp.int32, x.shape, 0)
    return jnp.where(r == x.shape[0] - 1, 0.0, pltpu.roll(x, x.shape[0] - 1, 0))


def put_split(ref, value, rows, lanes):
    hi = value.astype(BF)
    lo = (value - hi.astype(F32)).astype(BF)
    step = ref.shape[0] // 3
    ref[pl.ds(rows, value.shape[0]), lanes] = hi
    ref[pl.ds(step + rows, value.shape[0]), lanes] = hi
    ref[pl.ds(2 * step + rows, value.shape[0]), lanes] = lo


def top_row(shape):
    return lax.broadcasted_iota(jnp.int32, shape, 0) == 0


def butterfly(even, odd, lanes):
    ce, se = even[pl.ds(0, H), lanes], even[pl.ds(H, H), lanes]
    co, so = odd[pl.ds(0, H), lanes], odd[pl.ds(H, H), lanes]
    top = top_row(ce.shape)
    return ce + co, ce - co, jnp.where(top, se, se + so), jnp.where(top, so, se - so)


def spectrum_product(a, k, conj):
    a1, a2, b1, b2 = a
    k1, k2, l1, l2 = k
    top = top_row(a1.shape)
    aa, bb, cc, dd = a1 * k1, b1 * l1, a2 * k2, b2 * l2
    if conj:
        y1 = jnp.where(top, aa, aa + bb)
        y2 = jnp.where(top, cc, cc + dd)
        m1 = jnp.where(top, bb + dd, b1 * k1 - a1 * l1)
        m2 = jnp.where(top, b2 * l1 - b1 * l2, b2 * k2 - a2 * l2)
    else:
        y1 = jnp.where(top, aa, aa - bb)
        y2 = jnp.where(top, cc, cc - dd)
        m1 = jnp.where(top, bb - dd, a1 * l1 + b1 * k1)
        m2 = jnp.where(top, b1 * l2 + b2 * l1, a2 * l2 + b2 * k2)
    return y1, y2, m1, m2


def put_inverse(rhs_e, rhs_o, y, lanes):
    y1, y2, m1, m2 = y
    top = top_row(y1.shape)
    unit = 1.0 / T
    w = jnp.where(top, 0.5 * unit, unit)
    put_split(rhs_e, (y1 + y2) * w, 0, lanes)
    put_split(rhs_o, (y1 - y2) * w, 0, lanes)
    put_split(rhs_e, jnp.where(top, m1, m1 + m2) * unit, H, lanes)
    put_split(rhs_o, jnp.where(top, m2, m1 - m2) * unit, H, lanes)


def lanes_of(block):
    return pl.ds(block * 128, 128)


def short_conv(u_ref, sw_ref, sb_ref, block):
    out = []
    for s in range(3):
        at = lanes_of(s * (C // 128) + block)
        ue, uo = u_ref[pl.ds(0, H), at], u_ref[pl.ds(H, H), at]
        t0, t1, t2 = (sw_ref[j : j + 1, at] for j in range(3))
        bias = sb_ref[0:1, at]
        uo_d = down_one(uo)
        we = t2 * ue + t1 * uo_d + t0 * down_one(ue) + bias
        wo = t2 * uo + t1 * ue + t0 * uo_d + bias
        out.append((we, wo))
    return out


def hdot(a, b, dims=(1, 0)):
    return lax.dot_general(
        a, b, (((dims[0],), (dims[1],)), ((), ())), precision=HIGH, preferred_element_type=F32
    )


def decay_of(half_at, times_ref):
    slow = math.log(0.01) / 1.5
    fast = math.log(0.01) / 0.3
    channel = (half_at * C + lax.broadcasted_iota(jnp.int32, (1, C), 1)).astype(F32)
    rates = jnp.abs(slow + (fast - slow) * channel / (D - 1))
    return jnp.exp(-times_ref[:, 0:1] * rates) + 0.05


def sin_cos(x):
    k = jnp.floor(x * (2 / math.pi) + 0.5)
    r = ((x - k * 1.5703125) - k * 4.837512969970703125e-4) - k * 7.54978995489188e-8
    rr = r * r
    sine = r + r * rr * (-1.6666654611e-1 + rr * (8.3321608736e-3 + rr * -1.9515295891e-4))
    cosine = 1.0 - 0.5 * rr + rr * rr * (
        4.166664568298827e-2 + rr * (-1.388731625493765e-3 + rr * 2.443315711809948e-5)
    )
    quarter = k - 4.0 * jnp.floor(k * 0.25)
    odd = (quarter == 1.0) | (quarter == 3.0)
    s = jnp.where(odd, cosine, sine)
    c = jnp.where(odd, sine, cosine)
    return jnp.where(quarter >= 2.0, -s, s), jnp.where((quarter == 1.0) | (quarter == 2.0), -c, c)


def filter_forward(
    at_ref, feats_ref, times_ref, first_ref, inner_ref, bias_ref, out_ref, fe_ref, fo_ref,
    ks_ref, sin_ref, cos_ref, both_ref, wide_ref, first_s, bias_s, k_s, rhs_e, rhs_o, se, so,
):
    for ref in (both_ref, wide_ref, first_s, bias_s):
        ref[...] = jnp.zeros_like(ref)
    for l in range(2):
        at = pl.ds(l * NET, NET)
        first_s[0:EMB, at] = first_ref[l]
        bias_s[0:3, at] = bias_ref[l]
        wide_ref[l, at, :] = out_ref[l]
        for i in range(2):
            both_ref[i, at, at] = inner_ref[l, i]
    low = feats_ref[...]
    for i in range(3):
        weight = first_s[...] if i == 0 else both_ref[i - 1]
        low, cosine = sin_cos(hdot(low, weight) + bias_s[i : i + 1, :])
        sin_ref[i] = low
        cos_ref[i] = cosine
    decay = decay_of(at_ref[0], times_ref)
    for l in range(2):
        k_s[...] = hdot(sin_ref[2], wide_ref[l]) * decay
        for b in range(C // 128):
            at = lanes_of(b)
            put_split(rhs_e, k_s[pl.ds(0, H), at], 0, at)
            put_split(rhs_o, k_s[pl.ds(H, H), at], 0, at)
        se[...] = dot(fe_ref[...], rhs_e[...])
        so[...] = dot(fo_ref[...], rhs_o[...])
        for b in range(C // 128):
            at = lanes_of(b)
            for i, v in enumerate(butterfly(se, so, at)):
                ks_ref[l, i, :, at] = v


def filter_backward(at_ref, feats_ref, times_ref, inner_ref, out_ref, sin_ref, cos_ref, dk0_ref, dk1_ref, gout_ref, gnet_ref):
    decay = decay_of(at_ref[0], times_ref)
    ds = jnp.zeros((T, 128), F32)
    for l, dk_ref in enumerate((dk0_ref, dk1_ref)):
        dk = dk_ref[...] * decay
        gout_ref[l] = hdot(sin_ref[2], dk, (0, 0))[l * NET : (l + 1) * NET]
        ds += hdot(dk, out_ref[l], (1, 1))
    lane = lax.broadcasted_iota(jnp.int32, (NET, 128), 1)
    gnet_ref[...] = jnp.zeros_like(gnet_ref)
    for i in (2, 1, 0):
        da = ds * cos_ref[i]
        gnet_ref[40 + i : 41 + i, pl.ds(256, 128)] = jnp.sum(da, 0, keepdims=True)
        if i > 0:
            block = hdot(sin_ref[i - 1], da, (0, 0))
            gnet_ref[:, pl.ds((i - 1) * 128, 128)] = jnp.where(lane < NET, block[:NET], block[NET:])
            ds = hdot(da, inner_ref[i - 1], (1, 1))
        else:
            gnet_ref[0:40, pl.ds(256, 128)] = hdot(feats_ref[...], da, (0, 0))[0:40]


def arrange(at_ref, own_ref, other_ref, out_ref, tmp):
    for half, first in ((0, own_ref), (1, other_ref)):
        for b in range(C // 128):
            tmp[b] = first[:, lanes_of(b)].astype(F32)

        def put(first_lane):
            for b in range(C // 128):
                to = pl.ds(first_lane + b * 128, 128)
                out_ref[pl.ds(0, H), to] = tmp[b, pl.ds(0, H, stride=2), :]
                out_ref[pl.ds(H, H), to] = tmp[b, pl.ds(1, H, stride=2), :]

        pl.when(at_ref[0] == half)(functools.partial(put, 0))
        pl.when(at_ref[0] != half)(functools.partial(put, C))


def by_slot(at_ref, src_ref, out_ref, tmp):
    def put(first_lane):
        for b in range(C // 128):
            lanes = pl.ds(first_lane + b * 128, 128)
            tmp[b, pl.ds(0, H, stride=2), :] = src_ref[pl.ds(0, H), lanes]
            tmp[b, pl.ds(1, H, stride=2), :] = src_ref[pl.ds(H, H), lanes]

    pl.when(at_ref[0] == 0)(functools.partial(put, 0))
    pl.when(at_ref[0] != 0)(functools.partial(put, C))
    for b in range(C // 128):
        out_ref[:, lanes_of(b)] = tmp[b].astype(out_ref.dtype)


def finish_result(at_ref, x_ref, own_ref, other_ref, vec_ref, out_ref, x_s, tmp):
    def body(start, c):
        x_s[pl.ds(start, RB), :] = add_branch(x_ref, own_ref, other_ref, vec_ref.at[0], 5, at_ref[1], start, RB)
        return c

    row_loop(body)
    by_slot(at_ref, x_s, out_ref, tmp)


def finish_grad(at_ref, g_ref, own_ref, other_ref, x_ref, vec_ref, out_ref, x_s, tmp):
    def body(start, c):
        at = pl.ds(start, RB)
        dn = own_ref[at, :].astype(F32) + other_ref[at, :].astype(F32)
        x_s[at, :] = g_ref[at, :] + norm_pull(dn, x_ref[at, :], vec_ref[0, 0:1, :])[0]
        return c

    row_loop(body)
    by_slot(at_ref, x_s, out_ref, tmp)


def add_branch(x_ref, own_ref, other_ref, vec_ref, row, length, start, rows):
    at = pl.ds(start, rows)
    y = own_ref[at, :].astype(F32) + other_ref[at, :].astype(F32) + vec_ref[row : row + 1, :]
    return x_ref[at, :] + row_mask(start, rows, length) * y


RB = 128


def row_loop(body, init=0):
    def step(i, c):
        return body(pl.multiple_of(i * RB, RB), c)

    return lax.fori_loop(0, T // RB, step, init)


def mixer_forward(joined, *refs):
    at_ref, x_ref = refs[:2]
    refs = refs[2:]
    if joined:
        own_ref, other_ref, prev_ref = refs[:3]
        refs = refs[3:]
    (vec_ref, inw_ref, inb_ref, sw_ref, sb_ref, ks_ref, skip_ref, fe_ref, fo_ref, ie_ref, io_ref, outw_ref) = refs[:12]
    refs = refs[12:]
    if joined:
        xo_ref = refs[0]
        refs = refs[1:]
    u_ref, qs_ref, g_ref, p_ref, a_s, w0_s, q_s, rhs_e, rhs_o, se, so, rhs2_e, rhs2_o, z_s = refs

    def first(start, c):
        at = pl.ds(start, RB)
        if joined:
            x = add_branch(x_ref, own_ref, other_ref, prev_ref.at[0], 5, at_ref[1], start, RB)
            xo_ref[at, :] = x
        else:
            x = x_ref[at, :]
        xhat, _ = normalize(x)
        a_s[at, :] = (xhat * vec_ref[0, 0:1, :] + vec_ref[0, 1:2, :]).astype(BF)
        return c

    row_loop(first)
    for s in range(3):
        at = pl.ds(s * C, C)
        u_ref[:, at] = dot(a_s[...], inw_ref[0, s]) + inb_ref[0, 0:1, at]
    for b in range(C // 128):
        at = lanes_of(b)
        (w0e, w0o), (w1e, w1o), (w2e, w2o) = short_conv(u_ref, sw_ref.at[0], sb_ref.at[0], b)
        w0_s[pl.ds(0, H), at] = w0e
        w0_s[pl.ds(H, H), at] = w0o
        qe, qo = w2e * w1e, w2o * w1o
        q_s[pl.ds(0, H), at] = qe
        q_s[pl.ds(H, H), at] = qo
        put_split(rhs_e, qe, 0, at)
        put_split(rhs_o, qo, 0, at)
    se[...] = dot(fe_ref[...], rhs_e[...])
    so[...] = dot(fo_ref[...], rhs_o[...])
    for b in range(C // 128):
        at = lanes_of(b)
        spec = butterfly(se, so, at)
        for i, v in enumerate(spec):
            qs_ref[i, :, at] = v
        y = spectrum_product(spec, [ks_ref[0, i, :, at] for i in range(4)], False)
        put_inverse(rhs2_e, rhs2_o, y, at)
    se[pl.ds(0, H), :] = dot(ie_ref[...], rhs2_e[...])
    se[pl.ds(H, H), :] = dot(io_ref[...], rhs2_o[...])

    def last(start, c):
        at = pl.ds(start, RB)
        g = se[at, :] + skip_ref[0, 0:1, :] * q_s[at, :]
        g_ref[at, :] = g
        z_s[at, :] = (g * w0_s[at, :]).astype(BF)
        return c

    row_loop(last)
    p_ref[...] = dot(z_s[...], outw_ref[0]).astype(BF)


def gelu_parts(h):
    c0 = math.sqrt(2 / math.pi)
    hh = h * h
    t = jnp.tanh(c0 * (h + 0.044715 * (hh * h)))
    half = 0.5 * (1.0 + t)
    return half, t, hh, c0


def collect(j, acc, part):
    @pl.when(j == 0)
    def _():
        acc[...] = part

    @pl.when(j > 0)
    def _():
        acc[...] += part


def ff_forward(at_ref, x_ref, own_ref, other_ref, vec_ref, up_ref, upb_ref, dn_ref, xo_ref, h_ref, p_ref, b_s, acc):
    j = pl.program_id(0)

    @pl.when(j == 0)
    def _():
        def first(start, c):
            at = pl.ds(start, RB)
            x = add_branch(x_ref, own_ref, other_ref, vec_ref.at[0], 4, at_ref[1], start, RB)
            xo_ref[at, :] = x
            xhat, _ = normalize(x)
            b_s[at, :] = (xhat * vec_ref[0, 2:3, :] + vec_ref[0, 3:4, :]).astype(BF)
            return c

        row_loop(first)

    h = dot(b_s[...], up_ref[0]) + upb_ref[0]
    h_ref[...] = h
    half, _, _, _ = gelu_parts(h)
    collect(j, acc, dot((h * half).astype(BF), dn_ref[0]))

    @pl.when(j == pl.num_programs(0) - 1)
    def _():
        p_ref[...] = acc[...].astype(BF)


def ff_backward(joined, *refs):
    at_ref, g_ref = refs[:2]
    refs = refs[2:]
    if joined:
        own_ref, other_ref, xn_ref, nvec_ref = refs[:4]
        refs = refs[4:]
    x_ref, h_ref, vec_ref, up_ref, dn_ref = refs[:5]
    refs = refs[5:]
    if joined:
        go_ref, ngrad_ref = refs[:2]
        refs = refs[2:]
    e_ref, dh_ref, dm_ref, b_ref, gupb_ref, gdnb_ref, p_ref, acc = refs
    j = pl.program_id(0)

    @pl.when(j == 0)
    def _():
        def first(start, c):
            at = pl.ds(start, RB)
            g = g_ref[at, :]
            sums, s1, s2 = c
            if joined:
                dn = own_ref[at, :].astype(F32) + other_ref[at, :].astype(F32)
                dx, dg = norm_pull(dn, xn_ref[at, :], nvec_ref[0, 0:1, :])
                g = g + dx
                go_ref[at, :] = g
                s1 = s1 + jnp.sum(dg, 0, keepdims=True)
                s2 = s2 + jnp.sum(dn, 0, keepdims=True)
            dm = (row_mask(start, RB, at_ref[1]) * g).astype(BF)
            dm_ref[at, :] = dm
            xhat, _ = normalize(x_ref[at, :])
            b_ref[at, :] = (xhat * vec_ref[0, 2:3, :] + vec_ref[0, 3:4, :]).astype(BF)
            return sums + jnp.sum(dm.astype(F32), 0, keepdims=True), s1, s2

        zero = jnp.zeros((1, D), F32)
        sums, s1, s2 = row_loop(first, (zero, zero, zero))
        gdnb_ref[...] = sums
        if joined:
            ngrad_ref[0:1, :] = s1
            ngrad_ref[1:2, :] = s2

    h = h_ref[...]
    half, t, hh, c0 = gelu_parts(h)
    e_ref[...] = (h * half).astype(BF)
    slope = half + 0.5 * c0 * h * (1.0 - t * t) * (1.0 + 3 * 0.044715 * hh)
    dh = (dot_nt(dm_ref[...], dn_ref[0]) * slope).astype(BF)
    dh_ref[...] = dh
    gupb_ref[...] = jnp.sum(dh.astype(F32), 0, keepdims=True)
    collect(j, acc, dot_nt(dh, up_ref[0]))

    @pl.when(j == pl.num_programs(0) - 1)
    def _():
        p_ref[...] = acc[...].astype(BF)


FIRST, SECOND = 5, 6


def put_pieces(at_ref, ref, first, value):
    for n in range(value.shape[0] // PIECE):
        block = first + n // 4
        at = lax.rem(block - at_ref[FIRST] + 4, 4), lax.rem(n % 4 - at_ref[SECOND] + 4, 4), pl.ds(0, PIECE)
        ref[at] = value[n * PIECE : (n + 1) * PIECE]


def put_halves(at_ref, keep_ref, give_ref, first, low, high):
    @pl.when(at_ref[4] == 0)
    def _():
        put_pieces(at_ref, keep_ref, first, low)
        put_pieces(Swapped(at_ref), give_ref, first, high)

    @pl.when(at_ref[4] != 0)
    def _():
        put_pieces(at_ref, keep_ref, first, high)
        put_pieces(Swapped(at_ref), give_ref, first, low)


class Swapped:
    def __init__(self, at_ref):
        self.at_ref = at_ref

    def __getitem__(self, i):
        return self.at_ref[{FIRST: SECOND, SECOND: FIRST}.get(i, i)]


def ff_weights(at_ref, e_ref, dm_ref, b_ref, dh_ref, keep_ref, give_ref):
    j = pl.program_id(0)
    down = dot_tn(e_ref[...], dm_ref[...]).astype(BF)
    up = dot_tn(dh_ref[...], b_ref[...]).astype(BF)
    put_halves(at_ref, keep_ref, give_ref, 2 * j, down, up)


def mixer_backward(
    last, at_ref, g_in_ref, own_ref, other_ref, x1_ref, x0_ref, u_ref, qs_ref, g_ref, ks_ref, vec_ref, inw_ref, outw_ref,
    sw_ref, sb_ref, skip_ref, fe_ref, fo_ref, ie_ref, io_ref,
    go_ref, ngrad_ref, goutb_ref, ginb_ref, gsw_ref, gsb_ref, gskip_ref, dk_ref, p_ref, dy_ref, a_ref, z_ref, du_ref,
    nown_ref, dz_s, dg_s, w1_s, w2_s, dw0_s, rhs_e, rhs_o, se, so, rhs2_e, rhs2_o, inv_s,
):
    def first(start, c):
        at = pl.ds(start, RB)
        sums, s1, s2 = c
        dn = own_ref[at, :].astype(F32) + other_ref[at, :].astype(F32)
        dx, dg = norm_pull(dn, x1_ref[at, :], vec_ref[0, 2:3, :])
        g = g_in_ref[at, :] + dx
        go_ref[at, :] = g
        dy = (row_mask(start, RB, at_ref[1]) * g).astype(BF)
        dy_ref[at, :] = dy
        xhat, _ = normalize(x0_ref[at, :])
        a_ref[at, :] = (xhat * vec_ref[0, 0:1, :] + vec_ref[0, 1:2, :]).astype(BF)
        return (
            sums + jnp.sum(dy.astype(F32), 0, keepdims=True),
            s1 + jnp.sum(dg, 0, keepdims=True),
            s2 + jnp.sum(dn, 0, keepdims=True),
        )

    zero = jnp.zeros((1, D), F32)
    sums, s1, s2 = row_loop(first, (zero, zero, zero))
    goutb_ref[...] = sums
    ngrad_ref[0:1, :] = s1
    ngrad_ref[1:2, :] = s2
    dz_s[...] = dot_nt(dy_ref[...], outw_ref[0])
    halves = (pl.ds(0, H), pl.ds(H, H))
    for b in range(C // 128):
        at = lanes_of(b)
        w0, w1, w2 = short_conv(u_ref, sw_ref.at[0], sb_ref.at[0], b)
        dskip = 0.0
        for i, (rows, rhs) in enumerate(zip(halves, (rhs_e, rhs_o))):
            dz, g = dz_s[rows, at], g_ref[rows, at]
            z_ref[rows, at] = (g * w0[i]).astype(BF)
            dw0_s[rows, at] = dz * g
            dg = dz * w0[i]
            dg_s[rows, at] = dg
            dskip = dskip + jnp.sum(dg * (w2[i] * w1[i]), 0, keepdims=True)
            w1_s[rows, at] = w1[i]
            w2_s[rows, at] = w2[i]
            put_split(rhs, dg, 0, at)
        gskip_ref[0:1, at] = dskip
    se[...] = dot(fe_ref[...], rhs_e[...])
    so[...] = dot(fo_ref[...], rhs_o[...])
    for b in range(C // 128):
        at = lanes_of(b)
        spec = butterfly(se, so, at)
        put_inverse(rhs2_e, rhs2_o, spectrum_product(spec, [ks_ref[0, i, :, at] for i in range(4)], True), at)
        put_inverse(
            rhs2_e, rhs2_o, spectrum_product(spec, [qs_ref[i, :, at] for i in range(4)], True), pl.ds(C + b * 128, 128)
        )
    inv_s[pl.ds(0, H), :] = dot(ie_ref[...], rhs2_e[...])
    inv_s[pl.ds(H, H), :] = dot(io_ref[...], rhs2_o[...])
    dk_ref[...] = inv_s[:, pl.ds(C, C)]
    for b in range(C // 128):
        at = lanes_of(b)
        dw = [[dw0_s[rows, at] for rows in halves], [], []]
        for rows in halves:
            dq = inv_s[rows, at] + skip_ref[0, 0:1, at] * dg_s[rows, at]
            dw[1].append(dq * w2_s[rows, at])
            dw[2].append(dq * w1_s[rows, at])
        for s in range(3):
            to = lanes_of(s * (C // 128) + b)
            ue, uo = u_ref[halves[0], to], u_ref[halves[1], to]
            t0, t1, t2 = (sw_ref[0, j : j + 1, to] for j in range(3))
            de, do = dw[s]
            de_u, do_u = up_one(de), up_one(do)
            due = (t2 * de + t1 * do + t0 * de_u).astype(BF)
            duo = (t2 * do + t1 * de_u + t0 * do_u).astype(BF)
            du_ref[halves[0], to] = due
            du_ref[halves[1], to] = duo
            uo_d = down_one(uo)
            gsw_ref[0:1, to] = jnp.sum(de * down_one(ue) + do * uo_d, 0, keepdims=True)
            gsw_ref[1:2, to] = jnp.sum(de * uo_d + do * ue, 0, keepdims=True)
            gsw_ref[2:3, to] = jnp.sum(de * ue + do * uo, 0, keepdims=True)
            gsb_ref[0:1, to] = jnp.sum(de + do, 0, keepdims=True)
            ginb_ref[0:1, to] = jnp.sum(due.astype(F32) + duo.astype(F32), 0, keepdims=True)
    part = dot_nt(du_ref[:, pl.ds(0, C)], inw_ref[0, 0])
    for s in range(1, 3):
        part += dot_nt(du_ref[:, pl.ds(s * C, C)], inw_ref[0, s])
    p_ref[...] = part.astype(BF)
    nown_ref[...] = jnp.zeros_like(nown_ref)
    if last:

        def terms(start, c):
            at = pl.ds(start, RB)
            dn = p_ref[at, :].astype(F32)
            xhat, _ = normalize(x0_ref[at, :])
            return c[0] + jnp.sum(dn * xhat, 0, keepdims=True), c[1] + jnp.sum(dn, 0, keepdims=True)

        s1, s2 = row_loop(terms, (zero, zero))
        nown_ref[0:1, :] = s1
        nown_ref[1:2, :] = s2


def put_split_rows(value):
    hi = value.astype(BF).astype(F32)
    return jnp.concatenate([hi, value - hi], 0).astype(BF)


def put_pack(at_ref, ref, rows, half):
    for n in range(16):
        at = lax.rem(n // 4 - at_ref[FIRST] + 4, 4), lax.rem(n % 4 - at_ref[SECOND] + 4, 4), pl.ds(PIECE, 16)
        first = half * (PACK // 2) + n * 8
        ref[at] = put_split_rows(rows[first : first + 8, :])


def mixer_weights(packed, at_ref, *refs):
    if packed:
        pack_ref, refs = refs[0], refs[1:]
    a_ref, du_ref, z_ref, dy_ref, keep_ref, give_ref = refs
    for n in range(2):
        low = dot_tn(a_ref[...], du_ref[:, pl.ds(n * C, C)]).astype(BF)
        if n == 0:
            high = dot_tn(a_ref[...], du_ref[:, pl.ds(2 * C, C)]).astype(BF)
        else:
            high = dot_tn(dy_ref[...], z_ref[...]).astype(BF)
        put_halves(at_ref, keep_ref, give_ref, 2 * n, low, high)
    if packed:

        @pl.when(at_ref[4] == 0)
        def _():
            put_pack(at_ref, keep_ref, pack_ref, 0)
            put_pack(Swapped(at_ref), give_ref, pack_ref, 1)

        @pl.when(at_ref[4] != 0)
        def _():
            put_pack(at_ref, keep_ref, pack_ref, 1)
            put_pack(Swapped(at_ref), give_ref, pack_ref, 0)


def add_parts(count, sides, *refs):
    ins, outs = refs[:count], refs[count:]
    lane = 0
    for side in range(sides):
        some = ins[side * count // sides : (side + 1) * count // sides]
        lanes = slice(lane, lane + some[0].shape[-1])
        lane = lanes.stop
        for i, out in enumerate(outs):
            total = functools.reduce(jnp.add, [(r[i] if len(outs) > 1 else r[...]).astype(F32) for r in some])
            rows = (slice(None),) * (total.ndim - 2)
            out[rows + (slice(0, PIECE), lanes)] = total[rows + (slice(0, PIECE),)].astype(BF)
            if total.shape[-2] > PIECE:
                for n in range(total.shape[0] if total.ndim > 2 else 1):
                    value = total[n] if total.ndim > 2 else total
                    value = value[PIECE : PIECE + 8] + value[PIECE + 8 : PIECE + 16]
                    to = (n, slice(PIECE, PIECE + 16)) if total.ndim > 2 else slice(PIECE, PIECE + 16)
                    out[to] = put_split_rows(value)


def gather_block(at_ref, ref, block, tmp, first_lane, pack_ref=None, first=0):
    width = tmp.shape[-1]
    lanes = slice(first_lane, first_lane + width)
    for m in range(4):
        if len(ref.shape) == 5:
            by_x = (at_ref[4] == 0) != isinstance(at_ref, Swapped)
            at = 0, jnp.where(by_x, m, block), jnp.where(by_x, block, m)
        else:
            at = lax.rem(at_ref[FIRST] - block + 4, 4), lax.rem(at_ref[SECOND] - m + 4, 4)
        tmp[pl.ds(m * PIECE, PIECE), :] = ref[at + (slice(0, PIECE), lanes)].astype(F32)
        if pack_ref is not None:
            extra = ref[at + (slice(PIECE, PIECE + 16),)].astype(F32)
            pack_ref[pl.ds(pl.multiple_of(first + m * 8, 8), 8), :] = extra[:8] + extra[8:]


def gather_half(at_ref, half, refs, *args):
    own = at_ref[4] == half
    pl.when(own)(lambda: gather_block(at_ref, refs[0], *args))
    pl.when(jnp.logical_not(own))(lambda: gather_block(Swapped(at_ref), refs[1], *args))


def place_ff(at_ref, *refs):
    ins, (gup_ref, gdn_ref, tmp) = refs[:2], refs[-3:]
    block = pl.program_id(0)
    gather_half(at_ref, 0, ins, block, tmp, 0)
    gdn_ref[0] = tmp[...]
    gather_half(at_ref, 1, ins, block, tmp, 0)
    gup_ref[0] = tmp[...].T


def place_mixer(packed, lane, at_ref, *refs):
    ins, outs, tmp = refs[:2], refs[2:-1], refs[-1]
    gin_ref, gout_ref = outs[:2]
    step = pl.program_id(0)
    args = ins, lax.rem(step, 4), tmp, lane, outs[2] if packed else None, step * 32
    gather_half(at_ref, step // 4, *args)

    @pl.when(step < 6)
    def _():
        gin_ref[0, 0] = tmp[...]

    @pl.when(step >= 6)
    def _():
        gout_ref[0] = tmp[...].T


PACK = 256
SHARED = 72
LAYER_ROWS = 92


def pack_small(at_ref, gnet_ref, gout_ref, nown_ref, *refs):
    out_ref = refs[-1]
    out_ref[...] = jnp.zeros_like(out_ref)
    out_ref[0:NET, :] = gnet_ref[...]
    for j in range(2):
        for i in range(2):
            row = NET + 2 * j + i
            out_ref[row : row + 1, :] = nown_ref[j : j + 1, i * C : (i + 1) * C]
    for l in range(2):
        n0, n1, gdnb, goutb, gupb, ginb, gsw, gsb, gskip = refs[9 * l : 9 * l + 9]
        row = SHARED + LAYER_ROWS * l

        def put(value):
            nonlocal row
            out_ref[row : row + value.shape[0], :] = value
            row += value.shape[0]

        for ref in (n0, n1, gdnb, goutb):
            put(jnp.where(at_ref[0] == 0, ref[:, :C], ref[:, C:]))
        for ref in (gupb, ginb, gsw, gsb):
            for j in range(ref.shape[0]):
                for i in range(ref.shape[1] // C):
                    put(ref[j : j + 1, i * C : (i + 1) * C])
        put(gskip[...])
        put(gout_ref[l])


def sds(shape, dtype=F32):
    return jax.ShapeDtypeStruct(shape, dtype)


def params(us):
    return dict(
        compiler_params=pltpu.CompilerParams(vmem_limit_bytes=VMEM_LIMIT),
        cost_estimate=pl.CostEstimate(flops=int(us * 1e9), bytes_accessed=10000, transcendentals=0),
    )


SMEM = pl.BlockSpec(memory_space=pltpu.SMEM)
WHOLE = pl.BlockSpec(memory_space=pltpu.VMEM)
ANY = pl.BlockSpec(memory_space=pl.ANY)
SLOTS = pltpu.VMEM((C // 128, T, 128), F32)


def layer_of(x, l):
    rest = x.ndim - 1
    return pl.BlockSpec((1,) + x.shape[1:], lambda *_: (l,) + (0,) * rest, pipeline_mode=pl.Buffered(1))


def fixed(shape):
    return pl.BlockSpec(shape, lambda *_: (0,) * len(shape))


def spectrum_scratch():
    return [pltpu.VMEM((3 * H, C), BF)] * 2 + [pltpu.VMEM((T, C), F32)] * 2


def run_filter_forward(at, first, inner, bias, out):
    layers = out.shape[0]
    return pl.pallas_call(
        filter_forward,
        in_specs=[SMEM] + [WHOLE] * 8,
        out_specs=[WHOLE] * 5,
        out_shape=[
            sds((layers, 4, H, C)), sds((3, T, 128)), sds((3, T, 128)), sds((2, 128, 128)), sds((layers, 128, C)),
        ],
        scratch_shapes=[pltpu.VMEM((128, 128), F32), pltpu.VMEM((8, 128), F32), pltpu.VMEM((T, C), F32)]
        + spectrum_scratch(),
        name="filter_forward",
        **params(12),
    )(at, FEATS, TIMES, first, inner, bias, out, FE, FO)


def run_filter_backward(at, inner, out, sines, cosines, dks):
    return pl.pallas_call(
        filter_backward,
        in_specs=[SMEM] + [WHOLE] * 8,
        out_specs=[WHOLE] * 2,
        out_shape=[sds((2, NET, C)), sds((NET, C))],
        name="filter_backward",
        **params(8),
    )(at, FEATS, TIMES, inner, out, sines, cosines, *dks)


def run_arrange(at, own, other):
    return pl.pallas_call(
        arrange,
        in_specs=[SMEM, WHOLE, WHOLE],
        out_specs=WHOLE,
        out_shape=sds((T, D)),
        scratch_shapes=[SLOTS],
        name="arrange",
        **params(2),
    )(at, own, other)


def run_finish_result(at, x, own, other, vec, l):
    return pl.pallas_call(
        finish_result,
        grid=(1,),
        in_specs=[SMEM, WHOLE, WHOLE, WHOLE, layer_of(vec, l)],
        out_specs=WHOLE,
        out_shape=sds((T, C), BF),
        scratch_shapes=[pltpu.VMEM((T, D), F32), SLOTS],
        name="finish_result",
        **params(3),
    )(at, x, own, other, vec)


def run_finish_grad(at, g, own, other, x, vec, l, after):
    return pl.pallas_call(
        functools.partial(body_without, finish_grad, 6, len(after)),
        grid=(1,),
        in_specs=[SMEM, WHOLE, WHOLE, WHOLE, WHOLE, layer_of(vec, l)] + [ANY] * len(after),
        out_specs=WHOLE,
        out_shape=sds((T, C)),
        scratch_shapes=[pltpu.VMEM((T, D), F32), SLOTS],
        name="finish_grad",
        **params(4),
    )(at, g, own, other, x, vec, *after)


def run_mixer_forward(l, joint, at, x, vec, inw, inb, sw, sb, ks, skip, outw, after):
    joined = joint is not None
    args = [at, x] + (list(joint) + [vec] if joined else [])
    specs = [SMEM] + [WHOLE] * 3 + [layer_of(vec, l - 1)] if joined else [SMEM, WHOLE]
    args += [vec, inw, inb, sw, sb, ks, skip, FE, FO, IE, IO, outw]
    specs += [layer_of(m, l) for m in (vec, inw, inb, sw, sb, ks, skip)] + [WHOLE] * 4 + [layer_of(outw, l)]
    outs = ([sds((T, D))] if joined else []) + [sds((T, 3 * C)), sds((4, H, C)), sds((T, C)), sds((T, D), BF)]
    return pl.pallas_call(
        functools.partial(body_without, functools.partial(mixer_forward, joined), len(args), len(after)),
        grid=(1,),
        in_specs=specs + [ANY] * len(after),
        out_specs=[WHOLE] * len(outs),
        out_shape=outs,
        scratch_shapes=[pltpu.VMEM((T, D), BF), pltpu.VMEM((T, C), F32), pltpu.VMEM((T, C), F32)]
        + spectrum_scratch()
        + [pltpu.VMEM((6 * H, C), BF)] * 2
        + [pltpu.VMEM((T, C), BF)],
        name="mixer_forward",
        **params(11),
    )(*args, *after)


FC = 512


def up_spec(l):
    return pl.BlockSpec((1, D, FC), lambda j: (l, 0, j))


def down_spec(l):
    return pl.BlockSpec((1, FC, D), lambda j: (l, j, 0))


def hidden_spec(rows, width=FC):
    return pl.BlockSpec((rows, width), lambda j: (0, j))


def run_ff_forward(l, at, x, own, other, vec, up, upb, dn, after):
    return pl.pallas_call(
        functools.partial(body_without, ff_forward, 8, len(after)),
        grid=(FH // FC,),
        in_specs=[
            SMEM, fixed((T, D)), fixed((T, D)), fixed((T, D)), layer_of(vec, l),
            up_spec(l), pl.BlockSpec((1, 1, FC), lambda j: (l, 0, j)), down_spec(l),
        ] + [ANY] * len(after),
        out_specs=[fixed((T, D)), hidden_spec(T), fixed((T, D))],
        out_shape=[sds((T, D)), sds((T, FH)), sds((T, D), BF)],
        scratch_shapes=[pltpu.VMEM((T, D), BF), pltpu.VMEM((T, D), F32)],
        name="ff_forward",
        **params(10),
    )(at, x, own, other, vec, up, upb, dn, *after)


def run_ff_backward(l, at, g, joint, x, h, vec, up, dn, after):
    joined = joint is not None
    args = [at, g] + (list(joint) + [vec] if joined else []) + [x, h, vec, up, dn]
    specs = [SMEM, fixed((T, D))]
    if joined:
        specs += [fixed((T, D))] * 3 + [layer_of(vec, l + 1)]
    specs += [fixed((T, D)), hidden_spec(T), layer_of(vec, l), up_spec(l), down_spec(l)]
    out_specs = [fixed((T, D)), fixed((2, D))] if joined else []
    outs = [sds((T, D)), sds((2, D))] if joined else []
    out_specs += [hidden_spec(T), hidden_spec(T), fixed((T, D)), fixed((T, D)), hidden_spec(1), fixed((1, D)), fixed((T, D))]
    outs += [
        sds((T, FH), BF), sds((T, FH), BF), sds((T, D), BF), sds((T, D), BF), sds((1, FH)), sds((1, D)), sds((T, D), BF),
    ]
    return pl.pallas_call(
        functools.partial(body_without, functools.partial(ff_backward, joined), len(args), len(after)),
        grid=(FH // FC,),
        in_specs=specs + [ANY] * len(after),
        out_specs=out_specs,
        out_shape=outs,
        scratch_shapes=[pltpu.VMEM((T, D), F32)],
        name="ff_backward",
        **params(10),
    )(*args, *after)


def run_ff_weights(at, e, dm, b, dh):
    wide = FH // 2
    return pl.pallas_call(
        ff_weights,
        grid=(2,),
        in_specs=[SMEM, hidden_spec(T, wide), fixed((T, D)), fixed((T, D)), hidden_spec(T, wide)],
        out_specs=[fixed((4, 4, PIECE, D))] * 2,
        out_shape=[sds((4, 4, PIECE, D), BF)] * 2,
        name="ff_weights",
        **params(7),
    )(at, e, dm, b, dh)


def run_mixer_backward(l, last, at, g_in, own, other, x1, x0, u, qs, g, ks, vec, inw, outw, sw, sb, skip, after):
    args = [at, g_in, own, other, x1, x0, u, qs, g, ks, vec, inw, outw, sw, sb, skip, FE, FO, IE, IO]
    specs = [SMEM] + [WHOLE] * 8 + [layer_of(m, l) for m in (ks, vec, inw, outw, sw, sb, skip)] + [WHOLE] * 4
    outs = [
        sds((T, D)), sds((2, D)), sds((1, D)), sds((1, 3 * C)), sds((3, 3 * C)), sds((1, 3 * C)), sds((1, C)),
        sds((T, C)), sds((T, D), BF), sds((T, D), BF), sds((T, D), BF), sds((T, C), BF), sds((T, 3 * C), BF), sds((2, D)),
    ]
    tc = pltpu.VMEM((T, C), F32)
    return pl.pallas_call(
        functools.partial(body_without, functools.partial(mixer_backward, last), len(args), len(after)),
        grid=(1,),
        in_specs=specs + [ANY] * len(after),
        out_specs=[WHOLE] * len(outs),
        out_shape=outs,
        scratch_shapes=[
            tc, tc, tc, tc, tc, *spectrum_scratch(),
            pltpu.VMEM((6 * H, 2 * C), BF), pltpu.VMEM((6 * H, 2 * C), BF), pltpu.VMEM((T, 2 * C), F32),
        ],
        name="mixer_backward",
        **params(15),
    )(*args, *after)


def run_mixer_weights(at, a, du, z, dy, pack=None):
    packed = [] if pack is None else [pack]
    rows = PIECE + 16 * len(packed)
    return pl.pallas_call(
        functools.partial(mixer_weights, bool(packed)),
        in_specs=[SMEM] + [WHOLE] * (4 + len(packed)),
        out_specs=[WHOLE] * 2,
        out_shape=[sds((4, 4, rows, C), BF)] * 2,
        name="mixer_weights",
        **params(5),
    )(at, *packed, a, du, z, dy)


def run_add(parts, count, after=(), sides=1):
    shape = parts[0].shape[1:] if count > 1 else parts[0].shape
    width = sum(p.shape[-1] for p in parts[:: len(parts) // sides])
    made = pl.pallas_call(
        functools.partial(body_without, functools.partial(add_parts, len(parts), sides), len(parts), len(after)),
        in_specs=[WHOLE] * len(parts) + [ANY] * len(after),
        out_specs=[WHOLE] * count,
        out_shape=[sds(shape[:-1] + (width,), BF)] * count,
        name="add_parts",
        **params(1),
    )(*parts, *after)
    return list(made)


def copy(ref, out_ref):
    out_ref[...] = ref[...]


def run_copy_after(x, after):
    return pl.pallas_call(
        functools.partial(body_without, copy, 1, len(after)),
        in_specs=[WHOLE] + [ANY] * len(after),
        out_specs=WHOLE,
        out_shape=sds(x.shape, x.dtype),
        name="copy_after",
        **params(1),
    )(x, *after)


def run_place(body, at, ins, into, shapes, out_specs, steps, width, name):
    aliases = {} if into is None else {3: 0, 4: 1}
    into = [] if into is None else list(into)
    return pl.pallas_call(
        functools.partial(body_without, body, 3, len(into)),
        grid=(steps,),
        in_specs=[SMEM] + [fixed(m.shape) for m in ins] + [ANY] * len(into),
        out_specs=out_specs,
        out_shape=[sds(s) for s in shapes],
        scratch_shapes=[pltpu.VMEM((4 * PIECE, width), F32)],
        input_output_aliases=aliases,
        name=name,
        **params(6),
    )(at, *ins, *into)


def body_without(body, first, count, *refs):
    body(*refs[:first], *refs[first + count :])


def run_place_ff(l, layers, at, ins, into):
    specs = [
        pl.BlockSpec((1, D, 4 * PIECE), lambda p: (l, 0, p)),
        pl.BlockSpec((1, 4 * PIECE, D), lambda p: (l, p, 0)),
    ]
    return run_place(place_ff, at, ins, into, [(layers, D, FH), (layers, FH, D)], specs, 4, D, "place_ff")


def run_place_mixer(l, layers, at, ins, into, lane):
    packed = ins[0].shape[-2] > PIECE
    specs = [
        pl.BlockSpec((1, 1, C, C), lambda n: (l, jnp.minimum(n, 5) // 2, jnp.minimum(n, 5) % 2, 0)),
        pl.BlockSpec((1, C, C), lambda n: (l, 0, jnp.maximum(n - 6, 0))),
    ] + [fixed((PACK, C))] * packed
    shapes = [(layers, 3, D, C), (layers, C, D)] + [(PACK, C)] * packed
    body = functools.partial(place_mixer, packed, lane)
    return run_place(body, at, ins, into, shapes, specs, 8, C, "place_mixer")


SWAP = [(0, 1), (1, 0)]


def swap(x, axis):
    return lax.ppermute(x, axis, SWAP)


def shift(x, axis, k):
    pairs = []
    for y, x_at, c in np.ndindex(4, 4, 2):
        along_x = (axis == FIRST) == (c == 0)
        to = (y, (x_at + k) % 4) if along_x else ((y + k) % 4, x_at)
        pairs.append(((y * 4 + x_at) * 2 + c, (to[0] * 4 + to[1]) * 2 + c))
    return lax.ppermute(x, ("y", "x", "c"), pairs)


def spread_sum(*halves):
    after = yield [h for pair in halves for h in pair]
    parts = [part for keep, give in halves for part in (keep, swap(give, "c"))]
    blocks = run_add(parts, 4, after, len(halves))
    after = yield blocks
    pieces = run_add([blocks[0]] + [shift(blocks[k], FIRST, k) for k in range(1, 4)], 4, after)
    after = yield pieces
    [piece] = run_add([pieces[0]] + [shift(pieces[m], SECOND, m) for m in range(1, 4)], 1, after)
    yield run_add([piece, swap(piece, "zl")], 1)


def gather_near(piece):
    row = jnp.stack([piece] + [shift(piece, SECOND, m) for m in range(1, 4)])
    mine = jnp.stack([row] + [shift(row, FIRST, k) for k in range(1, 4)])
    return [mine, swap(mine, "c")]


def gather_plane(piece):
    mine = lax.all_gather(piece, ("y", "x"), axis=0, tiled=False)
    mine = mine.reshape(1, 4, 4, *piece.shape)
    return [mine, swap(mine, "c")]


def run_pack_small(at, gnet, gout, nown, small):
    return pl.pallas_call(
        pack_small,
        in_specs=[SMEM] + [WHOLE] * (3 + len(small)),
        out_specs=WHOLE,
        out_shape=sds((PACK, C)),
        name="pack_small",
        **params(2),
    )(at, gnet, gout, nown, *small)


def shards(
    tokens, lengths, norm_gain, norm_bias, in_weight, in_bias, short_weight, short_bias, filter_first, filter_inner,
    filter_biases, filter_out, filter_skip, out_weight, out_bias, up_weight, up_bias, down_weight, down_bias, cotangent,
):
    layers = norm_gain.shape[0]
    half_at = lax.axis_index("zh")
    core = lax.axis_index("c")
    x_at, y_at = lax.axis_index("x"), lax.axis_index("y")
    order = jnp.where(core == 0, x_at, y_at), jnp.where(core == 0, y_at, x_at)
    at = jnp.stack([half_at, lengths[0], x_at, y_at, core, *order]).astype(jnp.int32)

    tokens_other = swap(tokens, "zh")
    rows = jnp.stack(
        [norm_gain[:, 0], norm_bias[:, 0], norm_gain[:, 1], norm_bias[:, 1], out_bias, down_bias, out_bias, out_bias], 1
    )
    other = swap(rows, "zh")
    low = half_at == 0
    vec = jnp.concatenate([jnp.where(low, rows, other), jnp.where(low, other, rows)], 2)

    ks, sines, cosines, inner, fout = run_filter_forward(at, filter_first, filter_inner, filter_biases, filter_out)

    x = run_arrange(at, tokens, tokens_other)
    inw = in_weight.transpose(0, 2, 1, 3)
    inb = in_bias.reshape(layers, 1, 3 * C)
    sw = short_weight.reshape(layers, 3, 3 * C)
    sb = short_bias.reshape(layers, 1, 3 * C)
    skip = filter_skip.reshape(layers, 1, C)
    upb = up_bias.reshape(layers, 1, FH)

    cot = run_copy_after(cotangent, [x])
    grad = run_arrange(at, cotangent, swap(cot, "zh"))
    saved = []
    joint = None
    for l in range(layers):
        after = [cot] if l == 0 else []
        made = run_mixer_forward(l, joint, at, x, vec, inw, inb, sw, sb, ks, skip, out_weight, after)
        if joint is not None:
            x, made = made[0], made[1:]
        u, qs, g, p = made
        after = [grad] if l == 0 else []
        x1, h, p2 = run_ff_forward(l, at, x, p, swap(p, "zh"), vec, up_weight, upb, down_weight, after)
        saved.append((x, u, qs, g, x1, h))
        joint = (p2, swap(p2, "zh")) if l < layers - 1 else p2
        x = x1

    joint = None
    sums = []
    small = [None] * layers
    norms = {}

    def advance(after):
        made = []
        for entry in sums:
            try:
                entry[1] = entry[0].send(after) if entry[1] else next(entry[0])
            except StopIteration:
                pass
            made += entry[1]
        return made

    def begin(*halves):
        sums.append([spread_sum(*halves), []])

    result = None
    waits = []
    for l in reversed(range(layers)):
        x0, u, qs, g, x1, h = saved[l]
        made = run_ff_backward(l, at, grad, joint, x1, h, vec, up_weight, down_weight, waits)
        if joint is not None:
            grad, norms[l + 1] = made[:2]
            made = made[2:]
        e, dh, dm, b, gupb, gdnb, p = made
        p_other = swap(p, "zh")
        halves = run_ff_weights(at, e, dm, b, dh)
        if l == 0:
            begin(halves)
        waits = advance([p]) if l == 0 else list(halves)
        if l == layers - 1:
            p2 = run_copy_after(p2, [p_other])
            waits.append(p2)
        made = run_mixer_backward(
            l, l == 0, at, grad, p, p_other, x1, x0, u, qs, g, ks, vec, inw, out_weight, sw, sb, skip, waits
        )
        grad, norm1, goutb, ginb, gsw, gsb, gskip, dk, p, dy, a, z, du, nown = made
        joint = (p, swap(p, "zh"), x0)
        small[l] = (norm1, gdnb, goutb, gupb, ginb, gsw, gsb, gskip, dk)
        pack = None
        if l == 0:
            norms[0] = jnp.zeros_like(nown)
            gfout, gnet = run_filter_backward(at, inner, fout, sines, cosines, [s[-1] for s in small])
            pack = run_pack_small(at, gnet, gfout, nown, [m for l in range(layers) for m in (norms[l], *small[l][:-1])])
        mixer_halves = run_mixer_weights(at, a, du, z, dy, pack)
        if l == 0:
            begin(mixer_halves)
        else:
            begin(halves, mixer_halves)
        waits = advance([p])
        if l == layers - 1:
            result = run_finish_result(at, saved[l][4], p2, swap(p2, "zh"), vec, l)
            waits.append(result)

    grad = run_finish_grad(at, grad, *joint, vec, 0, waits)
    for _ in range(4):
        advance([])
    later, ff, mixer = (entry[1][0] for entry in sums)
    later = gather_plane(later)
    ff_out = run_place_ff(1, layers, at, later, None)
    mixer_out = run_place_mixer(1, layers, at, later, None, D)
    ff_out = run_place_ff(0, layers, at, gather_near(ff), ff_out)
    *mixer_out, pack = run_place_mixer(0, layers, at, gather_near(mixer), mixer_out, 0)

    net = pack[:SHARED]
    net = net + swap(net, "zh")
    pack = pack[SHARED:].reshape(layers, -1, C)
    first_norm = jnp.where(low, net[NET : NET + 4 : 2], net[NET + 1 : NET + 4 : 2])
    norm_rows = jnp.stack([jnp.concatenate([first_norm, pack[0, 2:4]]), pack[1, :4]])

    def apart(a):
        return jnp.stack([a[..., :NET], a[..., NET:]])

    return (
        result,
        grad,
        norm_rows[:, 0:4:2],
        norm_rows[:, 1:4:2],
        mixer_out[0].transpose(0, 2, 1, 3),
        pack[:, 10:13],
        pack[:, 13:22].reshape(short_weight.shape),
        pack[:, 22:25],
        apart(net[:EMB, 256:]),
        jnp.stack([apart(net[:NET, :128]), apart(net[:NET, 128:256])], 1),
        apart(net[40:43, 256:]),
        pack[:, 26:90],
        pack[:, 25],
        mixer_out[1],
        pack[:, 5],
        ff_out[0],
        pack[:, 6:10].reshape(layers, FH),
        ff_out[1],
        pack[:, 4],
    )


def solution(mesh):
    names = ("zl", "y", "x", "c", "zh")
    fine = Mesh(mesh.devices.reshape(2, 4, 4, 2, 2), names)
    dp = ("zl", "y", "x", "c")
    rows = P(dp, "zh")
    third, fourth = P(None, None, "zh"), P(None, None, None, "zh")
    second, middle = P(None, "zh"), P(None, "zh", None)
    placed = (
        rows, P(dp), third, third, fourth, third, fourth, third, P(), P(), P(), third, second, middle, second, third,
        second, middle, second, rows,
    )
    return jax.shard_map(
        shards,
        mesh=fine,
        in_specs=placed,
        out_specs=(
            rows, rows, third, third, fourth, third, fourth, third, P(), P(), P(), third, second, middle, second, third,
            second, middle, second,
        ),
        check_vma=False,
    )
```

```python
import functools
import math

import jax
import jax.numpy as jnp
import ml_dtypes
import numpy as np
from jax import lax
from jax.experimental import pallas as pl
from jax.experimental.pallas import tpu as pltpu
from jax.sharding import Mesh
from jax.sharding import PartitionSpec as P

D = 768
T = 512
H = T // 2
C = 384
FH = 1536
NET = 64
EMB = 33
BANDS = 16
PIECE = 96
EPSILON = 1e-05
HIGH = lax.Precision.HIGHEST
F32 = jnp.float32
BF = jnp.bfloat16
VMEM_LIMIT = 56 * 2**20

ORDER = np.concatenate([np.arange(0, T, 2), np.arange(1, T, 2)])


def split_table(t):
    hi = t.astype(ml_dtypes.bfloat16)
    lo = (t - hi.astype(np.float64)).astype(ml_dtypes.bfloat16)
    return hi, lo


def wave_tables():
    n = np.arange(H)
    even = 2 * math.pi * (np.outer(n, 2 * n) % (2 * T)) / (2 * T)
    odd = 2 * math.pi * (np.outer(n, 2 * n + 1) % (2 * T)) / (2 * T)
    alt = np.where(n % 2 == 0, 1.0, -1.0)
    out = []
    for ang in (even, odd):
        co, si = np.cos(ang), np.sin(ang)
        si[0] = alt
        hi, lo = split_table(np.concatenate([co, si], 0))
        out.append(np.concatenate([hi, lo, hi], 1))
        hi, lo = split_table(np.concatenate([co.T, si.T], 1))
        out.append(np.concatenate([hi, lo, hi], 1))
    fe, ie, fo, io = out
    return fe, fo, ie, io


FE, FO, IE, IO = wave_tables()


def slot_features():
    slots = ORDER.astype(np.float64)
    freqs = 0.0001 + (BANDS - 1 - 0.0001) * np.arange(BANDS) / (BANDS - 1)
    angle = 2 * math.pi * slots[:, None] * freqs[None, :] / T
    times = (slots / (T - 1))[:, None]
    feats = np.concatenate([times, np.cos(angle), -np.sin(angle), np.zeros((T, 128 - EMB))], 1)
    return feats.astype(np.float32), np.broadcast_to(times, (T, 128)).astype(np.float32)


FEATS, TIMES = slot_features()


def dot(a, b):
    return lax.dot_general(a, b, (((1,), (0,)), ((), ())), preferred_element_type=F32)


def dot_nt(a, b):
    return lax.dot_general(a, b, (((1,), (1,)), ((), ())), preferred_element_type=F32)


def dot_tn(a, b):
    return lax.dot_general(a, b, (((0,), (0,)), ((), ())), preferred_element_type=F32)


def normalize(x):
    mean = jnp.mean(x, -1, keepdims=True)
    scale = lax.rsqrt(jnp.mean(x * x, -1, keepdims=True) - mean * mean + EPSILON)
    return (x - mean) * scale, scale


def norm_pull(dn, x, gain):
    xhat, scale = normalize(x)
    ds = dn * gain
    first = jnp.mean(ds, -1, keepdims=True)
    second = jnp.mean(ds * xhat, -1, keepdims=True)
    return scale * (ds - first - xhat * second), dn * xhat


def row_mask(start, rows, length):
    r = start + lax.broadcasted_iota(jnp.int32, (rows, 1), 0)
    slot = jnp.where(r < H, 2 * r, 2 * (r - H) + 1)
    return (slot < length).astype(F32)


def down_one(x):
    r = lax.broadcasted_iota(jnp.int32, x.shape, 0)
    return jnp.where(r == 0, 0.0, pltpu.roll(x, 1, 0))


def up_one(x):
    r = lax.broadcasted_iota(jnp.int32, x.shape, 0)
    return jnp.where(r == x.shape[0] - 1, 0.0, pltpu.roll(x, x.shape[0] - 1, 0))


def put_split(ref, value, rows, lanes):
    hi = value.astype(BF)
    lo = (value - hi.astype(F32)).astype(BF)
    step = ref.shape[0] // 3
    ref[pl.ds(rows, value.shape[0]), lanes] = hi
    ref[pl.ds(step + rows, value.shape[0]), lanes] = hi
    ref[pl.ds(2 * step + rows, value.shape[0]), lanes] = lo


def top_row(shape):
    return lax.broadcasted_iota(jnp.int32, shape, 0) == 0


def butterfly(even, odd, lanes):
    ce, se = even[pl.ds(0, H), lanes], even[pl.ds(H, H), lanes]
    co, so = odd[pl.ds(0, H), lanes], odd[pl.ds(H, H), lanes]
    top = top_row(ce.shape)
    return ce + co, ce - co, jnp.where(top, se, se + so), jnp.where(top, so, se - so)


def spectrum_product(a, k, conj):
    a1, a2, b1, b2 = a
    k1, k2, l1, l2 = k
    top = top_row(a1.shape)
    aa, bb, cc, dd = a1 * k1, b1 * l1, a2 * k2, b2 * l2
    if conj:
        y1 = jnp.where(top, aa, aa + bb)
        y2 = jnp.where(top, cc, cc + dd)
        m1 = jnp.where(top, bb + dd, b1 * k1 - a1 * l1)
        m2 = jnp.where(top, b2 * l1 - b1 * l2, b2 * k2 - a2 * l2)
    else:
        y1 = jnp.where(top, aa, aa - bb)
        y2 = jnp.where(top, cc, cc - dd)
        m1 = jnp.where(top, bb - dd, a1 * l1 + b1 * k1)
        m2 = jnp.where(top, b1 * l2 + b2 * l1, a2 * l2 + b2 * k2)
    return y1, y2, m1, m2


def put_inverse(rhs_e, rhs_o, y, lanes):
    y1, y2, m1, m2 = y
    top = top_row(y1.shape)
    unit = 1.0 / T
    w = jnp.where(top, 0.5 * unit, unit)
    put_split(rhs_e, (y1 + y2) * w, 0, lanes)
    put_split(rhs_o, (y1 - y2) * w, 0, lanes)
    put_split(rhs_e, jnp.where(top, m1, m1 + m2) * unit, H, lanes)
    put_split(rhs_o, jnp.where(top, m2, m1 - m2) * unit, H, lanes)


def lanes_of(block):
    return pl.ds(block * 128, 128)


def short_conv(u_ref, sw_ref, sb_ref, block):
    out = []
    for s in range(3):
        at = lanes_of(s * (C // 128) + block)
        ue, uo = u_ref[pl.ds(0, H), at], u_ref[pl.ds(H, H), at]
        t0, t1, t2 = (sw_ref[j : j + 1, at] for j in range(3))
        bias = sb_ref[0:1, at]
        uo_d = down_one(uo)
        we = t2 * ue + t1 * uo_d + t0 * down_one(ue) + bias
        wo = t2 * uo + t1 * ue + t0 * uo_d + bias
        out.append((we, wo))
    return out


def hdot(a, b, dims=(1, 0)):
    return lax.dot_general(
        a, b, (((dims[0],), (dims[1],)), ((), ())), precision=HIGH, preferred_element_type=F32
    )


def decay_of(half_at, times_ref):
    slow = math.log(0.01) / 1.5
    fast = math.log(0.01) / 0.3
    channel = (half_at * C + lax.broadcasted_iota(jnp.int32, (1, C), 1)).astype(F32)
    rates = jnp.abs(slow + (fast - slow) * channel / (D - 1))
    return jnp.exp(-times_ref[:, 0:1] * rates) + 0.05


def sin_cos(x):
    k = jnp.floor(x * (2 / math.pi) + 0.5)
    r = ((x - k * 1.5703125) - k * 4.837512969970703125e-4) - k * 7.54978995489188e-8
    rr = r * r
    sine = r + r * rr * (-1.6666654611e-1 + rr * (8.3321608736e-3 + rr * -1.9515295891e-4))
    cosine = 1.0 - 0.5 * rr + rr * rr * (
        4.166664568298827e-2 + rr * (-1.388731625493765e-3 + rr * 2.443315711809948e-5)
    )
    quarter = k - 4.0 * jnp.floor(k * 0.25)
    odd = (quarter == 1.0) | (quarter == 3.0)
    s = jnp.where(odd, cosine, sine)
    c = jnp.where(odd, sine, cosine)
    return jnp.where(quarter >= 2.0, -s, s), jnp.where((quarter == 1.0) | (quarter == 2.0), -c, c)


def filter_forward(
    at_ref, feats_ref, times_ref, first_ref, inner_ref, bias_ref, out_ref, fe_ref, fo_ref,
    ks_ref, sin_ref, cos_ref, both_ref, wide_ref, first_s, bias_s, k_s, rhs_e, rhs_o, se, so,
):
    for ref in (both_ref, wide_ref, first_s, bias_s):
        ref[...] = jnp.zeros_like(ref)
    for l in range(2):
        at = pl.ds(l * NET, NET)
        first_s[0:EMB, at] = first_ref[l]
        bias_s[0:3, at] = bias_ref[l]
        wide_ref[l, at, :] = out_ref[l]
        for i in range(2):
            both_ref[i, at, at] = inner_ref[l, i]
    low = feats_ref[...]
    for i in range(3):
        weight = first_s[...] if i == 0 else both_ref[i - 1]
        low, cosine = sin_cos(hdot(low, weight) + bias_s[i : i + 1, :])
        sin_ref[i] = low
        cos_ref[i] = cosine
    decay = decay_of(at_ref[0], times_ref)
    for l in range(2):
        k_s[...] = hdot(sin_ref[2], wide_ref[l]) * decay
        for b in range(C // 128):
            at = lanes_of(b)
            put_split(rhs_e, k_s[pl.ds(0, H), at], 0, at)
            put_split(rhs_o, k_s[pl.ds(H, H), at], 0, at)
        se[...] = dot(fe_ref[...], rhs_e[...])
        so[...] = dot(fo_ref[...], rhs_o[...])
        for b in range(C // 128):
            at = lanes_of(b)
            for i, v in enumerate(butterfly(se, so, at)):
                ks_ref[l, i, :, at] = v


def filter_backward(at_ref, feats_ref, times_ref, inner_ref, out_ref, sin_ref, cos_ref, dk0_ref, dk1_ref, gout_ref, gnet_ref):
    decay = decay_of(at_ref[0], times_ref)
    ds = jnp.zeros((T, 128), F32)
    for l, dk_ref in enumerate((dk0_ref, dk1_ref)):
        dk = dk_ref[...] * decay
        gout_ref[l] = hdot(sin_ref[2], dk, (0, 0))[l * NET : (l + 1) * NET]
        ds += hdot(dk, out_ref[l], (1, 1))
    lane = lax.broadcasted_iota(jnp.int32, (NET, 128), 1)
    gnet_ref[...] = jnp.zeros_like(gnet_ref)
    for i in (2, 1, 0):
        da = ds * cos_ref[i]
        gnet_ref[40 + i : 41 + i, pl.ds(256, 128)] = jnp.sum(da, 0, keepdims=True)
        if i > 0:
            block = hdot(sin_ref[i - 1], da, (0, 0))
            gnet_ref[:, pl.ds((i - 1) * 128, 128)] = jnp.where(lane < NET, block[:NET], block[NET:])
            ds = hdot(da, inner_ref[i - 1], (1, 1))
        else:
            gnet_ref[0:40, pl.ds(256, 128)] = hdot(feats_ref[...], da, (0, 0))[0:40]


def arrange(at_ref, own_ref, other_ref, out_ref, tmp):
    for half, first in ((0, own_ref), (1, other_ref)):
        for b in range(C // 128):
            tmp[b] = first[:, lanes_of(b)].astype(F32)

        def put(first_lane):
            for b in range(C // 128):
                to = pl.ds(first_lane + b * 128, 128)
                out_ref[pl.ds(0, H), to] = tmp[b, pl.ds(0, H, stride=2), :]
                out_ref[pl.ds(H, H), to] = tmp[b, pl.ds(1, H, stride=2), :]

        pl.when(at_ref[0] == half)(functools.partial(put, 0))
        pl.when(at_ref[0] != half)(functools.partial(put, C))


def by_slot(at_ref, src_ref, out_ref, tmp):
    def put(first_lane):
        for b in range(C // 128):
            lanes = pl.ds(first_lane + b * 128, 128)
            tmp[b, pl.ds(0, H, stride=2), :] = src_ref[pl.ds(0, H), lanes]
            tmp[b, pl.ds(1, H, stride=2), :] = src_ref[pl.ds(H, H), lanes]

    pl.when(at_ref[0] == 0)(functools.partial(put, 0))
    pl.when(at_ref[0] != 0)(functools.partial(put, C))
    for b in range(C // 128):
        out_ref[:, lanes_of(b)] = tmp[b].astype(out_ref.dtype)


def finish_result(at_ref, x_ref, own_ref, other_ref, vec_ref, out_ref, y_s, tmp):
    def put(first_lane):
        lanes = pl.ds(first_lane, C)

        def body(start, c):
            rows = pl.ds(start, RB)
            y = own_ref[rows, :].astype(F32) + other_ref[rows, :].astype(F32) + vec_ref[0, 5:6, lanes]
            y_s[rows, lanes] = x_ref[rows, lanes] + row_mask(start, RB, at_ref[1]) * y
            return c

        row_loop(body)

    pl.when(at_ref[0] == 0)(functools.partial(put, 0))
    pl.when(at_ref[0] != 0)(functools.partial(put, C))
    by_slot(at_ref, y_s, out_ref, tmp)


def finish_grad(at_ref, g_ref, own_ref, other_ref, x_ref, vec_ref, out_ref, x_s, tmp):
    def body(start, c):
        at = pl.ds(start, RB)
        dn = own_ref[at, :].astype(F32) + other_ref[at, :].astype(F32)
        x_s[at, :] = g_ref[at, :] + norm_pull(dn, x_ref[at, :], vec_ref[0, 0:1, :])[0]
        return c

    row_loop(body)
    by_slot(at_ref, x_s, out_ref, tmp)


def add_branch(x_ref, own_ref, other_ref, vec_ref, row, length, start, rows):
    at = pl.ds(start, rows)
    y = own_ref[at, :].astype(F32) + other_ref[at, :].astype(F32) + vec_ref[row : row + 1, :]
    return x_ref[at, :] + row_mask(start, rows, length) * y


RB = 128


def row_loop(body, init=0):
    def step(i, c):
        return body(pl.multiple_of(i * RB, RB), c)

    return lax.fori_loop(0, T // RB, step, init)


def mixer_forward(joined, *refs):
    at_ref, x_ref = refs[:2]
    refs = refs[2:]
    if joined:
        own_ref, other_ref, prev_ref = refs[:3]
        refs = refs[3:]
    (vec_ref, inw_ref, inb_ref, sw_ref, sb_ref, ks_ref, skip_ref, fe_ref, fo_ref, ie_ref, io_ref, outw_ref) = refs[:12]
    refs = refs[12:]
    if joined:
        xo_ref = refs[0]
        refs = refs[1:]
    u_ref, qs_ref, g_ref, p_ref, a_s, w0_s, q_s, rhs_e, rhs_o, se, so, rhs2_e, rhs2_o, z_s = refs

    def first(start, c):
        at = pl.ds(start, RB)
        if joined:
            x = add_branch(x_ref, own_ref, other_ref, prev_ref.at[0], 5, at_ref[1], start, RB)
            xo_ref[at, :] = x
        else:
            x = x_ref[at, :]
        xhat, _ = normalize(x)
        a_s[at, :] = (xhat * vec_ref[0, 0:1, :] + vec_ref[0, 1:2, :]).astype(BF)
        return c

    row_loop(first)
    for s in range(3):
        at = pl.ds(s * C, C)
        u_ref[:, at] = dot(a_s[...], inw_ref[0, s]) + inb_ref[0, 0:1, at]
    for b in range(C // 128):
        at = lanes_of(b)
        (w0e, w0o), (w1e, w1o), (w2e, w2o) = short_conv(u_ref, sw_ref.at[0], sb_ref.at[0], b)
        w0_s[pl.ds(0, H), at] = w0e
        w0_s[pl.ds(H, H), at] = w0o
        qe, qo = w2e * w1e, w2o * w1o
        q_s[pl.ds(0, H), at] = qe
        q_s[pl.ds(H, H), at] = qo
        put_split(rhs_e, qe, 0, at)
        put_split(rhs_o, qo, 0, at)
    se[...] = dot(fe_ref[...], rhs_e[...])
    so[...] = dot(fo_ref[...], rhs_o[...])
    for b in range(C // 128):
        at = lanes_of(b)
        spec = butterfly(se, so, at)
        for i, v in enumerate(spec):
            qs_ref[i, :, at] = v
        y = spectrum_product(spec, [ks_ref[0, i, :, at] for i in range(4)], False)
        put_inverse(rhs2_e, rhs2_o, y, at)
    se[pl.ds(0, H), :] = dot(ie_ref[...], rhs2_e[...])
    se[pl.ds(H, H), :] = dot(io_ref[...], rhs2_o[...])

    def last(start, c):
        at = pl.ds(start, RB)
        g = se[at, :] + skip_ref[0, 0:1, :] * q_s[at, :]
        g_ref[at, :] = g
        z_s[at, :] = (g * w0_s[at, :]).astype(BF)
        return c

    row_loop(last)
    p_ref[...] = dot(z_s[...], outw_ref[0]).astype(BF)


def gelu_parts(h):
    c0 = math.sqrt(2 / math.pi)
    hh = h * h
    t = jnp.tanh(c0 * (h + 0.044715 * (hh * h)))
    half = 0.5 * (1.0 + t)
    return half, t, hh, c0


def collect(j, acc, part):
    @pl.when(j == 0)
    def _():
        acc[...] = part

    @pl.when(j > 0)
    def _():
        acc[...] += part


def ff_forward(last, at_ref, x_ref, own_ref, other_ref, vec_ref, up_ref, upb_ref, dn_ref, xo_ref, h_ref, *refs):
    *p_refs, b_s, acc = refs
    j = pl.program_id(0)

    @pl.when(j == 0)
    def _():
        def first(start, c):
            at = pl.ds(start, RB)
            x = add_branch(x_ref, own_ref, other_ref, vec_ref.at[0], 4, at_ref[1], start, RB)
            xo_ref[at, :] = x
            xhat, _ = normalize(x)
            b_s[at, :] = (xhat * vec_ref[0, 2:3, :] + vec_ref[0, 3:4, :]).astype(BF)
            return c

        row_loop(first)

    h = dot(b_s[...], up_ref[0]) + upb_ref[0]
    h_ref[...] = h
    half, _, _, _ = gelu_parts(h)
    collect(j, acc, dot((h * half).astype(BF), dn_ref[0]))

    @pl.when(j == pl.num_programs(0) - 1)
    def _():
        if not last:
            p_refs[0][...] = acc[...].astype(BF)
        else:
            low, high = acc[:, :C].astype(BF), acc[:, C:].astype(BF)
            own = at_ref[0] == 0
            p_refs[0][...] = jnp.where(own, low, high)
            p_refs[1][...] = jnp.where(own, high, low)


def put_by_core(at_ref, keep_ref, give_ref, at, low, high):
    @pl.when(at_ref[4] == 0)
    def _():
        keep_ref[at] = low
        give_ref[at] = high

    @pl.when(at_ref[4] != 0)
    def _():
        keep_ref[at] = high
        give_ref[at] = low


def ff_backward(joined, *refs):
    at_ref, g_ref = refs[:2]
    refs = refs[2:]
    if joined:
        own_ref, other_ref, xn_ref, nvec_ref = refs[:4]
        refs = refs[4:]
    x_ref, h_ref, vec_ref, up_ref, dn_ref = refs[:5]
    refs = refs[5:]
    if joined:
        go_ref, ngrad_ref = refs[:2]
        refs = refs[2:]
    keep_ref, give_ref, gupb_ref, gdnb_ref, p_ref, dm_s, acc = refs
    j = pl.program_id(0)

    @pl.when(j == 0)
    def _():
        def first(start, c):
            at = pl.ds(start, RB)
            g = g_ref[at, :]
            sums, s1, s2 = c
            if joined:
                dn = own_ref[at, :].astype(F32) + other_ref[at, :].astype(F32)
                dx, dg = norm_pull(dn, xn_ref[at, :], nvec_ref[0, 0:1, :])
                g = g + dx
                go_ref[at, :] = g
                s1 = s1 + jnp.sum(dg, 0, keepdims=True)
                s2 = s2 + jnp.sum(dn, 0, keepdims=True)
            dm = (row_mask(start, RB, at_ref[1]) * g).astype(BF)
            dm_s[at, :] = dm
            xhat, _ = normalize(x_ref[at, :])
            b = (xhat * vec_ref[0, 2:3, :] + vec_ref[0, 3:4, :]).astype(BF)
            put_by_core(at_ref, keep_ref, give_ref, (at, pl.ds(0, D)), dm, b)
            return sums + jnp.sum(dm.astype(F32), 0, keepdims=True), s1, s2

        zero = jnp.zeros((1, D), F32)
        sums, s1, s2 = row_loop(first, (zero, zero, zero))
        gdnb_ref[...] = sums
        if joined:
            ngrad_ref[0:1, :] = s1
            ngrad_ref[1:2, :] = s2

    h = h_ref[...]
    half, t, hh, c0 = gelu_parts(h)
    e = (h * half).astype(BF)
    slope = half + 0.5 * c0 * h * (1.0 - t * t) * (1.0 + 3 * 0.044715 * hh)
    dh = (dot_nt(dm_s[...], dn_ref[0]) * slope).astype(BF)
    put_by_core(at_ref, keep_ref, give_ref, (slice(None), pl.ds(pl.multiple_of(D + j * FC, 128), FC)), e, dh)
    gupb_ref[...] = jnp.sum(dh.astype(F32), 0, keepdims=True)
    collect(j, acc, dot_nt(dh, up_ref[0]))

    @pl.when(j == pl.num_programs(0) - 1)
    def _():
        p_ref[...] = acc[...].astype(BF)


FIRST, SECOND = 5, 6
WIDE = 3 * D


class Swapped:
    def __init__(self, at_ref):
        self.at_ref = at_ref

    def __getitem__(self, i):
        return self.at_ref[{FIRST: SECOND, SECOND: FIRST}.get(i, i)]


def put_pieces(at_ref, ref, value):
    for n in range(4):
        ref[lax.rem(n - at_ref[SECOND] + 4, 4), pl.ds(0, PIECE)] = value[n * PIECE : (n + 1) * PIECE]


def ff_weights(at_ref, mine_ref, got_ref, *outs):
    for k, out_ref in enumerate(outs):
        block = lax.rem(at_ref[FIRST] + k, 4)
        lanes = pl.ds(pl.multiple_of(D + block * 4 * PIECE, 128), 4 * PIECE)
        total = sum(dot_tn(ref[:, lanes], ref[:, pl.ds(0, D)]) for ref in (mine_ref, got_ref))
        put_pieces(at_ref, out_ref, total.astype(BF))


def mixer_backward(
    last, at_ref, g_in_ref, own_ref, other_ref, x1_ref, x0_ref, u_ref, qs_ref, g_ref, ks_ref, vec_ref, inw_ref, outw_ref,
    sw_ref, sb_ref, skip_ref, fe_ref, fo_ref, ie_ref, io_ref,
    go_ref, ngrad_ref, goutb_ref, ginb_ref, gsw_ref, gsb_ref, gskip_ref, dk_ref, p_ref, keep_ref, give_ref,
    nown_ref, dy_ref, a_ref, z_ref, du_ref, dz_s, dg_s, w1_s, w2_s, dw0_s, rhs_e, rhs_o, se, so, rhs2_e, rhs2_o, inv_s,
):
    def first(start, c):
        at = pl.ds(start, RB)
        sums, s1, s2 = c
        dn = own_ref[at, :].astype(F32) + other_ref[at, :].astype(F32)
        dx, dg = norm_pull(dn, x1_ref[at, :], vec_ref[0, 2:3, :])
        g = g_in_ref[at, :] + dx
        go_ref[at, :] = g
        dy = (row_mask(start, RB, at_ref[1]) * g).astype(BF)
        dy_ref[at, :] = dy
        xhat, _ = normalize(x0_ref[at, :])
        a_ref[at, :] = (xhat * vec_ref[0, 0:1, :] + vec_ref[0, 1:2, :]).astype(BF)
        return (
            sums + jnp.sum(dy.astype(F32), 0, keepdims=True),
            s1 + jnp.sum(dg, 0, keepdims=True),
            s2 + jnp.sum(dn, 0, keepdims=True),
        )

    zero = jnp.zeros((1, D), F32)
    sums, s1, s2 = row_loop(first, (zero, zero, zero))
    goutb_ref[...] = sums
    ngrad_ref[0:1, :] = s1
    ngrad_ref[1:2, :] = s2
    dz_s[...] = dot_nt(dy_ref[...], outw_ref[0])
    halves = (pl.ds(0, H), pl.ds(H, H))
    for b in range(C // 128):
        at = lanes_of(b)
        w0, w1, w2 = short_conv(u_ref, sw_ref.at[0], sb_ref.at[0], b)
        dskip = 0.0
        for i, (rows, rhs) in enumerate(zip(halves, (rhs_e, rhs_o))):
            dz, g = dz_s[rows, at], g_ref[rows, at]
            z_ref[rows, at] = (g * w0[i]).astype(BF)
            dw0_s[rows, at] = dz * g
            dg = dz * w0[i]
            dg_s[rows, at] = dg
            dskip = dskip + jnp.sum(dg * (w2[i] * w1[i]), 0, keepdims=True)
            w1_s[rows, at] = w1[i]
            w2_s[rows, at] = w2[i]
            put_split(rhs, dg, 0, at)
        gskip_ref[0:1, at] = dskip
    se[...] = dot(fe_ref[...], rhs_e[...])
    so[...] = dot(fo_ref[...], rhs_o[...])
    for b in range(C // 128):
        at = lanes_of(b)
        spec = butterfly(se, so, at)
        put_inverse(rhs2_e, rhs2_o, spectrum_product(spec, [ks_ref[0, i, :, at] for i in range(4)], True), at)
        put_inverse(
            rhs2_e, rhs2_o, spectrum_product(spec, [qs_ref[i, :, at] for i in range(4)], True), pl.ds(C + b * 128, 128)
        )
    inv_s[pl.ds(0, H), :] = dot(ie_ref[...], rhs2_e[...])
    inv_s[pl.ds(H, H), :] = dot(io_ref[...], rhs2_o[...])
    dk_ref[...] = inv_s[:, pl.ds(C, C)]
    for b in range(C // 128):
        at = lanes_of(b)
        dw = [[dw0_s[rows, at] for rows in halves], [], []]
        for rows in halves:
            dq = inv_s[rows, at] + skip_ref[0, 0:1, at] * dg_s[rows, at]
            dw[1].append(dq * w2_s[rows, at])
            dw[2].append(dq * w1_s[rows, at])
        for s in range(3):
            to = lanes_of(s * (C // 128) + b)
            ue, uo = u_ref[halves[0], to], u_ref[halves[1], to]
            t0, t1, t2 = (sw_ref[0, j : j + 1, to] for j in range(3))
            de, do = dw[s]
            de_u, do_u = up_one(de), up_one(do)
            due = (t2 * de + t1 * do + t0 * de_u).astype(BF)
            duo = (t2 * do + t1 * de_u + t0 * do_u).astype(BF)
            du_ref[halves[0], to] = due
            du_ref[halves[1], to] = duo
            uo_d = down_one(uo)
            gsw_ref[0:1, to] = jnp.sum(de * down_one(ue) + do * uo_d, 0, keepdims=True)
            gsw_ref[1:2, to] = jnp.sum(de * uo_d + do * ue, 0, keepdims=True)
            gsw_ref[2:3, to] = jnp.sum(de * ue + do * uo, 0, keepdims=True)
            gsb_ref[0:1, to] = jnp.sum(de + do, 0, keepdims=True)
            ginb_ref[0:1, to] = jnp.sum(due.astype(F32) + duo.astype(F32), 0, keepdims=True)
    part = dot_nt(du_ref[:, pl.ds(0, C)], inw_ref[0, 0])
    for s in range(1, 3):
        part += dot_nt(du_ref[:, pl.ds(s * C, C)], inw_ref[0, s])
    p_ref[...] = part.astype(BF)

    def spread(start, c):
        rows = pl.ds(start, RB)
        a, dy, z = a_ref[rows, :], dy_ref[rows, :], z_ref[rows, :]
        du = [du_ref[rows, pl.ds(s * C, C)] for s in range(3)]
        lane = 0
        for low, high in ((a, a), (du[0], du[2]), (a, dy), (du[1], z)):
            put_by_core(at_ref, keep_ref, give_ref, (rows, pl.ds(lane, low.shape[1])), low, high)
            lane += low.shape[1]
        return c

    row_loop(spread)
    nown_ref[...] = jnp.zeros_like(nown_ref)
    if last:

        def terms(start, c):
            at = pl.ds(start, RB)
            dn = p_ref[at, :].astype(F32)
            xhat, _ = normalize(x0_ref[at, :])
            return c[0] + jnp.sum(dn * xhat, 0, keepdims=True), c[1] + jnp.sum(dn, 0, keepdims=True)

        s1, s2 = row_loop(terms, (zero, zero))
        nown_ref[0:1, :] = s1
        nown_ref[1:2, :] = s2


def put_split_rows(value):
    hi = value.astype(BF).astype(F32)
    return jnp.concatenate([hi, value - hi], 0).astype(BF)


def mixer_weights(packed, at_ref, mine_ref, got_ref, *refs):
    if packed:
        pack_refs, refs = refs[:2], refs[2:]
    for k, out_ref in enumerate(refs):
        block = lax.rem(at_ref[FIRST] + k, 4)
        left = pl.multiple_of(jnp.where(block < 2, block, block + 1) * C, 128)
        right = pl.multiple_of(jnp.where(block < 2, D, 2 * D + C), 128)
        total = sum(dot_tn(ref[:, pl.ds(left, C)], ref[:, pl.ds(right, C)]) for ref in (mine_ref, got_ref))
        put_pieces(at_ref, out_ref, total.astype(BF))
        if packed:
            for n in range(4):
                rows = pl.ds(pl.multiple_of(block * 32 + n * 8, 8), 8)
                value = pack_refs[0][rows, :] + pack_refs[1][rows, :]
                out_ref[lax.rem(n - at_ref[SECOND] + 4, 4), pl.ds(PIECE, 16)] = put_split_rows(value)


def add_parts(count, sides, *refs):
    ins, outs = refs[:count], refs[count:]
    lane = 0
    for side in range(sides):
        some = ins[side * count // sides : (side + 1) * count // sides]
        lanes = slice(lane, lane + some[0].shape[-1])
        lane = lanes.stop
        for i, out in enumerate(outs):
            total = functools.reduce(jnp.add, [(r[i] if len(outs) > 1 else r[...]).astype(F32) for r in some])
            rows = (slice(None),) * (total.ndim - 2)
            out[rows + (slice(0, PIECE), lanes)] = total[rows + (slice(0, PIECE),)].astype(BF)
            if total.shape[-2] > PIECE:
                for n in range(total.shape[0] if total.ndim > 2 else 1):
                    value = total[n] if total.ndim > 2 else total
                    value = value[PIECE : PIECE + 8] + value[PIECE + 8 : PIECE + 16]
                    to = (n, slice(PIECE, PIECE + 16)) if total.ndim > 2 else slice(PIECE, PIECE + 16)
                    out[to] = put_split_rows(value)


def gather_block(at_ref, ref, block, tmp, first_lane, pack_ref=None, first=0):
    width = tmp.shape[-1]
    lanes = slice(first_lane, first_lane + width)
    for m in range(4):
        if len(ref.shape) == 5:
            by_x = (at_ref[4] == 0) != isinstance(at_ref, Swapped)
            at = 0, jnp.where(by_x, m, block), jnp.where(by_x, block, m)
        else:
            at = lax.rem(at_ref[FIRST] - block + 4, 4), lax.rem(at_ref[SECOND] - m + 4, 4)
        tmp[pl.ds(m * PIECE, PIECE), :] = ref[at + (slice(0, PIECE), lanes)].astype(F32)
        if pack_ref is not None:
            extra = ref[at + (slice(PIECE, PIECE + 16),)].astype(F32)
            pack_ref[pl.ds(pl.multiple_of(first + m * 8, 8), 8), :] = extra[:8] + extra[8:]


def gather_half(at_ref, half, refs, *args):
    own = at_ref[4] == half
    pl.when(own)(lambda: gather_block(at_ref, refs[0], *args))
    pl.when(jnp.logical_not(own))(lambda: gather_block(Swapped(at_ref), refs[1], *args))


def place_ff(at_ref, *refs):
    ins, (gup_ref, gdn_ref, tmp) = refs[:2], refs[-3:]
    block = pl.program_id(0)
    gather_half(at_ref, 0, ins, block, tmp, 0)
    gdn_ref[0] = tmp[...]
    gather_half(at_ref, 1, ins, block, tmp, 0)
    gup_ref[0] = tmp[...].T


def place_mixer(packed, lane, at_ref, *refs):
    ins, outs, tmp = refs[:2], refs[2:-1], refs[-1]
    gin_ref, gout_ref = outs[:2]
    step = pl.program_id(0)
    args = ins, lax.rem(step, 4), tmp, lane, outs[2] if packed else None, step * 32
    gather_half(at_ref, step // 4, *args)

    @pl.when(step < 6)
    def _():
        gin_ref[0, 0] = tmp[...]

    @pl.when(step >= 6)
    def _():
        gout_ref[0] = tmp[...].T


PACK = 256
SHARED = 72
LAYER_ROWS = 92


def pack_small(at_ref, gnet_ref, gout_ref, nown_ref, *refs):
    keep_ref, give_ref, out_ref = refs[-3:]
    out_ref[...] = jnp.zeros_like(out_ref)
    out_ref[0:NET, :] = gnet_ref[...]
    for j in range(2):
        for i in range(2):
            row = NET + 2 * j + i
            out_ref[row : row + 1, :] = nown_ref[j : j + 1, i * C : (i + 1) * C]
    for l in range(2):
        n0, n1, gdnb, goutb, gupb, ginb, gsw, gsb, gskip = refs[9 * l : 9 * l + 9]
        row = SHARED + LAYER_ROWS * l

        def put(value):
            nonlocal row
            out_ref[row : row + value.shape[0], :] = value
            row += value.shape[0]

        for ref in (n0, n1, gdnb, goutb):
            put(jnp.where(at_ref[0] == 0, ref[:, :C], ref[:, C:]))
        for ref in (gupb, ginb, gsw, gsb):
            for j in range(ref.shape[0]):
                for i in range(ref.shape[1] // C):
                    put(ref[j : j + 1, i * C : (i + 1) * C])
        put(gskip[...])
        put(gout_ref[l])
    put_by_core(at_ref, keep_ref, give_ref, slice(None), out_ref[: PACK // 2], out_ref[PACK // 2 :])


def sds(shape, dtype=F32):
    return jax.ShapeDtypeStruct(shape, dtype)


def params(us):
    return dict(
        compiler_params=pltpu.CompilerParams(vmem_limit_bytes=VMEM_LIMIT),
        cost_estimate=pl.CostEstimate(flops=int(us * 1e9), bytes_accessed=10000, transcendentals=0),
    )


SMEM = pl.BlockSpec(memory_space=pltpu.SMEM)
WHOLE = pl.BlockSpec(memory_space=pltpu.VMEM)
ANY = pl.BlockSpec(memory_space=pl.ANY)
SLOTS = pltpu.VMEM((C // 128, T, 128), F32)


def layer_of(x, l):
    rest = x.ndim - 1
    return pl.BlockSpec((1,) + x.shape[1:], lambda *_: (l,) + (0,) * rest, pipeline_mode=pl.Buffered(1))


def fixed(shape):
    return pl.BlockSpec(shape, lambda *_: (0,) * len(shape))


def spectrum_scratch():
    return [pltpu.VMEM((3 * H, C), BF)] * 2 + [pltpu.VMEM((T, C), F32)] * 2


def run_filter_forward(at, first, inner, bias, out):
    layers = out.shape[0]
    return pl.pallas_call(
        filter_forward,
        in_specs=[SMEM] + [WHOLE] * 8,
        out_specs=[WHOLE] * 5,
        out_shape=[
            sds((layers, 4, H, C)), sds((3, T, 128)), sds((3, T, 128)), sds((2, 128, 128)), sds((layers, 128, C)),
        ],
        scratch_shapes=[pltpu.VMEM((128, 128), F32), pltpu.VMEM((8, 128), F32), pltpu.VMEM((T, C), F32)]
        + spectrum_scratch(),
        name="filter_forward",
        **params(12),
    )(at, FEATS, TIMES, first, inner, bias, out, FE, FO)


def run_filter_backward(at, inner, out, sines, cosines, dks):
    return pl.pallas_call(
        filter_backward,
        in_specs=[SMEM] + [WHOLE] * 8,
        out_specs=[WHOLE] * 2,
        out_shape=[sds((2, NET, C)), sds((NET, C))],
        name="filter_backward",
        **params(8),
    )(at, FEATS, TIMES, inner, out, sines, cosines, *dks)


def run_arrange(at, own, other):
    return pl.pallas_call(
        arrange,
        in_specs=[SMEM, WHOLE, WHOLE],
        out_specs=WHOLE,
        out_shape=sds((T, D)),
        scratch_shapes=[SLOTS],
        name="arrange",
        **params(2),
    )(at, own, other)


def run_finish_result(at, x, own, other, vec, l):
    return pl.pallas_call(
        finish_result,
        grid=(1,),
        in_specs=[SMEM, WHOLE, WHOLE, WHOLE, layer_of(vec, l)],
        out_specs=WHOLE,
        out_shape=sds((T, C), BF),
        scratch_shapes=[pltpu.VMEM((T, D), F32), SLOTS],
        name="finish_result",
        **params(3),
    )(at, x, own, other, vec)


def run_finish_grad(at, g, own, other, x, vec, l, after):
    return pl.pallas_call(
        functools.partial(body_without, finish_grad, 6, len(after)),
        grid=(1,),
        in_specs=[SMEM, WHOLE, WHOLE, WHOLE, WHOLE, layer_of(vec, l)] + [ANY] * len(after),
        out_specs=WHOLE,
        out_shape=sds((T, C)),
        scratch_shapes=[pltpu.VMEM((T, D), F32), SLOTS],
        name="finish_grad",
        **params(4),
    )(at, g, own, other, x, vec, *after)


def run_mixer_forward(l, joint, at, x, vec, inw, inb, sw, sb, ks, skip, outw, after):
    joined = joint is not None
    args = [at, x] + (list(joint) + [vec] if joined else [])
    specs = [SMEM] + [WHOLE] * 3 + [layer_of(vec, l - 1)] if joined else [SMEM, WHOLE]
    args += [vec, inw, inb, sw, sb, ks, skip, FE, FO, IE, IO, outw]
    specs += [layer_of(m, l) for m in (vec, inw, inb, sw, sb, ks, skip)] + [WHOLE] * 4 + [layer_of(outw, l)]
    outs = ([sds((T, D))] if joined else []) + [sds((T, 3 * C)), sds((4, H, C)), sds((T, C)), sds((T, D), BF)]
    return pl.pallas_call(
        functools.partial(body_without, functools.partial(mixer_forward, joined), len(args), len(after)),
        grid=(1,),
        in_specs=specs + [ANY] * len(after),
        out_specs=[WHOLE] * len(outs),
        out_shape=outs,
        scratch_shapes=[pltpu.VMEM((T, D), BF), pltpu.VMEM((T, C), F32), pltpu.VMEM((T, C), F32)]
        + spectrum_scratch()
        + [pltpu.VMEM((6 * H, C), BF)] * 2
        + [pltpu.VMEM((T, C), BF)],
        name="mixer_forward",
        **params(11),
    )(*args, *after)


FC = 512


def up_spec(l):
    return pl.BlockSpec((1, D, FC), lambda j: (l, 0, j))


def down_spec(l):
    return pl.BlockSpec((1, FC, D), lambda j: (l, j, 0))


def hidden_spec(rows, width=FC):
    return pl.BlockSpec((rows, width), lambda j: (0, j))


def run_ff_forward(l, last, at, x, own, other, vec, up, upb, dn, after):
    return pl.pallas_call(
        functools.partial(body_without, functools.partial(ff_forward, last), 8, len(after)),
        grid=(FH // FC,),
        in_specs=[
            SMEM, fixed((T, D)), fixed((T, D)), fixed((T, D)), layer_of(vec, l),
            up_spec(l), pl.BlockSpec((1, 1, FC), lambda j: (l, 0, j)), down_spec(l),
        ] + [ANY] * len(after),
        out_specs=[fixed((T, D)), hidden_spec(T)] + ([fixed((T, C))] * 2 if last else [fixed((T, D))]),
        out_shape=[sds((T, D)), sds((T, FH))] + ([sds((T, C), BF)] * 2 if last else [sds((T, D), BF)]),
        scratch_shapes=[pltpu.VMEM((T, D), BF), pltpu.VMEM((T, D), F32)],
        name="ff_forward",
        **params(10),
    )(at, x, own, other, vec, up, upb, dn, *after)


def run_ff_backward(l, at, g, joint, x, h, vec, up, dn, after):
    joined = joint is not None
    args = [at, g] + (list(joint) + [vec] if joined else []) + [x, h, vec, up, dn]
    specs = [SMEM, fixed((T, D))]
    if joined:
        specs += [fixed((T, D))] * 3 + [layer_of(vec, l + 1)]
    specs += [fixed((T, D)), hidden_spec(T), layer_of(vec, l), up_spec(l), down_spec(l)]
    out_specs = [fixed((T, D)), fixed((2, D))] if joined else []
    outs = [sds((T, D)), sds((2, D))] if joined else []
    out_specs += [fixed((T, WIDE)), fixed((T, WIDE)), hidden_spec(1), fixed((1, D)), fixed((T, D))]
    outs += [sds((T, WIDE), BF), sds((T, WIDE), BF), sds((1, FH)), sds((1, D)), sds((T, D), BF)]
    return pl.pallas_call(
        functools.partial(body_without, functools.partial(ff_backward, joined), len(args), len(after)),
        grid=(FH // FC,),
        in_specs=specs + [ANY] * len(after),
        out_specs=out_specs,
        out_shape=outs,
        scratch_shapes=[pltpu.VMEM((T, D), BF), pltpu.VMEM((T, D), F32)],
        name="ff_backward",
        **params(10),
    )(*args, *after)


def run_ff_weights(at, mine, got):
    return pl.pallas_call(
        ff_weights,
        in_specs=[SMEM, WHOLE, WHOLE],
        out_specs=[WHOLE] * 4,
        out_shape=[sds((4, PIECE, D), BF)] * 4,
        name="ff_weights",
        **params(7),
    )(at, mine, got)


def run_mixer_backward(l, last, at, g_in, own, other, x1, x0, u, qs, g, ks, vec, inw, outw, sw, sb, skip, after):
    args = [at, g_in, own, other, x1, x0, u, qs, g, ks, vec, inw, outw, sw, sb, skip, FE, FO, IE, IO]
    specs = [SMEM] + [WHOLE] * 8 + [layer_of(m, l) for m in (ks, vec, inw, outw, sw, sb, skip)] + [WHOLE] * 4
    outs = [
        sds((T, D)), sds((2, D)), sds((1, D)), sds((1, 3 * C)), sds((3, 3 * C)), sds((1, 3 * C)), sds((1, C)),
        sds((T, C)), sds((T, D), BF), sds((T, WIDE), BF), sds((T, WIDE), BF), sds((2, D)),
    ]
    tc = pltpu.VMEM((T, C), F32)
    return pl.pallas_call(
        functools.partial(body_without, functools.partial(mixer_backward, last), len(args), len(after)),
        grid=(1,),
        in_specs=specs + [ANY] * len(after),
        out_specs=[WHOLE] * len(outs),
        out_shape=outs,
        scratch_shapes=[
            pltpu.VMEM((T, D), BF), pltpu.VMEM((T, D), BF), pltpu.VMEM((T, C), BF), pltpu.VMEM((T, 3 * C), BF),
            tc, tc, tc, tc, tc, *spectrum_scratch(),
            pltpu.VMEM((6 * H, 2 * C), BF), pltpu.VMEM((6 * H, 2 * C), BF), pltpu.VMEM((T, 2 * C), F32),
        ],
        name="mixer_backward",
        **params(15),
    )(*args, *after)


def run_mixer_weights(at, mine, got, pack=()):
    rows = PIECE + (16 if pack else 0)
    return pl.pallas_call(
        functools.partial(mixer_weights, bool(pack)),
        in_specs=[SMEM] + [WHOLE] * (2 + len(pack)),
        out_specs=[WHOLE] * 4,
        out_shape=[sds((4, rows, C), BF)] * 4,
        name="mixer_weights",
        **params(5),
    )(at, mine, got, *pack)


def run_add(parts, count, after=(), sides=1):
    shape = parts[0].shape[1:] if count > 1 else parts[0].shape
    width = sum(p.shape[-1] for p in parts[:: len(parts) // sides])
    made = pl.pallas_call(
        functools.partial(body_without, functools.partial(add_parts, len(parts), sides), len(parts), len(after)),
        in_specs=[WHOLE] * len(parts) + [ANY] * len(after),
        out_specs=[WHOLE] * count,
        out_shape=[sds(shape[:-1] + (width,), BF)] * count,
        name="add_parts",
        **params(1),
    )(*parts, *after)
    return list(made)


def copy(ref, out_ref):
    out_ref[...] = ref[...]


def run_copy_after(x, after):
    return pl.pallas_call(
        functools.partial(body_without, copy, 1, len(after)),
        in_specs=[WHOLE] + [ANY] * len(after),
        out_specs=WHOLE,
        out_shape=sds(x.shape, x.dtype),
        name="copy_after",
        **params(1),
    )(x, *after)


def run_behind(arrays, after):
    count = len(arrays)
    return pl.pallas_call(
        lambda *refs: None,
        in_specs=[ANY] * (count + len(after)),
        out_specs=[ANY] * count,
        out_shape=[sds(x.shape, x.dtype) for x in arrays],
        input_output_aliases={i: i for i in range(count)},
        name="behind",
        **params(1),
    )(*arrays, *after)


def run_place(body, at, ins, into, shapes, out_specs, steps, width, name):
    aliases = {} if into is None else {3: 0, 4: 1}
    into = [] if into is None else list(into)
    return pl.pallas_call(
        functools.partial(body_without, body, 3, len(into)),
        grid=(steps,),
        in_specs=[SMEM] + [fixed(m.shape) for m in ins] + [ANY] * len(into),
        out_specs=out_specs,
        out_shape=[sds(s) for s in shapes],
        scratch_shapes=[pltpu.VMEM((4 * PIECE, width), F32)],
        input_output_aliases=aliases,
        name=name,
        **params(6),
    )(at, *ins, *into)


def body_without(body, first, count, *refs):
    body(*refs[:first], *refs[first + count :])


def run_place_ff(l, layers, at, ins, into):
    specs = [
        pl.BlockSpec((1, D, 4 * PIECE), lambda p: (l, 0, p)),
        pl.BlockSpec((1, 4 * PIECE, D), lambda p: (l, p, 0)),
    ]
    return run_place(place_ff, at, ins, into, [(layers, D, FH), (layers, FH, D)], specs, 4, D, "place_ff")


def run_place_mixer(l, layers, at, ins, into, lane):
    packed = ins[0].shape[-2] > PIECE
    specs = [
        pl.BlockSpec((1, 1, C, C), lambda n: (l, jnp.minimum(n, 5) // 2, jnp.minimum(n, 5) % 2, 0)),
        pl.BlockSpec((1, C, C), lambda n: (l, 0, jnp.maximum(n - 6, 0))),
    ] + [fixed((PACK, C))] * packed
    shapes = [(layers, 3, D, C), (layers, C, D)] + [(PACK, C)] * packed
    body = functools.partial(place_mixer, packed, lane)
    return run_place(body, at, ins, into, shapes, specs, 8, C, "place_mixer")


SWAP = [(0, 1), (1, 0)]


def swap(x, axis):
    return lax.ppermute(x, axis, SWAP)


def shift(x, axis, k):
    pairs = []
    for y, x_at, c in np.ndindex(4, 4, 2):
        along_x = (axis == FIRST) == (c == 0)
        to = (y, (x_at + k) % 4) if along_x else ((y + k) % 4, x_at)
        pairs.append(((y * 4 + x_at) * 2 + c, (to[0] * 4 + to[1]) * 2 + c))
    return lax.ppermute(x, ("y", "x", "c"), pairs)


def send_first(blocks):
    return [blocks[0]] + [shift(blocks[k], FIRST, k) for k in range(1, 4)]


def sum_first(*gradients, after=()):
    return run_add([p for came in gradients for p in came], 4, after, len(gradients))


def sum_second(pieces, after=()):
    return run_add([pieces[0]] + [shift(pieces[m], SECOND, m) for m in range(1, 4)], 1, after)[0]


def sum_near(piece, after=()):
    return run_add([piece, swap(piece, "zl")], 1, after)[0]


def gather_near(piece):
    row = jnp.stack([piece] + [shift(piece, SECOND, m) for m in range(1, 4)])
    mine = jnp.stack([row] + [shift(row, FIRST, k) for k in range(1, 4)])
    return [mine, swap(mine, "c")]


def gather_plane(piece):
    mine = lax.all_gather(piece, ("y", "x"), axis=0, tiled=False)
    mine = mine.reshape(1, 4, 4, *piece.shape)
    return [mine, swap(mine, "c")]


def run_pack_small(at, gnet, gout, nown, small):
    return pl.pallas_call(
        pack_small,
        in_specs=[SMEM] + [WHOLE] * (3 + len(small)),
        out_specs=[WHOLE] * 2,
        out_shape=[sds((PACK // 2, C))] * 2,
        scratch_shapes=[pltpu.VMEM((PACK, C), F32)],
        name="pack_small",
        **params(2),
    )(at, gnet, gout, nown, *small)


def shards(
    tokens, lengths, norm_gain, norm_bias, in_weight, in_bias, short_weight, short_bias, filter_first, filter_inner,
    filter_biases, filter_out, filter_skip, out_weight, out_bias, up_weight, up_bias, down_weight, down_bias, cotangent,
):
    layers = norm_gain.shape[0]
    half_at = lax.axis_index("zh")
    core = lax.axis_index("c")
    x_at, y_at = lax.axis_index("x"), lax.axis_index("y")
    order = jnp.where(core == 0, x_at, y_at), jnp.where(core == 0, y_at, x_at)
    at = jnp.stack([half_at, lengths[0], x_at, y_at, core, *order]).astype(jnp.int32)

    tokens_other = swap(tokens, "zh")
    rows = jnp.stack(
        [norm_gain[:, 0], norm_bias[:, 0], norm_gain[:, 1], norm_bias[:, 1], out_bias, down_bias, out_bias, out_bias], 1
    )
    other = swap(rows, "zh")
    low = half_at == 0
    vec = jnp.concatenate([jnp.where(low, rows, other), jnp.where(low, other, rows)], 2)

    ks, sines, cosines, inner, fout = run_filter_forward(at, filter_first, filter_inner, filter_biases, filter_out)

    x = run_arrange(at, tokens, tokens_other)
    inw = in_weight.transpose(0, 2, 1, 3)
    inb = in_bias.reshape(layers, 1, 3 * C)
    sw = short_weight.reshape(layers, 3, 3 * C)
    sb = short_bias.reshape(layers, 1, 3 * C)
    skip = filter_skip.reshape(layers, 1, C)
    upb = up_bias.reshape(layers, 1, FH)

    cot = run_copy_after(cotangent, [x])
    cot_other = swap(cot, "zh")
    grad = run_arrange(at, cotangent, cot_other)
    saved = []
    joint = None
    for l in range(layers):
        after = [cot] if l == 0 else []
        made = run_mixer_forward(l, joint, at, x, vec, inw, inb, sw, sb, ks, skip, out_weight, after)
        if joint is not None:
            x, made = made[0], made[1:]
        u, qs, g, p = made
        if l == 0:
            [p] = run_behind([p], [cot_other])
        after = [grad] if l == 0 else []
        last = l == layers - 1
        x1, h, *p2 = run_ff_forward(l, last, at, x, p, swap(p, "zh"), vec, up_weight, upb, down_weight, after)
        saved.append((x, u, qs, g, x1, h))
        joint = p2[0], swap(p2[-1], "zh")
        x = x1
    last_branch = joint

    joint = None
    small = [None] * layers
    norms = {}
    waits = []
    came = {}
    for l in reversed(range(layers)):
        x0, u, qs, g, x1, h = saved[l]
        made = run_ff_backward(l, at, grad, joint, x1, h, vec, up_weight, down_weight, waits)
        if joint is not None:
            grad, norms[l + 1] = made[:2]
            made = made[2:]
        keep, give, gupb, gdnb, p = made
        p, give = run_behind([p, give], [last_branch[1]] if l == layers - 1 else came["mixer", l + 1][1:])
        p_other = swap(p, "zh")
        halves = run_ff_weights(at, keep, swap(give, "c"))
        came["ff", l] = send_first(halves)
        waits = list(halves)
        made = run_mixer_backward(
            l, l == 0, at, grad, p, p_other, x1, x0, u, qs, g, ks, vec, inw, out_weight, sw, sb, skip, waits
        )
        grad, norm1, goutb, ginb, gsw, gsb, gskip, dk, p, keep, give, nown = made
        p, give = run_behind([p, give], came["ff", l][1:])
        joint = (p, swap(p, "zh"), x0)
        small[l] = (norm1, gdnb, goutb, gupb, ginb, gsw, gsb, gskip, dk)
        pack = ()
        if l == 0:
            norms[0] = jnp.zeros_like(nown)
            gfout, gnet = run_filter_backward(at, inner, fout, sines, cosines, [s[-1] for s in small])
            pack = run_pack_small(at, gnet, gfout, nown, [m for l in range(layers) for m in (norms[l], *small[l][:-1])])
            pack = pack[0], swap(pack[1], "c")
        halves = run_mixer_weights(at, keep, swap(give, "c"), pack)
        came["mixer", l] = send_first(halves)
        waits = list(halves)
        if l == layers - 1:
            result = run_finish_result(at, saved[l][4], *last_branch, vec, l)
            waits.append(result)

    later = sum_near(sum_second(sum_first(came["ff", 1], came["mixer", 1], after=[p])))
    ff = sum_near(sum_second(sum_first(came["ff", 0])))
    mixer = sum_near(sum_second(sum_first(came["mixer", 0])))
    grad = run_finish_grad(at, grad, *joint, vec, 0, waits)
    later = gather_plane(later)
    ff_out = run_place_ff(1, layers, at, later, None)
    mixer_out = run_place_mixer(1, layers, at, later, None, D)
    ff_out = run_place_ff(0, layers, at, gather_near(ff), ff_out)
    *mixer_out, pack = run_place_mixer(0, layers, at, gather_near(mixer), mixer_out, 0)

    net = pack[:SHARED]
    net = net + swap(net, "zh")
    pack = pack[SHARED:].reshape(layers, -1, C)
    first_norm = jnp.where(low, net[NET : NET + 4 : 2], net[NET + 1 : NET + 4 : 2])
    norm_rows = jnp.stack([jnp.concatenate([first_norm, pack[0, 2:4]]), pack[1, :4]])

    def apart(a):
        return jnp.stack([a[..., :NET], a[..., NET:]])

    return (
        result,
        grad,
        norm_rows[:, 0:4:2],
        norm_rows[:, 1:4:2],
        mixer_out[0].transpose(0, 2, 1, 3),
        pack[:, 10:13],
        pack[:, 13:22].reshape(short_weight.shape),
        pack[:, 22:25],
        apart(net[:EMB, 256:]),
        jnp.stack([apart(net[:NET, :128]), apart(net[:NET, 128:256])], 1),
        apart(net[40:43, 256:]),
        pack[:, 26:90],
        pack[:, 25],
        mixer_out[1],
        pack[:, 5],
        ff_out[0],
        pack[:, 6:10].reshape(layers, FH),
        ff_out[1],
        pack[:, 4],
    )


def solution(mesh):
    names = ("zl", "y", "x", "c", "zh")
    fine = Mesh(mesh.devices.reshape(2, 4, 4, 2, 2), names)
    dp = ("zl", "y", "x", "c")
    rows = P(dp, "zh")
    third, fourth = P(None, None, "zh"), P(None, None, None, "zh")
    second, middle = P(None, "zh"), P(None, "zh", None)
    placed = (
        rows, P(dp), third, third, fourth, third, fourth, third, P(), P(), P(), third, second, middle, second, third,
        second, middle, second, rows,
    )
    return jax.shard_map(
        shards,
        mesh=fine,
        in_specs=placed,
        out_specs=(
            rows, rows, third, third, fourth, third, fourth, third, P(), P(), P(), third, second, middle, second, third,
            second, middle, second,
        ),
        check_vma=False,
    )
```

```python
import functools
import math

import jax
import jax.numpy as jnp
import ml_dtypes
import numpy as np
from jax import lax
from jax.experimental import pallas as pl
from jax.experimental.pallas import tpu as pltpu
from jax.sharding import Mesh
from jax.sharding import PartitionSpec as P

D = 768
T = 512
H = T // 2
C = 384
FH = 1536
NET = 64
EMB = 33
BANDS = 16
PIECE = 96
EPSILON = 1e-05
HIGH = lax.Precision.HIGHEST
F32 = jnp.float32
BF = jnp.bfloat16

ORDER = np.concatenate([np.arange(0, T, 2), np.arange(1, T, 2)])


def split_table(t):
    hi = t.astype(ml_dtypes.bfloat16)
    lo = (t - hi.astype(np.float64)).astype(ml_dtypes.bfloat16)
    return hi, lo


def wave_tables():
    n = np.arange(H)
    even = 2 * math.pi * (np.outer(n, 2 * n) % (2 * T)) / (2 * T)
    odd = 2 * math.pi * (np.outer(n, 2 * n + 1) % (2 * T)) / (2 * T)
    alt = np.where(n % 2 == 0, 1.0, -1.0)
    out = []
    for ang in (even, odd):
        co, si = np.cos(ang), np.sin(ang)
        si[0] = alt
        hi, lo = split_table(np.concatenate([co, si], 0))
        out.append(np.concatenate([hi, lo, hi], 1))
        hi, lo = split_table(np.concatenate([co.T, si.T], 1))
        out.append(np.concatenate([hi, lo, hi], 1))
    fe, ie, fo, io = out
    return fe, fo, ie, io


FE, FO, IE, IO = wave_tables()


def slot_features():
    slots = ORDER.astype(np.float64)
    freqs = 0.0001 + (BANDS - 1 - 0.0001) * np.arange(BANDS) / (BANDS - 1)
    angle = 2 * math.pi * slots[:, None] * freqs[None, :] / T
    times = (slots / (T - 1))[:, None]
    feats = np.concatenate([times, np.cos(angle), -np.sin(angle), np.zeros((T, 128 - EMB))], 1)
    return feats.astype(np.float32), np.broadcast_to(times, (T, 128)).astype(np.float32)


FEATS, TIMES = slot_features()


def dot(a, b):
    return lax.dot_general(a, b, (((1,), (0,)), ((), ())), preferred_element_type=F32)


def dot_nt(a, b):
    return lax.dot_general(a, b, (((1,), (1,)), ((), ())), preferred_element_type=F32)


def dot_tn(a, b):
    return lax.dot_general(a, b, (((0,), (0,)), ((), ())), preferred_element_type=F32)


def normalize(x):
    mean = jnp.mean(x, -1, keepdims=True)
    scale = lax.rsqrt(jnp.mean(x * x, -1, keepdims=True) - mean * mean + EPSILON)
    return (x - mean) * scale, scale


def norm_pull(dn, x, gain):
    xhat, scale = normalize(x)
    ds = dn * gain
    first = jnp.mean(ds, -1, keepdims=True)
    second = jnp.mean(ds * xhat, -1, keepdims=True)
    return scale * (ds - first - xhat * second), dn * xhat


def row_mask(start, rows, length):
    r = start + lax.broadcasted_iota(jnp.int32, (rows, 1), 0)
    slot = jnp.where(r < H, 2 * r, 2 * (r - H) + 1)
    return (slot < length).astype(F32)


def down_one(x):
    r = lax.broadcasted_iota(jnp.int32, x.shape, 0)
    return jnp.where(r == 0, 0.0, pltpu.roll(x, 1, 0))


def up_one(x):
    r = lax.broadcasted_iota(jnp.int32, x.shape, 0)
    return jnp.where(r == x.shape[0] - 1, 0.0, pltpu.roll(x, x.shape[0] - 1, 0))


def put_split(ref, value, rows, lanes):
    hi = value.astype(BF)
    lo = (value - hi.astype(F32)).astype(BF)
    step = ref.shape[0] // 3
    ref[pl.ds(rows, value.shape[0]), lanes] = hi
    ref[pl.ds(step + rows, value.shape[0]), lanes] = hi
    ref[pl.ds(2 * step + rows, value.shape[0]), lanes] = lo


def top_row(shape):
    return lax.broadcasted_iota(jnp.int32, shape, 0) == 0


def butterfly(even, odd, lanes):
    ce, se = even[pl.ds(0, H), lanes], even[pl.ds(H, H), lanes]
    co, so = odd[pl.ds(0, H), lanes], odd[pl.ds(H, H), lanes]
    top = top_row(ce.shape)
    return ce + co, ce - co, jnp.where(top, se, se + so), jnp.where(top, so, se - so)


def spectrum_product(a, k, conj):
    a1, a2, b1, b2 = a
    k1, k2, l1, l2 = k
    top = top_row(a1.shape)
    aa, bb, cc, dd = a1 * k1, b1 * l1, a2 * k2, b2 * l2
    if conj:
        y1 = jnp.where(top, aa, aa + bb)
        y2 = jnp.where(top, cc, cc + dd)
        m1 = jnp.where(top, bb + dd, b1 * k1 - a1 * l1)
        m2 = jnp.where(top, b2 * l1 - b1 * l2, b2 * k2 - a2 * l2)
    else:
        y1 = jnp.where(top, aa, aa - bb)
        y2 = jnp.where(top, cc, cc - dd)
        m1 = jnp.where(top, bb - dd, a1 * l1 + b1 * k1)
        m2 = jnp.where(top, b1 * l2 + b2 * l1, a2 * l2 + b2 * k2)
    return y1, y2, m1, m2


def put_inverse(rhs_e, rhs_o, y, lanes):
    y1, y2, m1, m2 = y
    top = top_row(y1.shape)
    unit = 1.0 / T
    w = jnp.where(top, 0.5 * unit, unit)
    put_split(rhs_e, (y1 + y2) * w, 0, lanes)
    put_split(rhs_o, (y1 - y2) * w, 0, lanes)
    put_split(rhs_e, jnp.where(top, m1, m1 + m2) * unit, H, lanes)
    put_split(rhs_o, jnp.where(top, m2, m1 - m2) * unit, H, lanes)


def lanes_of(block):
    return pl.ds(block * 128, 128)


def short_conv(u_ref, sw_ref, sb_ref, block):
    out = []
    for s in range(3):
        at = lanes_of(s * (C // 128) + block)
        ue, uo = u_ref[pl.ds(0, H), at], u_ref[pl.ds(H, H), at]
        t0, t1, t2 = (sw_ref[j : j + 1, at] for j in range(3))
        bias = sb_ref[0:1, at]
        uo_d = down_one(uo)
        we = t2 * ue + t1 * uo_d + t0 * down_one(ue) + bias
        wo = t2 * uo + t1 * ue + t0 * uo_d + bias
        out.append((we, wo))
    return out


def hdot(a, b, dims=(1, 0)):
    return lax.dot_general(
        a, b, (((dims[0],), (dims[1],)), ((), ())), precision=HIGH, preferred_element_type=F32
    )


def decay_of(half_at, times_ref):
    slow = math.log(0.01) / 1.5
    fast = math.log(0.01) / 0.3
    channel = (half_at * C + lax.broadcasted_iota(jnp.int32, (1, C), 1)).astype(F32)
    rates = jnp.abs(slow + (fast - slow) * channel / (D - 1))
    return jnp.exp(-times_ref[:, 0:1] * rates) + 0.05


def sin_cos(x):
    k = jnp.floor(x * (2 / math.pi) + 0.5)
    r = ((x - k * 1.5703125) - k * 4.837512969970703125e-4) - k * 7.54978995489188e-8
    rr = r * r
    sine = r + r * rr * (-1.6666654611e-1 + rr * (8.3321608736e-3 + rr * -1.9515295891e-4))
    cosine = 1.0 - 0.5 * rr + rr * rr * (
        4.166664568298827e-2 + rr * (-1.388731625493765e-3 + rr * 2.443315711809948e-5)
    )
    quarter = k - 4.0 * jnp.floor(k * 0.25)
    odd = (quarter == 1.0) | (quarter == 3.0)
    s = jnp.where(odd, cosine, sine)
    c = jnp.where(odd, sine, cosine)
    return jnp.where(quarter >= 2.0, -s, s), jnp.where((quarter == 1.0) | (quarter == 2.0), -c, c)


def filter_forward(
    at_ref, feats_ref, times_ref, first_ref, inner_ref, bias_ref, out_ref, fe_ref, fo_ref,
    ks_ref, sin_ref, cos_ref, both_ref, wide_ref, first_s, bias_s, k_s, rhs_e, rhs_o, se, so,
):
    for ref in (both_ref, wide_ref, first_s, bias_s):
        ref[...] = jnp.zeros_like(ref)
    for l in range(2):
        at = pl.ds(l * NET, NET)
        first_s[0:EMB, at] = first_ref[l]
        bias_s[0:3, at] = bias_ref[l]
        wide_ref[l, at, :] = out_ref[l]
        for i in range(2):
            both_ref[i, at, at] = inner_ref[l, i]
    low = feats_ref[...]
    for i in range(3):
        weight = first_s[...] if i == 0 else both_ref[i - 1]
        low, cosine = sin_cos(hdot(low, weight) + bias_s[i : i + 1, :])
        sin_ref[i] = low
        cos_ref[i] = cosine
    decay = decay_of(at_ref[0], times_ref)
    for l in range(2):
        k_s[...] = hdot(sin_ref[2], wide_ref[l]) * decay
        for b in range(C // 128):
            at = lanes_of(b)
            put_split(rhs_e, k_s[pl.ds(0, H), at], 0, at)
            put_split(rhs_o, k_s[pl.ds(H, H), at], 0, at)
        se[...] = dot(fe_ref[...], rhs_e[...])
        so[...] = dot(fo_ref[...], rhs_o[...])
        for b in range(C // 128):
            at = lanes_of(b)
            for i, v in enumerate(butterfly(se, so, at)):
                ks_ref[l, i, :, at] = v


def filter_backward(at_ref, feats_ref, times_ref, inner_ref, out_ref, sin_ref, cos_ref, dk0_ref, dk1_ref, gout_ref, gnet_ref):
    decay = decay_of(at_ref[0], times_ref)
    ds = jnp.zeros((T, 128), F32)
    for l, dk_ref in enumerate((dk0_ref, dk1_ref)):
        dk = dk_ref[...] * decay
        gout_ref[l] = hdot(sin_ref[2], dk, (0, 0))[l * NET : (l + 1) * NET]
        ds += hdot(dk, out_ref[l], (1, 1))
    lane = lax.broadcasted_iota(jnp.int32, (NET, 128), 1)
    gnet_ref[...] = jnp.zeros_like(gnet_ref)
    for i in (2, 1, 0):
        da = ds * cos_ref[i]
        gnet_ref[40 + i : 41 + i, pl.ds(256, 128)] = jnp.sum(da, 0, keepdims=True)
        if i > 0:
            block = hdot(sin_ref[i - 1], da, (0, 0))
            gnet_ref[:, pl.ds((i - 1) * 128, 128)] = jnp.where(lane < NET, block[:NET], block[NET:])
            ds = hdot(da, inner_ref[i - 1], (1, 1))
        else:
            gnet_ref[0:40, pl.ds(256, 128)] = hdot(feats_ref[...], da, (0, 0))[0:40]


def arrange(at_ref, own_ref, other_ref, out_ref, tmp):
    for half, first in ((0, own_ref), (1, other_ref)):
        for b in range(C // 128):
            tmp[b] = first[:, lanes_of(b)].astype(F32)

        def put(first_lane):
            for b in range(C // 128):
                to = pl.ds(first_lane + b * 128, 128)
                out_ref[pl.ds(0, H), to] = tmp[b, pl.ds(0, H, stride=2), :]
                out_ref[pl.ds(H, H), to] = tmp[b, pl.ds(1, H, stride=2), :]

        pl.when(at_ref[0] == half)(functools.partial(put, 0))
        pl.when(at_ref[0] != half)(functools.partial(put, C))


def my_lanes(at_ref, row):
    return jnp.where(at_ref[0] == 0, row[:, :C], row[:, C:])


def by_slot(at_ref, src_ref, out_ref, tmp):
    def put(first_lane):
        for b in range(C // 128):
            lanes = pl.ds(first_lane + b * 128, 128)
            tmp[b, pl.ds(0, H, stride=2), :] = src_ref[pl.ds(0, H), lanes]
            tmp[b, pl.ds(1, H, stride=2), :] = src_ref[pl.ds(H, H), lanes]

    pl.when(at_ref[0] == 0)(functools.partial(put, 0))
    pl.when(at_ref[0] != 0)(functools.partial(put, C))
    for b in range(C // 128):
        out_ref[:, lanes_of(b)] = tmp[b].astype(out_ref.dtype)


def finish_result(at_ref, x_ref, own_ref, other_ref, vec_ref, out_ref, y_s, tmp):
    def put(first_lane):
        lanes = pl.ds(first_lane, C)

        def body(start, c):
            rows = pl.ds(start, RB)
            y = own_ref[rows, :].astype(F32) + other_ref[rows, :].astype(F32) + vec_ref[0, 5:6, lanes]
            y_s[rows, lanes] = x_ref[rows, lanes] + row_mask(start, RB, at_ref[1]) * y
            return c

        row_loop(body)

    pl.when(at_ref[0] == 0)(functools.partial(put, 0))
    pl.when(at_ref[0] != 0)(functools.partial(put, C))
    by_slot(at_ref, y_s, out_ref, tmp)


def finish_grad(at_ref, g_ref, own_ref, other_ref, x_ref, vec_ref, out_ref, x_s, tmp):
    def body(start, c):
        at = pl.ds(start, RB)
        dn = own_ref[at, :].astype(F32) + other_ref[at, :].astype(F32)
        x_s[at, :] = g_ref[at, :] + norm_pull(dn, x_ref[at, :], vec_ref[0, 0:1, :])[0]
        return c

    row_loop(body)
    by_slot(at_ref, x_s, out_ref, tmp)


def add_branch(x_ref, own_ref, other_ref, vec_ref, row, length, start, rows):
    at = pl.ds(start, rows)
    y = own_ref[at, :].astype(F32) + other_ref[at, :].astype(F32) + vec_ref[row : row + 1, :]
    return x_ref[at, :] + row_mask(start, rows, length) * y


RB = 128


def row_loop(body, init=0):
    def step(i, c):
        return body(pl.multiple_of(i * RB, RB), c)

    return lax.fori_loop(0, T // RB, step, init)


def mixer_forward(l, joined, *refs):
    at_ref, x_ref = refs[:2]
    refs = refs[2:]
    if joined:
        own_ref, other_ref, prev_ref = refs[:3]
        refs = refs[3:]
    (vec_ref, inw_ref, inb_ref, sw_ref, sb_ref, ks_ref, skip_ref, fe_ref, fo_ref, ie_ref, io_ref, outw_ref) = refs[:12]
    refs = refs[12:]
    if joined:
        xo_ref = refs[0]
        refs = refs[1:]
    u_ref, qs_ref, g_ref, p_ref, a_s, w0_s, q_s, rhs_e, rhs_o, se, so, rhs2_e, rhs2_o, z_s = refs

    def first(start, c):
        at = pl.ds(start, RB)
        if joined:
            x = add_branch(x_ref, own_ref, other_ref, prev_ref.at[l - 1], 5, at_ref[1], start, RB)
            xo_ref[at, :] = x
        else:
            x = x_ref[at, :]
        xhat, _ = normalize(x)
        a_s[at, :] = (xhat * vec_ref[l, 0:1, :] + vec_ref[l, 1:2, :]).astype(BF)
        return c

    row_loop(first)
    for s in range(3):
        at = pl.ds(s * C, C)
        u_ref[:, at] = dot(a_s[...], inw_ref[l, s]) + inb_ref[l, 0:1, at]
    for b in range(C // 128):
        at = lanes_of(b)
        (w0e, w0o), (w1e, w1o), (w2e, w2o) = short_conv(u_ref, sw_ref.at[l], sb_ref.at[l], b)
        w0_s[pl.ds(0, H), at] = w0e
        w0_s[pl.ds(H, H), at] = w0o
        qe, qo = w2e * w1e, w2o * w1o
        q_s[pl.ds(0, H), at] = qe
        q_s[pl.ds(H, H), at] = qo
        put_split(rhs_e, qe, 0, at)
        put_split(rhs_o, qo, 0, at)
    se[...] = dot(fe_ref[...], rhs_e[...])
    so[...] = dot(fo_ref[...], rhs_o[...])
    for b in range(C // 128):
        at = lanes_of(b)
        spec = butterfly(se, so, at)
        for i, v in enumerate(spec):
            qs_ref[i, :, at] = v
        y = spectrum_product(spec, [ks_ref[l, i, :, at] for i in range(4)], False)
        put_inverse(rhs2_e, rhs2_o, y, at)
    se[pl.ds(0, H), :] = dot(ie_ref[...], rhs2_e[...])
    se[pl.ds(H, H), :] = dot(io_ref[...], rhs2_o[...])

    def last(start, c):
        at = pl.ds(start, RB)
        g = se[at, :] + skip_ref[l, 0:1, :] * q_s[at, :]
        g_ref[at, :] = g
        z_s[at, :] = (g * w0_s[at, :]).astype(BF)
        return c

    row_loop(last)
    p_ref[...] = dot(z_s[...], outw_ref[l]).astype(BF)


def gelu_parts(h):
    c0 = math.sqrt(2 / math.pi)
    hh = h * h
    t = jnp.tanh(c0 * (h + 0.044715 * (hh * h)))
    half = 0.5 * (1.0 + t)
    return half, t, hh, c0


def collect(j, acc, part):
    @pl.when(j == 0)
    def _():
        acc[...] = part

    @pl.when(j > 0)
    def _():
        acc[...] += part


def ff_forward(last, at_ref, x_ref, own_ref, other_ref, vec_ref, up_ref, upb_ref, dn_ref, xo_ref, h_ref, *refs):
    *p_refs, b_s, acc = refs
    j = pl.program_id(0)

    @pl.when(j == 0)
    def _():
        def first(start, c):
            at = pl.ds(start, RB)
            x = add_branch(x_ref, own_ref, other_ref, vec_ref.at[0], 4, at_ref[1], start, RB)
            xo_ref[at, :] = x
            xhat, _ = normalize(x)
            b_s[at, :] = (xhat * vec_ref[0, 2:3, :] + vec_ref[0, 3:4, :]).astype(BF)
            return c

        row_loop(first)

    h = dot(b_s[...], up_ref[0]) + upb_ref[0]
    h_ref[...] = h
    half, _, _, _ = gelu_parts(h)
    collect(j, acc, dot((h * half).astype(BF), dn_ref[0]))

    @pl.when(j == pl.num_programs(0) - 1)
    def _():
        if not last:
            p_refs[0][...] = acc[...].astype(BF)
        else:
            low, high = acc[:, :C].astype(BF), acc[:, C:].astype(BF)
            own = at_ref[0] == 0
            p_refs[0][...] = jnp.where(own, low, high)
            p_refs[1][...] = jnp.where(own, high, low)


def put_by_core(at_ref, keep_ref, give_ref, at, low, high):
    @pl.when(at_ref[4] == 0)
    def _():
        keep_ref[at] = low
        give_ref[at] = high

    @pl.when(at_ref[4] != 0)
    def _():
        keep_ref[at] = high
        give_ref[at] = low


def ff_backward(joined, *refs):
    at_ref, g_ref = refs[:2]
    refs = refs[2:]
    if joined:
        own_ref, other_ref, xn_ref, nvec_ref = refs[:4]
        refs = refs[4:]
    x_ref, h_ref, vec_ref, up_ref, dn_ref = refs[:5]
    refs = refs[5:]
    if joined:
        go_ref, refs = refs[0], refs[1:]
    keep_ref, give_ref, small_ref, p_ref, dm_s, acc, upb_s = refs
    j = pl.program_id(0)

    @pl.when(j == 0)
    def _():
        def first(start, c):
            at = pl.ds(start, RB)
            g = g_ref[at, :]
            sums, s1, s2 = c
            if joined:
                dn = own_ref[at, :].astype(F32) + other_ref[at, :].astype(F32)
                dx, dg = norm_pull(dn, xn_ref[at, :], nvec_ref[0, 0:1, :])
                g = g + dx
                go_ref[at, :] = g
                s1 = s1 + jnp.sum(dg, 0, keepdims=True)
                s2 = s2 + jnp.sum(dn, 0, keepdims=True)
            dm = (row_mask(start, RB, at_ref[1]) * g).astype(BF)
            dm_s[at, :] = dm
            xhat, _ = normalize(x_ref[at, :])
            b = (xhat * vec_ref[0, 2:3, :] + vec_ref[0, 3:4, :]).astype(BF)
            put_by_core(at_ref, keep_ref, give_ref, (at, pl.ds(0, D)), dm, b)
            return sums + jnp.sum(dm.astype(F32), 0, keepdims=True), s1, s2

        zero = jnp.zeros((1, D), F32)
        sums, s1, s2 = row_loop(first, (zero, zero, zero))
        small_ref[...] = jnp.zeros_like(small_ref)
        for i, row in enumerate((s1, s2, sums)):
            small_ref[i : i + 1, :] = my_lanes(at_ref, row)

    h = h_ref[...]
    half, t, hh, c0 = gelu_parts(h)
    e = (h * half).astype(BF)
    slope = half + 0.5 * c0 * h * (1.0 - t * t) * (1.0 + 3 * 0.044715 * hh)
    dh = (dot_nt(dm_s[...], dn_ref[0]) * slope).astype(BF)
    put_by_core(at_ref, keep_ref, give_ref, (slice(None), pl.ds(pl.multiple_of(D + j * FC, 128), FC)), e, dh)
    upb_s[0:1, pl.ds(pl.multiple_of(j * FC, 128), FC)] = jnp.sum(dh.astype(F32), 0, keepdims=True)
    collect(j, acc, dot_nt(dh, up_ref[0]))

    @pl.when(j == pl.num_programs(0) - 1)
    def _():
        p_ref[...] = acc[...].astype(BF)
        for i in range(4):
            small_ref[3 + i : 4 + i, :] = upb_s[0:1, i * C : (i + 1) * C]


FIRST, SECOND = 5, 6
WIDE = 3 * D


class Swapped:
    def __init__(self, at_ref):
        self.at_ref = at_ref

    def __getitem__(self, i):
        return self.at_ref[{FIRST: SECOND, SECOND: FIRST}.get(i, i)]


def put_pieces(at_ref, ref, value):
    for n in range(4):
        ref[lax.rem(n - at_ref[SECOND] + 4, 4), pl.ds(0, PIECE)] = value[n * PIECE : (n + 1) * PIECE]


def ff_weights(at_ref, mine_ref, got_ref, *outs):
    for k, out_ref in enumerate(outs):
        block = lax.rem(at_ref[FIRST] + k, 4)
        lanes = pl.ds(pl.multiple_of(D + block * 4 * PIECE, 128), 4 * PIECE)
        total = sum(dot_tn(ref[:, lanes], ref[:, pl.ds(0, D)]) for ref in (mine_ref, got_ref))
        put_pieces(at_ref, out_ref, total.astype(BF))


def mixer_backward(
    l, last, at_ref, g_in_ref, own_ref, other_ref, x1_ref, x0_ref, u_ref, qs_ref, g_ref, ks_ref, vec_ref, inw_ref, outw_ref,
    sw_ref, sb_ref, skip_ref, fe_ref, fo_ref, ie_ref, io_ref,
    go_ref, small_ref, dk_ref, p_ref, keep_ref, give_ref, dy_ref, a_ref, z_ref, du_ref, dz_s, dg_s, w1_s, w2_s, dw0_s, rhs_e, rhs_o, se, so, rhs2_e, rhs2_o, inv_s,
):
    small_ref[...] = jnp.zeros_like(small_ref)

    def first(start, c):
        at = pl.ds(start, RB)
        sums, s1, s2 = c
        dn = own_ref[at, :].astype(F32) + other_ref[at, :].astype(F32)
        dx, dg = norm_pull(dn, x1_ref[at, :], vec_ref[l, 2:3, :])
        g = g_in_ref[at, :] + dx
        go_ref[at, :] = g
        dy = (row_mask(start, RB, at_ref[1]) * g).astype(BF)
        dy_ref[at, :] = dy
        xhat, _ = normalize(x0_ref[at, :])
        a_ref[at, :] = (xhat * vec_ref[l, 0:1, :] + vec_ref[l, 1:2, :]).astype(BF)
        return (
            sums + jnp.sum(dy.astype(F32), 0, keepdims=True),
            s1 + jnp.sum(dg, 0, keepdims=True),
            s2 + jnp.sum(dn, 0, keepdims=True),
        )

    zero = jnp.zeros((1, D), F32)
    sums, s1, s2 = row_loop(first, (zero, zero, zero))
    for i, row in enumerate((s1, s2, sums)):
        small_ref[i : i + 1, :] = my_lanes(at_ref, row)
    dz_s[...] = dot_nt(dy_ref[...], outw_ref[l])
    halves = (pl.ds(0, H), pl.ds(H, H))
    for b in range(C // 128):
        at = lanes_of(b)
        w0, w1, w2 = short_conv(u_ref, sw_ref.at[l], sb_ref.at[l], b)
        dskip = 0.0
        for i, (rows, rhs) in enumerate(zip(halves, (rhs_e, rhs_o))):
            dz, g = dz_s[rows, at], g_ref[rows, at]
            z_ref[rows, at] = (g * w0[i]).astype(BF)
            dw0_s[rows, at] = dz * g
            dg = dz * w0[i]
            dg_s[rows, at] = dg
            dskip = dskip + jnp.sum(dg * (w2[i] * w1[i]), 0, keepdims=True)
            w1_s[rows, at] = w1[i]
            w2_s[rows, at] = w2[i]
            put_split(rhs, dg, 0, at)
        small_ref[18:19, at] = dskip
    se[...] = dot(fe_ref[...], rhs_e[...])
    so[...] = dot(fo_ref[...], rhs_o[...])
    for b in range(C // 128):
        at = lanes_of(b)
        spec = butterfly(se, so, at)
        put_inverse(rhs2_e, rhs2_o, spectrum_product(spec, [ks_ref[l, i, :, at] for i in range(4)], True), at)
        put_inverse(
            rhs2_e, rhs2_o, spectrum_product(spec, [qs_ref[i, :, at] for i in range(4)], True), pl.ds(C + b * 128, 128)
        )
    inv_s[pl.ds(0, H), :] = dot(ie_ref[...], rhs2_e[...])
    inv_s[pl.ds(H, H), :] = dot(io_ref[...], rhs2_o[...])
    dk_ref[...] = inv_s[:, pl.ds(C, C)]
    for b in range(C // 128):
        at = lanes_of(b)
        dw = [[dw0_s[rows, at] for rows in halves], [], []]
        for rows in halves:
            dq = inv_s[rows, at] + skip_ref[l, 0:1, at] * dg_s[rows, at]
            dw[1].append(dq * w2_s[rows, at])
            dw[2].append(dq * w1_s[rows, at])
        for s in range(3):
            to = lanes_of(s * (C // 128) + b)
            ue, uo = u_ref[halves[0], to], u_ref[halves[1], to]
            t0, t1, t2 = (sw_ref[l, j : j + 1, to] for j in range(3))
            de, do = dw[s]
            de_u, do_u = up_one(de), up_one(do)
            due = (t2 * de + t1 * do + t0 * de_u).astype(BF)
            duo = (t2 * do + t1 * de_u + t0 * do_u).astype(BF)
            du_ref[halves[0], to] = due
            du_ref[halves[1], to] = duo
            uo_d = down_one(uo)
            small_ref[3 + s : 4 + s, at] = jnp.sum(due.astype(F32) + duo.astype(F32), 0, keepdims=True)
            taps = de * down_one(ue) + do * uo_d, de * uo_d + do * ue, de * ue + do * uo
            for j, tap in enumerate(taps):
                small_ref[6 + 3 * j + s : 7 + 3 * j + s, at] = jnp.sum(tap, 0, keepdims=True)
            small_ref[15 + s : 16 + s, at] = jnp.sum(de + do, 0, keepdims=True)
    part = dot_nt(du_ref[:, pl.ds(0, C)], inw_ref[l, 0])
    for s in range(1, 3):
        part += dot_nt(du_ref[:, pl.ds(s * C, C)], inw_ref[l, s])
    p_ref[...] = part.astype(BF)

    def spread(start, c):
        rows = pl.ds(start, RB)
        a, dy, z = a_ref[rows, :], dy_ref[rows, :], z_ref[rows, :]
        du = [du_ref[rows, pl.ds(s * C, C)] for s in range(3)]
        lane = 0
        for low, high in ((a, a), (du[0], du[2]), (a, dy), (du[1], z)):
            put_by_core(at_ref, keep_ref, give_ref, (rows, pl.ds(lane, low.shape[1])), low, high)
            lane += low.shape[1]
        return c

    row_loop(spread)
    if last:

        def terms(start, c):
            at = pl.ds(start, RB)
            dn = p_ref[at, :].astype(F32)
            xhat, _ = normalize(x0_ref[at, :])
            return c[0] + jnp.sum(dn * xhat, 0, keepdims=True), c[1] + jnp.sum(dn, 0, keepdims=True)

        s1, s2 = row_loop(terms, (zero, zero))
        for i, row in enumerate((s1, s2)):
            for half in range(2):
                small_ref[20 + 2 * i + half : 21 + 2 * i + half, :] = row[:, half * C : (half + 1) * C]


def put_split_rows(value):
    hi = value.astype(BF).astype(F32)
    return jnp.concatenate([hi, value - hi], 0).astype(BF)


def mixer_weights(packed, at_ref, mine_ref, got_ref, *refs):
    if packed:
        pack_refs, refs = refs[:2], refs[2:]
    for k, out_ref in enumerate(refs):
        block = lax.rem(at_ref[FIRST] + k, 4)
        left = pl.multiple_of(jnp.where(block < 2, block, block + 1) * C, 128)
        right = pl.multiple_of(jnp.where(block < 2, D, 2 * D + C), 128)
        total = sum(dot_tn(ref[:, pl.ds(left, C)], ref[:, pl.ds(right, C)]) for ref in (mine_ref, got_ref))
        put_pieces(at_ref, out_ref, total.astype(BF))
        if packed:
            for n in range(4):
                rows = pl.ds(pl.multiple_of(block * 32 + n * 8, 8), 8)
                value = pack_refs[0][rows, :] + pack_refs[1][rows, :]
                out_ref[lax.rem(n - at_ref[SECOND] + 4, 4), pl.ds(PIECE, 16)] = put_split_rows(value)


def add_parts(count, sides, *refs):
    ins, outs = refs[:count], refs[count:]
    lane = 0
    for side in range(sides):
        some = ins[side * count // sides : (side + 1) * count // sides]
        lanes = slice(lane, lane + some[0].shape[-1])
        lane = lanes.stop
        for i, out in enumerate(outs):
            total = functools.reduce(jnp.add, [(r[i] if len(outs) > 1 else r[...]).astype(F32) for r in some])
            rows = (slice(None),) * (total.ndim - 2)
            out[rows + (slice(0, PIECE), lanes)] = total[rows + (slice(0, PIECE),)].astype(BF)
            if total.shape[-2] > PIECE:
                for n in range(total.shape[0] if total.ndim > 2 else 1):
                    value = total[n] if total.ndim > 2 else total
                    value = value[PIECE : PIECE + 8] + value[PIECE + 8 : PIECE + 16]
                    to = (n, slice(PIECE, PIECE + 16)) if total.ndim > 2 else slice(PIECE, PIECE + 16)
                    out[to] = put_split_rows(value)


def gather_block(at_ref, ref, block, tmp, pack_ref=None, first=0):
    for m in range(4):
        if len(ref.shape) == 5:
            by_x = (at_ref[4] == 0) != isinstance(at_ref, Swapped)
            at = 0, jnp.where(by_x, m, block), jnp.where(by_x, block, m)
        else:
            at = lax.rem(at_ref[FIRST] - block + 4, 4), lax.rem(at_ref[SECOND] - m + 4, 4)
        tmp[pl.ds(m * PIECE, PIECE), :] = ref[at + (slice(0, PIECE),)].astype(tmp.dtype)
        if pack_ref is not None:
            extra = ref[at + (slice(PIECE, PIECE + 16),)].astype(F32)
            pack_ref[pl.ds(pl.multiple_of(first + m * 8, 8), 8), :] = extra[:8] + extra[8:]


def gather_half(at_ref, half, refs, *args):
    own = at_ref[4] == half
    pl.when(own)(lambda: gather_block(at_ref, refs[0], *args))
    pl.when(jnp.logical_not(own))(lambda: gather_block(Swapped(at_ref), refs[1], *args))


def place_ff(at_ref, *refs):
    ins, (gup_ref, gdn_ref, tmp) = refs[:2], refs[-3:]
    block = pl.program_id(0)
    gather_half(at_ref, 0, ins, block, gdn_ref.at[0])
    gather_half(at_ref, 1, ins, block, tmp)
    gup_ref[0] = tmp[...].T.astype(F32)


def place_mixer(packed, at_ref, *refs):
    ins, outs, tmp = refs[:2], refs[2:-1], refs[-1]
    gin_ref, gout_ref = outs[:2]
    pack_ref = outs[2] if packed else None
    step = pl.program_id(0)
    for i in range(2):
        block = lax.rem(step, 2) * 2 + i
        first = step * 64 + i * 32

        @pl.when(step < 3)
        def _():
            to = gin_ref.at[0, 0, pl.ds(i * C, C), :]
            gather_half(at_ref, step // 2, ins, block, to, pack_ref, first)

        @pl.when(step == 3)
        def _():
            gather_half(at_ref, 1, ins, block, tmp, pack_ref, first)
            gout_ref[0, :, pl.ds(i * C, C)] = tmp[...].T.astype(F32)


PACK = 256
SHARED = 72
LAYER_ROWS = 92


def pack_small(at_ref, gnet_ref, gout_ref, *refs):
    keep_ref, give_ref, out_ref = refs[-3:]
    out_ref[...] = jnp.zeros_like(out_ref)
    out_ref[0:NET, :] = gnet_ref[...]
    out_ref[NET : NET + 4, :] = refs[1][20:24, :]
    for l in range(2):
        ff_ref, mixer_ref = refs[2 * l : 2 * l + 2]
        row = SHARED + LAYER_ROWS * l
        if l > 0:
            out_ref[row : row + 2, :] = refs[0][0:2, :]
        out_ref[row + 2 : row + 4, :] = mixer_ref[0:2, :]
        out_ref[row + 4 : row + 5, :] = ff_ref[2:3, :]
        out_ref[row + 5 : row + 6, :] = mixer_ref[2:3, :]
        out_ref[row + 6 : row + 10, :] = ff_ref[3:7, :]
        out_ref[row + 10 : row + 26, :] = mixer_ref[3:19, :]
        out_ref[row + 26 : row + 90, :] = gout_ref[l]
    put_by_core(at_ref, keep_ref, give_ref, slice(None), out_ref[: PACK // 2], out_ref[PACK // 2 :])


def sds(shape, dtype=F32):
    return jax.ShapeDtypeStruct(shape, dtype)


def params(us, mib=32):
    return dict(
        compiler_params=pltpu.CompilerParams(vmem_limit_bytes=mib * 2**20),
        cost_estimate=pl.CostEstimate(flops=int(us * 1e9), bytes_accessed=10000, transcendentals=0),
    )


SMEM = pl.BlockSpec(memory_space=pltpu.SMEM)
WHOLE = pl.BlockSpec(memory_space=pltpu.VMEM)
ANY = pl.BlockSpec(memory_space=pl.ANY)
SLOTS = pltpu.VMEM((C // 128, T, 128), F32)


def layer_of(x, l):
    rest = x.ndim - 1
    return pl.BlockSpec((1,) + x.shape[1:], lambda *_: (l,) + (0,) * rest, pipeline_mode=pl.Buffered(1))


def fixed(shape):
    return pl.BlockSpec(shape, lambda *_: (0,) * len(shape))


def spectrum_scratch():
    return [pltpu.VMEM((3 * H, C), BF)] * 2 + [pltpu.VMEM((T, C), F32)] * 2


def run_filter_forward(at, first, inner, bias, out):
    layers = out.shape[0]
    return pl.pallas_call(
        filter_forward,
        in_specs=[SMEM] + [WHOLE] * 8,
        out_specs=[WHOLE] * 5,
        out_shape=[
            sds((layers, 4, H, C)), sds((3, T, 128)), sds((3, T, 128)), sds((2, 128, 128)), sds((layers, 128, C)),
        ],
        scratch_shapes=[pltpu.VMEM((128, 128), F32), pltpu.VMEM((8, 128), F32), pltpu.VMEM((T, C), F32)]
        + spectrum_scratch(),
        name="filter_forward",
        **params(12, 8),
    )(at, FEATS, TIMES, first, inner, bias, out, FE, FO)


def run_filter_backward(at, inner, out, sines, cosines, dks):
    return pl.pallas_call(
        filter_backward,
        in_specs=[SMEM] + [WHOLE] * 8,
        out_specs=[WHOLE] * 2,
        out_shape=[sds((2, NET, C)), sds((NET, C))],
        name="filter_backward",
        **params(8, 8),
    )(at, FEATS, TIMES, inner, out, sines, cosines, *dks)


def run_arrange(at, own, other):
    return pl.pallas_call(
        arrange,
        in_specs=[SMEM, WHOLE, WHOLE],
        out_specs=WHOLE,
        out_shape=sds((T, D)),
        scratch_shapes=[SLOTS],
        name="arrange",
        **params(2, 6),
    )(at, own, other)


def run_finish_result(at, x, own, other, vec, l):
    return pl.pallas_call(
        finish_result,
        grid=(1,),
        in_specs=[SMEM, WHOLE, WHOLE, WHOLE, layer_of(vec, l)],
        out_specs=WHOLE,
        out_shape=sds((T, C), BF),
        scratch_shapes=[pltpu.VMEM((T, D), F32), SLOTS],
        name="finish_result",
        **params(3, 8),
    )(at, x, own, other, vec)


def run_finish_grad(at, g, own, other, x, vec, l, after):
    return pl.pallas_call(
        functools.partial(body_without, finish_grad, 6, len(after)),
        grid=(1,),
        in_specs=[SMEM, WHOLE, WHOLE, WHOLE, WHOLE, layer_of(vec, l)] + [ANY] * len(after),
        out_specs=WHOLE,
        out_shape=sds((T, C)),
        scratch_shapes=[pltpu.VMEM((T, D), F32), SLOTS],
        name="finish_grad",
        **params(4, 8),
    )(at, g, own, other, x, vec, *after)


def run_mixer_forward(l, joint, at, x, vec, inw, inb, sw, sb, ks, skip, outw):
    joined = joint is not None
    args = [at, x] + (list(joint) + [vec] if joined else [])
    args += [vec, inw, inb, sw, sb, ks, skip, FE, FO, IE, IO, outw]
    outs = ([sds((T, D))] if joined else []) + [sds((T, 3 * C)), sds((4, H, C)), sds((T, C)), sds((T, D), BF)]
    return pl.pallas_call(
        functools.partial(mixer_forward, l, joined),
        in_specs=[SMEM] + [WHOLE] * (len(args) - 1),
        out_specs=[WHOLE] * len(outs),
        out_shape=outs,
        scratch_shapes=[pltpu.VMEM((T, D), BF), pltpu.VMEM((T, C), F32), pltpu.VMEM((T, C), F32)]
        + spectrum_scratch()
        + [pltpu.VMEM((6 * H, C), BF)] * 2
        + [pltpu.VMEM((T, C), BF)],
        name="mixer_forward",
        **params(11, 10),
    )(*args)


FC = 512


def up_spec(l):
    return pl.BlockSpec((1, D, FC), lambda j: (l, 0, j))


def down_spec(l):
    return pl.BlockSpec((1, FC, D), lambda j: (l, j, 0))


def hidden_spec(rows, width=FC):
    return pl.BlockSpec((rows, width), lambda j: (0, j))


def run_ff_forward(l, last, at, x, own, other, vec, up, upb, dn, after):
    return pl.pallas_call(
        functools.partial(body_without, functools.partial(ff_forward, last), 8, len(after)),
        grid=(FH // FC,),
        in_specs=[
            SMEM, fixed((T, D)), fixed((T, D)), fixed((T, D)), layer_of(vec, l),
            up_spec(l), pl.BlockSpec((1, 1, FC), lambda j: (l, 0, j)), down_spec(l),
        ] + [ANY] * len(after),
        out_specs=[fixed((T, D)), hidden_spec(T)] + ([fixed((T, C))] * 2 if last else [fixed((T, D))]),
        out_shape=[sds((T, D)), sds((T, FH))] + ([sds((T, C), BF)] * 2 if last else [sds((T, D), BF)]),
        scratch_shapes=[pltpu.VMEM((T, D), BF), pltpu.VMEM((T, D), F32)],
        name="ff_forward",
        **params(10, 16),
    )(at, x, own, other, vec, up, upb, dn, *after)


def run_ff_backward(l, at, g, joint, x, h, vec, up, dn, after):
    joined = joint is not None
    args = [at, g] + (list(joint) + [vec] if joined else []) + [x, h, vec, up, dn]
    specs = [SMEM, fixed((T, D))]
    if joined:
        specs += [fixed((T, D))] * 3 + [layer_of(vec, l + 1)]
    specs += [fixed((T, D)), hidden_spec(T), layer_of(vec, l), up_spec(l), down_spec(l)]
    out_specs = [fixed((T, D))] if joined else []
    outs = [sds((T, D))] if joined else []
    out_specs += [fixed((T, WIDE)), fixed((T, WIDE)), fixed((8, C)), fixed((T, D))]
    outs += [sds((T, WIDE), BF), sds((T, WIDE), BF), sds((8, C)), sds((T, D), BF)]
    return pl.pallas_call(
        functools.partial(body_without, functools.partial(ff_backward, joined), len(args), len(after)),
        grid=(FH // FC,),
        in_specs=specs + [ANY] * len(after),
        out_specs=out_specs,
        out_shape=outs,
        scratch_shapes=[pltpu.VMEM((T, D), BF), pltpu.VMEM((T, D), F32), pltpu.VMEM((8, FH), F32)],
        name="ff_backward",
        **params(10, 20),
    )(*args, *after)


def run_ff_weights(at, mine, got):
    return pl.pallas_call(
        ff_weights,
        in_specs=[SMEM, WHOLE, WHOLE],
        out_specs=[WHOLE] * 4,
        out_shape=[sds((4, PIECE, D), BF)] * 4,
        name="ff_weights",
        **params(7, 12),
    )(at, mine, got)


def run_mixer_backward(l, last, at, g_in, own, other, x1, x0, u, qs, g, ks, vec, inw, outw, sw, sb, skip, after):
    args = [at, g_in, own, other, x1, x0, u, qs, g, ks, vec, inw, outw, sw, sb, skip, FE, FO, IE, IO]
    outs = [
        sds((T, D)), sds((24, C)), sds((T, C)), sds((T, D), BF), sds((T, WIDE), BF), sds((T, WIDE), BF),
    ]
    tc = pltpu.VMEM((T, C), F32)
    return pl.pallas_call(
        functools.partial(body_without, functools.partial(mixer_backward, l, last), len(args), len(after)),
        in_specs=[SMEM] + [WHOLE] * (len(args) - 1) + [ANY] * len(after),
        out_specs=[WHOLE] * len(outs),
        out_shape=outs,
        scratch_shapes=[
            pltpu.VMEM((T, D), BF), pltpu.VMEM((T, D), BF), pltpu.VMEM((T, C), BF), pltpu.VMEM((T, 3 * C), BF),
            tc, tc, tc, tc, tc, *spectrum_scratch(),
            pltpu.VMEM((6 * H, 2 * C), BF), pltpu.VMEM((6 * H, 2 * C), BF), pltpu.VMEM((T, 2 * C), F32),
        ],
        name="mixer_backward",
        **params(15, 19),
    )(*args, *after)


def run_mixer_weights(at, mine, got, pack, after):
    rows = PIECE + (16 if pack else 0)
    return pl.pallas_call(
        functools.partial(body_without, functools.partial(mixer_weights, bool(pack)), 3 + len(pack), len(after)),
        in_specs=[SMEM] + [WHOLE] * (2 + len(pack)) + [ANY] * len(after),
        out_specs=[WHOLE] * 4,
        out_shape=[sds((4, rows, C), BF)] * 4,
        name="mixer_weights",
        **params(5, 12),
    )(at, mine, got, *pack, *after)


def run_add(parts, count, after=(), sides=1):
    shape = parts[0].shape[1:] if count > 1 else parts[0].shape
    width = sum(p.shape[-1] for p in parts[:: len(parts) // sides])
    made = pl.pallas_call(
        functools.partial(body_without, functools.partial(add_parts, len(parts), sides), len(parts), len(after)),
        in_specs=[WHOLE] * len(parts) + [ANY] * len(after),
        out_specs=[WHOLE] * count,
        out_shape=[sds(shape[:-1] + (width,), BF)] * count,
        name="add_parts",
        **params(1, 8),
    )(*parts, *after)
    return list(made)


def run_behind(arrays, after):
    count = len(arrays)
    return pl.pallas_call(
        lambda *refs: None,
        in_specs=[ANY] * (count + len(after)),
        out_specs=[ANY] * count,
        out_shape=[sds(x.shape, x.dtype) for x in arrays],
        input_output_aliases={i: i for i in range(count)},
        name="behind",
        **params(1, 4),
    )(*arrays, *after)


def run_place(body, at, ins, into, shapes, out_specs, steps, width, name):
    aliases = {} if into is None else {3: 0, 4: 1}
    into = [] if into is None else list(into)
    return pl.pallas_call(
        functools.partial(body_without, body, 3, len(into)),
        grid=(steps,),
        in_specs=[SMEM] + [lane_block(m.shape, width) for m in ins] + [ANY] * len(into),
        out_specs=out_specs,
        out_shape=[sds(s) for s in shapes],
        scratch_shapes=[pltpu.VMEM((4 * PIECE, width), BF)],
        input_output_aliases=aliases,
        name=name,
        **params(6, 20),
    )(at, *ins, *into)


def lane_block(shape, width):
    last = 0 if shape[-1] == width or width == D else D // width
    return pl.BlockSpec(shape[:-1] + (width,), lambda *_: (0,) * (len(shape) - 1) + (last,))


def body_without(body, first, count, *refs):
    body(*refs[:first], *refs[first + count :])


def run_place_ff(l, layers, at, ins, into):
    specs = [
        pl.BlockSpec((1, D, 4 * PIECE), lambda p: (l, 0, p)),
        pl.BlockSpec((1, 4 * PIECE, D), lambda p: (l, p, 0)),
    ]
    return run_place(place_ff, at, ins, into, [(layers, D, FH), (layers, FH, D)], specs, 4, D, "place_ff")


def run_place_mixer(l, layers, at, ins, into):
    packed = ins[0].shape[-2] > PIECE
    specs = [
        pl.BlockSpec((1, 1, D, C), lambda n: (l, jnp.minimum(n, 2), 0, 0)),
        pl.BlockSpec((1, C, D), lambda n: (l, 0, 0)),
    ] + [fixed((PACK, C))] * packed
    shapes = [(layers, 3, D, C), (layers, C, D)] + [(PACK, C)] * packed
    body = functools.partial(place_mixer, packed)
    return run_place(body, at, ins, into, shapes, specs, 4, C, "place_mixer")


SWAP = [(0, 1), (1, 0)]


def swap(x, axis):
    return lax.ppermute(x, axis, SWAP)


def shift(x, axis, k):
    pairs = []
    for y, x_at, c in np.ndindex(4, 4, 2):
        along_x = (axis == FIRST) == (c == 0)
        to = (y, (x_at + k) % 4) if along_x else ((y + k) % 4, x_at)
        pairs.append(((y * 4 + x_at) * 2 + c, (to[0] * 4 + to[1]) * 2 + c))
    return lax.ppermute(x, ("y", "x", "c"), pairs)


def send_first(blocks):
    return [blocks[0]] + [shift(blocks[k], FIRST, k) for k in range(1, 4)]


def sum_first(*gradients, after=()):
    return run_add([p for came in gradients for p in came], 4, after, len(gradients))


def send_second(pieces):
    return [pieces[0]] + [shift(pieces[m], SECOND, m) for m in range(1, 4)]


def sum_second(came, after=()):
    return run_add(came, 1, after)[0]


def sum_near(piece, after=()):
    return run_add([piece, swap(piece, "zl")], 1, after)[0]


def gather_second(piece):
    return jnp.stack([piece] + [shift(piece, SECOND, m) for m in range(1, 4)])


def gather_first(row):
    return jnp.stack([row] + [shift(row, FIRST, k) for k in range(1, 4)])


def gather_plane(piece, after):
    mine = lax.all_gather(piece, ("y", "x"), axis=0, tiled=False)
    mine = mine.reshape(1, 4, 4, *piece.shape)
    [mine] = run_behind([mine], after)
    return [mine, swap(mine, "c")]


def run_pack_small(at, gnet, gout, small):
    return pl.pallas_call(
        pack_small,
        in_specs=[SMEM] + [WHOLE] * (2 + len(small)),
        out_specs=[WHOLE] * 2,
        out_shape=[sds((PACK // 2, C))] * 2,
        scratch_shapes=[pltpu.VMEM((PACK, C), F32)],
        name="pack_small",
        **params(2, 4),
    )(at, gnet, gout, *small)


def shards(
    tokens, lengths, norm_gain, norm_bias, in_weight, in_bias, short_weight, short_bias, filter_first, filter_inner,
    filter_biases, filter_out, filter_skip, out_weight, out_bias, up_weight, up_bias, down_weight, down_bias, cotangent,
):
    layers = norm_gain.shape[0]
    half_at = lax.axis_index("zh")
    core = lax.axis_index("c")
    x_at, y_at = lax.axis_index("x"), lax.axis_index("y")
    order = jnp.where(core == 0, x_at, y_at), jnp.where(core == 0, y_at, x_at)
    at = jnp.stack([half_at, lengths[0], x_at, y_at, core, *order]).astype(jnp.int32)

    tokens_other = swap(tokens, "zh")
    rows = jnp.stack(
        [norm_gain[:, 0], norm_bias[:, 0], norm_gain[:, 1], norm_bias[:, 1], out_bias, down_bias, out_bias, out_bias], 1
    )
    other = swap(rows, "zh")
    low = half_at == 0
    vec = jnp.concatenate([jnp.where(low, rows, other), jnp.where(low, other, rows)], 2)

    ks, sines, cosines, inner, fout = run_filter_forward(at, filter_first, filter_inner, filter_biases, filter_out)

    x = run_arrange(at, tokens, tokens_other)
    inw = in_weight.transpose(0, 2, 1, 3)
    inb = in_bias.reshape(layers, 1, 3 * C)
    sw = short_weight.reshape(layers, 3, 3 * C)
    sb = short_bias.reshape(layers, 1, 3 * C)
    skip = filter_skip.reshape(layers, 1, C)
    upb = up_bias.reshape(layers, 1, FH)

    cot_other = swap(cotangent, "zh")
    grad = run_arrange(at, cotangent, cot_other)
    saved = []
    joint = None
    for l in range(layers):
        made = run_mixer_forward(l, joint, at, x, vec, inw, inb, sw, sb, ks, skip, out_weight)
        if joint is not None:
            x, made = made[0], made[1:]
        u, qs, g, p = made
        if l == 0:
            [p] = run_behind([p], [cot_other])
        after = [grad] if l == 0 else []
        last = l == layers - 1
        x1, h, *p2 = run_ff_forward(l, last, at, x, p, swap(p, "zh"), vec, up_weight, upb, down_weight, after)
        saved.append((x, u, qs, g, x1, h))
        joint = p2[0], swap(p2[-1], "zh")
        x = x1
    last_branch = joint

    joint = None
    small = [None] * layers
    waits = []
    came = {}
    for l in reversed(range(layers)):
        x0, u, qs, g, x1, h = saved[l]
        made = run_ff_backward(l, at, grad, joint, x1, h, vec, up_weight, down_weight, waits)
        if joint is not None:
            grad, made = made[0], made[1:]
        keep, give, ff_small, p = made
        p, give = run_behind([p, give], [last_branch[1]] if l == layers - 1 else came["mixer", l + 1][1:])
        p_other = swap(p, "zh")
        halves = run_ff_weights(at, keep, swap(give, "c"))
        came["ff", l] = send_first(halves)
        waits = list(halves)
        if l < layers - 1:
            later = send_second(sum_first(came["ff", l + 1], came["mixer", l + 1], after=[p]))
            waits += later[1:]
        made = run_mixer_backward(
            l, l == 0, at, grad, p, p_other, x1, x0, u, qs, g, ks, vec, inw, out_weight, sw, sb, skip, waits
        )
        grad, mixer_small, dk, p, keep, give = made
        p, give = run_behind([p, give], came["ff", l][1:])
        joint = (p, swap(p, "zh"), x0)
        small[l] = (ff_small, mixer_small, dk)
        pack = ()
        if l == 0:
            gfout, gnet = run_filter_backward(at, inner, fout, sines, cosines, [s[-1] for s in small])
            pack = run_pack_small(at, gnet, gfout, [m for some in small for m in some[:-1]])
            pack = pack[0], swap(pack[1], "c")
            later = sum_near(sum_second(later, [p]), [gnet])
            ff = send_second(sum_first(came["ff", 0]))
        halves = run_mixer_weights(at, keep, swap(give, "c"), pack, [] if l else ff[1:])
        came["mixer", l] = send_first(halves)
        waits = list(halves)
        if l == layers - 1:
            result = run_finish_result(at, saved[l][4], *last_branch, vec, l)
            waits.append(result)

    ff = sum_near(sum_second(ff, came["mixer", 0][:1]))
    mixer = sum_second(send_second(sum_first(came["mixer", 0], after=[ff])))
    [ff] = run_behind([ff], [mixer])
    ff = gather_second(ff)
    mixer = gather_first(gather_second(sum_near(mixer, [ff])))
    later = gather_plane(later, [mixer])
    mixer_out = run_place_mixer(1, layers, at, later, None)
    *mixer_out, pack = run_place_mixer(0, layers, at, [mixer, swap(mixer, "c")], mixer_out)
    ff_out = run_place_ff(1, layers, at, later, None)
    grad = run_finish_grad(at, grad, *joint, vec, 0, [ff_out[0], mixer_out[0]])
    [ff] = run_behind([ff], [mixer])
    ff = gather_first(ff)
    ff_out = run_place_ff(0, layers, at, [ff, swap(ff, "c")], ff_out)

    net = pack[:SHARED]
    net = net + swap(net, "zh")
    pack = pack[SHARED:].reshape(layers, -1, C)
    first_norm = jnp.where(low, net[NET : NET + 4 : 2], net[NET + 1 : NET + 4 : 2])
    norm_rows = jnp.stack([jnp.concatenate([first_norm, pack[0, 2:4]]), pack[1, :4]])

    def apart(a):
        return jnp.stack([a[..., :NET], a[..., NET:]])

    return (
        result,
        grad,
        norm_rows[:, 0:4:2],
        norm_rows[:, 1:4:2],
        mixer_out[0].transpose(0, 2, 1, 3),
        pack[:, 10:13],
        pack[:, 13:22].reshape(short_weight.shape),
        pack[:, 22:25],
        apart(net[:EMB, 256:]),
        jnp.stack([apart(net[:NET, :128]), apart(net[:NET, 128:256])], 1),
        apart(net[40:43, 256:]),
        pack[:, 26:90],
        pack[:, 25],
        mixer_out[1],
        pack[:, 5],
        ff_out[0],
        pack[:, 6:10].reshape(layers, FH),
        ff_out[1],
        pack[:, 4],
    )


def solution(mesh):
    names = ("zl", "y", "x", "c", "zh")
    fine = Mesh(mesh.devices.reshape(2, 4, 4, 2, 2), names)
    dp = ("zl", "y", "x", "c")
    rows = P(dp, "zh")
    third, fourth = P(None, None, "zh"), P(None, None, None, "zh")
    second, middle = P(None, "zh"), P(None, "zh", None)
    placed = (
        rows, P(dp), third, third, fourth, third, fourth, third, P(), P(), P(), third, second, middle, second, third,
        second, middle, second, rows,
    )
    return jax.shard_map(
        shards,
        mesh=fine,
        in_specs=placed,
        out_specs=(
            rows, rows, third, third, fourth, third, fourth, third, P(), P(), P(), third, second, middle, second, third,
            second, middle, second,
        ),
        check_vma=False,
    )
```

```python
import functools
import math

import jax
import jax.numpy as jnp
import ml_dtypes
import numpy as np
from jax import lax
from jax.experimental import pallas as pl
from jax.experimental.pallas import tpu as pltpu
from jax.sharding import Mesh
from jax.sharding import PartitionSpec as P

D = 768
T = 512
H = T // 2
C = 384
FH = 1536
NET = 64
EMB = 33
BANDS = 16
PIECE = 96
EPSILON = 1e-05
HIGH = lax.Precision.HIGHEST
F32 = jnp.float32
BF = jnp.bfloat16

ORDER = np.concatenate([np.arange(0, T, 2), np.arange(1, T, 2)])


def split_table(t):
    hi = t.astype(ml_dtypes.bfloat16)
    lo = (t - hi.astype(np.float64)).astype(ml_dtypes.bfloat16)
    return hi, lo


def wave_tables():
    n = np.arange(H)
    even = 2 * math.pi * (np.outer(n, 2 * n) % (2 * T)) / (2 * T)
    odd = 2 * math.pi * (np.outer(n, 2 * n + 1) % (2 * T)) / (2 * T)
    alt = np.where(n % 2 == 0, 1.0, -1.0)
    out = []
    for ang in (even, odd):
        co, si = np.cos(ang), np.sin(ang)
        si[0] = alt
        hi, lo = split_table(np.concatenate([co, si], 0))
        out.append(np.concatenate([hi, lo, hi], 1))
        hi, lo = split_table(np.concatenate([co.T, si.T], 1))
        out.append(np.concatenate([hi, lo, hi], 1))
    fe, ie, fo, io = out
    return np.concatenate([fe, fo, np.concatenate([ie, io], 0)], 1)


TABLE = wave_tables()
FORWARD_EVEN = slice(None), slice(0, 3 * H)
FORWARD_ODD = slice(None), slice(3 * H, 6 * H)
INVERSE_EVEN = slice(0, H), slice(6 * H, 12 * H)
INVERSE_ODD = slice(H, 2 * H), slice(6 * H, 12 * H)


def slot_features():
    slots = ORDER.astype(np.float64)
    freqs = 0.0001 + (BANDS - 1 - 0.0001) * np.arange(BANDS) / (BANDS - 1)
    angle = 2 * math.pi * slots[:, None] * freqs[None, :] / T
    times = (slots / (T - 1))[:, None]
    feats = np.concatenate([times, np.cos(angle), -np.sin(angle), np.zeros((T, 128 - EMB))], 1)
    return feats.astype(np.float32)


FEATS = slot_features()


def dot(a, b):
    return lax.dot_general(a, b, (((1,), (0,)), ((), ())), preferred_element_type=F32)


def dot_nt(a, b):
    return lax.dot_general(a, b, (((1,), (1,)), ((), ())), preferred_element_type=F32)


def dot_tn(a, b):
    return lax.dot_general(a, b, (((0,), (0,)), ((), ())), preferred_element_type=F32)


def normalize(x):
    mean = jnp.mean(x, -1, keepdims=True)
    scale = lax.rsqrt(jnp.mean(x * x, -1, keepdims=True) - mean * mean + EPSILON)
    return (x - mean) * scale, scale


def norm_pull(dn, x, gain):
    xhat, scale = normalize(x)
    ds = dn * gain
    first = jnp.mean(ds, -1, keepdims=True)
    second = jnp.mean(ds * xhat, -1, keepdims=True)
    return scale * (ds - first - xhat * second), dn * xhat


def row_mask(start, rows, length):
    r = start + lax.broadcasted_iota(jnp.int32, (rows, 1), 0)
    slot = jnp.where(r < H, 2 * r, 2 * (r - H) + 1)
    return (slot < length).astype(F32)


def down_one(x):
    r = lax.broadcasted_iota(jnp.int32, x.shape, 0)
    return jnp.where(r == 0, 0.0, pltpu.roll(x, 1, 0))


def up_one(x):
    r = lax.broadcasted_iota(jnp.int32, x.shape, 0)
    return jnp.where(r == x.shape[0] - 1, 0.0, pltpu.roll(x, x.shape[0] - 1, 0))


def put_split(ref, value, rows, lanes):
    hi = value.astype(BF)
    lo = (value - hi.astype(F32)).astype(BF)
    step = ref.shape[0] // 3
    ref[pl.ds(rows, value.shape[0]), lanes] = hi
    ref[pl.ds(step + rows, value.shape[0]), lanes] = hi
    ref[pl.ds(2 * step + rows, value.shape[0]), lanes] = lo


def top_row(shape):
    return lax.broadcasted_iota(jnp.int32, shape, 0) == 0


def butterfly(even, odd, lanes):
    ce, se = even[pl.ds(0, H), lanes], even[pl.ds(H, H), lanes]
    co, so = odd[pl.ds(0, H), lanes], odd[pl.ds(H, H), lanes]
    top = top_row(ce.shape)
    return ce + co, ce - co, jnp.where(top, se, se + so), jnp.where(top, so, se - so)


def spectrum_product(a, k, conj):
    a1, a2, b1, b2 = a
    k1, k2, l1, l2 = k
    top = top_row(a1.shape)
    aa, bb, cc, dd = a1 * k1, b1 * l1, a2 * k2, b2 * l2
    if conj:
        y1 = jnp.where(top, aa, aa + bb)
        y2 = jnp.where(top, cc, cc + dd)
        m1 = jnp.where(top, bb + dd, b1 * k1 - a1 * l1)
        m2 = jnp.where(top, b2 * l1 - b1 * l2, b2 * k2 - a2 * l2)
    else:
        y1 = jnp.where(top, aa, aa - bb)
        y2 = jnp.where(top, cc, cc - dd)
        m1 = jnp.where(top, bb - dd, a1 * l1 + b1 * k1)
        m2 = jnp.where(top, b1 * l2 + b2 * l1, a2 * l2 + b2 * k2)
    return y1, y2, m1, m2


def put_inverse(rhs_e, rhs_o, y, lanes):
    y1, y2, m1, m2 = y
    top = top_row(y1.shape)
    unit = 1.0 / T
    w = jnp.where(top, 0.5 * unit, unit)
    put_split(rhs_e, (y1 + y2) * w, 0, lanes)
    put_split(rhs_o, (y1 - y2) * w, 0, lanes)
    put_split(rhs_e, jnp.where(top, m1, m1 + m2) * unit, H, lanes)
    put_split(rhs_o, jnp.where(top, m2, m1 - m2) * unit, H, lanes)


def lanes_of(block):
    return pl.ds(block * 128, 128)


def short_conv(u_ref, sw_ref, sb_ref, block):
    out = []
    for s in range(3):
        at = lanes_of(s * (C // 128) + block)
        ue, uo = u_ref[pl.ds(0, H), at], u_ref[pl.ds(H, H), at]
        t0, t1, t2 = (sw_ref[j : j + 1, at] for j in range(3))
        bias = sb_ref[0:1, at]
        uo_d = down_one(uo)
        we = t2 * ue + t1 * uo_d + t0 * down_one(ue) + bias
        wo = t2 * uo + t1 * ue + t0 * uo_d + bias
        out.append((we, wo))
    return out


def hdot(a, b, dims=(1, 0)):
    return lax.dot_general(
        a, b, (((dims[0],), (dims[1],)), ((), ())), precision=HIGH, preferred_element_type=F32
    )


def decay_of(half_at, feats_ref):
    slow = math.log(0.01) / 1.5
    fast = math.log(0.01) / 0.3
    channel = (half_at * C + lax.broadcasted_iota(jnp.int32, (1, C), 1)).astype(F32)
    rates = jnp.abs(slow + (fast - slow) * channel / (D - 1))
    return jnp.exp(-feats_ref[:, 0:1] * rates) + 0.05


def sin_cos(x):
    k = jnp.floor(x * (2 / math.pi) + 0.5)
    r = ((x - k * 1.5703125) - k * 4.837512969970703125e-4) - k * 7.54978995489188e-8
    rr = r * r
    sine = r + r * rr * (-1.6666654611e-1 + rr * (8.3321608736e-3 + rr * -1.9515295891e-4))
    cosine = 1.0 - 0.5 * rr + rr * rr * (
        4.166664568298827e-2 + rr * (-1.388731625493765e-3 + rr * 2.443315711809948e-5)
    )
    quarter = k - 4.0 * jnp.floor(k * 0.25)
    odd = (quarter == 1.0) | (quarter == 3.0)
    s = jnp.where(odd, cosine, sine)
    c = jnp.where(odd, sine, cosine)
    return jnp.where(quarter >= 2.0, -s, s), jnp.where((quarter == 1.0) | (quarter == 2.0), -c, c)


def filter_forward(
    at_ref, feats_ref, first_ref, inner_ref, bias_ref, out_ref, table_ref,
    ks_ref, sin_ref, cos_ref, both_ref, wide_ref, first_s, bias_s, k_s, rhs_e, rhs_o, se, so,
):
    for ref in (both_ref, wide_ref, first_s, bias_s):
        ref[...] = jnp.zeros_like(ref)
    for l in range(2):
        at = pl.ds(l * NET, NET)
        first_s[0:EMB, at] = first_ref[l]
        bias_s[0:3, at] = bias_ref[l]
        wide_ref[l, at, :] = out_ref[l]
        for i in range(2):
            both_ref[i, at, at] = inner_ref[l, i]
    low = feats_ref[...]
    for i in range(3):
        weight = first_s[...] if i == 0 else both_ref[i - 1]
        low, cosine = sin_cos(hdot(low, weight) + bias_s[i : i + 1, :])
        sin_ref[i] = low
        cos_ref[i] = cosine
    decay = decay_of(at_ref[0], feats_ref)
    for l in range(2):
        k_s[...] = hdot(sin_ref[2], wide_ref[l]) * decay
        for b in range(C // 128):
            at = lanes_of(b)
            put_split(rhs_e, k_s[pl.ds(0, H), at], 0, at)
            put_split(rhs_o, k_s[pl.ds(H, H), at], 0, at)
        se[...] = dot(table_ref[FORWARD_EVEN], rhs_e[...])
        so[...] = dot(table_ref[FORWARD_ODD], rhs_o[...])
        for b in range(C // 128):
            at = lanes_of(b)
            for i, v in enumerate(butterfly(se, so, at)):
                ks_ref[l, i, :, at] = v


def filter_backward(at_ref, feats_ref, inner_ref, out_ref, sin_ref, cos_ref, dk0_ref, dk1_ref, gout_ref, gnet_ref):
    decay = decay_of(at_ref[0], feats_ref)
    ds = jnp.zeros((T, 128), F32)
    for l, dk_ref in enumerate((dk0_ref, dk1_ref)):
        dk = dk_ref[...] * decay
        gout_ref[l] = hdot(sin_ref[2], dk, (0, 0))[l * NET : (l + 1) * NET]
        ds += hdot(dk, out_ref[l], (1, 1))
    lane = lax.broadcasted_iota(jnp.int32, (NET, 128), 1)
    gnet_ref[...] = jnp.zeros_like(gnet_ref)
    for i in (2, 1, 0):
        da = ds * cos_ref[i]
        gnet_ref[40 + i : 41 + i, pl.ds(256, 128)] = jnp.sum(da, 0, keepdims=True)
        if i > 0:
            block = hdot(sin_ref[i - 1], da, (0, 0))
            gnet_ref[:, pl.ds((i - 1) * 128, 128)] = jnp.where(lane < NET, block[:NET], block[NET:])
            ds = hdot(da, inner_ref[i - 1], (1, 1))
        else:
            gnet_ref[0:40, pl.ds(256, 128)] = hdot(feats_ref[...], da, (0, 0))[0:40]


def arrange(at_ref, own_ref, other_ref, out_ref, tmp):
    for half, first in ((0, own_ref), (1, other_ref)):
        for b in range(C // 128):
            tmp[b] = first[:, lanes_of(b)].astype(F32)

        def put(first_lane):
            for b in range(C // 128):
                to = pl.ds(first_lane + b * 128, 128)
                out_ref[pl.ds(0, H), to] = tmp[b, pl.ds(0, H, stride=2), :]
                out_ref[pl.ds(H, H), to] = tmp[b, pl.ds(1, H, stride=2), :]

        pl.when(at_ref[0] == half)(functools.partial(put, 0))
        pl.when(at_ref[0] != half)(functools.partial(put, C))


def my_lanes(at_ref, row):
    return jnp.where(at_ref[0] == 0, row[:, :C], row[:, C:])


def by_slot(at_ref, src_ref, out_ref, tmp):
    def put(first_lane):
        for b in range(C // 128):
            lanes = pl.ds(first_lane + b * 128, 128)
            tmp[b, pl.ds(0, H, stride=2), :] = src_ref[pl.ds(0, H), lanes]
            tmp[b, pl.ds(1, H, stride=2), :] = src_ref[pl.ds(H, H), lanes]

    pl.when(at_ref[0] == 0)(functools.partial(put, 0))
    pl.when(at_ref[0] != 0)(functools.partial(put, C))
    for b in range(C // 128):
        out_ref[:, lanes_of(b)] = tmp[b].astype(out_ref.dtype)


def finish_result(at_ref, x_ref, own_ref, other_ref, vec_ref, out_ref, y_s, tmp):
    def put(first_lane):
        lanes = pl.ds(first_lane, C)

        def body(start, c):
            rows = pl.ds(start, RB)
            y = own_ref[rows, :].astype(F32) + other_ref[rows, :].astype(F32) + vec_ref[0, 5:6, lanes]
            y_s[rows, lanes] = x_ref[rows, lanes] + row_mask(start, RB, at_ref[1]) * y
            return c

        row_loop(body)

    pl.when(at_ref[0] == 0)(functools.partial(put, 0))
    pl.when(at_ref[0] != 0)(functools.partial(put, C))
    by_slot(at_ref, y_s, out_ref, tmp)


def finish_grad(at_ref, g_ref, own_ref, other_ref, x_ref, vec_ref, out_ref, x_s, tmp):
    def body(start, c):
        at = pl.ds(start, RB)
        dn = own_ref[at, :].astype(F32) + other_ref[at, :].astype(F32)
        x_s[at, :] = g_ref[at, :] + norm_pull(dn, x_ref[at, :], vec_ref[0, 0:1, :])[0]
        return c

    row_loop(body)
    by_slot(at_ref, x_s, out_ref, tmp)


def add_branch(x_ref, own_ref, other_ref, vec_ref, row, length, start, rows):
    at = pl.ds(start, rows)
    y = own_ref[at, :].astype(F32) + other_ref[at, :].astype(F32) + vec_ref[row : row + 1, :]
    return x_ref[at, :] + row_mask(start, rows, length) * y


RB = 128


def row_loop(body, init=0):
    def step(i, c):
        return body(pl.multiple_of(i * RB, RB), c)

    return lax.fori_loop(0, T // RB, step, init)


def mixer_forward(l, joined, *refs):
    at_ref, x_ref = refs[:2]
    refs = refs[2:]
    if joined:
        own_ref, other_ref, prev_ref = refs[:3]
        refs = refs[3:]
    (vec_ref, inw_ref, inb_ref, sw_ref, sb_ref, ks_ref, skip_ref, table_ref, outw_ref) = refs[:9]
    refs = refs[9:]
    if joined:
        xo_ref = refs[0]
        refs = refs[1:]
    u_ref, qs_ref, g_ref, p_ref, a_s, w0_s, q_s, rhs_e, rhs_o, se, so, rhs2_e, rhs2_o, z_s = refs

    def first(start, c):
        at = pl.ds(start, RB)
        if joined:
            x = add_branch(x_ref, own_ref, other_ref, prev_ref.at[l - 1], 5, at_ref[1], start, RB)
            xo_ref[at, :] = x
        else:
            x = x_ref[at, :]
        xhat, _ = normalize(x)
        a_s[at, :] = (xhat * vec_ref[l, 0:1, :] + vec_ref[l, 1:2, :]).astype(BF)
        return c

    row_loop(first)
    for s in range(3):
        at = pl.ds(s * C, C)
        u_ref[:, at] = dot(a_s[...], inw_ref[l, s]) + inb_ref[l, 0:1, at]
    for b in range(C // 128):
        at = lanes_of(b)
        (w0e, w0o), (w1e, w1o), (w2e, w2o) = short_conv(u_ref, sw_ref.at[l], sb_ref.at[l], b)
        w0_s[pl.ds(0, H), at] = w0e
        w0_s[pl.ds(H, H), at] = w0o
        qe, qo = w2e * w1e, w2o * w1o
        q_s[pl.ds(0, H), at] = qe
        q_s[pl.ds(H, H), at] = qo
        put_split(rhs_e, qe, 0, at)
        put_split(rhs_o, qo, 0, at)
    se[...] = dot(table_ref[FORWARD_EVEN], rhs_e[...])
    so[...] = dot(table_ref[FORWARD_ODD], rhs_o[...])
    for b in range(C // 128):
        at = lanes_of(b)
        spec = butterfly(se, so, at)
        for i, v in enumerate(spec):
            qs_ref[i, :, at] = v
        y = spectrum_product(spec, [ks_ref[l, i, :, at] for i in range(4)], False)
        put_inverse(rhs2_e, rhs2_o, y, at)
    se[pl.ds(0, H), :] = dot(table_ref[INVERSE_EVEN], rhs2_e[...])
    se[pl.ds(H, H), :] = dot(table_ref[INVERSE_ODD], rhs2_o[...])

    def last(start, c):
        at = pl.ds(start, RB)
        g = se[at, :] + skip_ref[l, 0:1, :] * q_s[at, :]
        g_ref[at, :] = g
        z_s[at, :] = (g * w0_s[at, :]).astype(BF)
        return c

    row_loop(last)
    p_ref[...] = dot(z_s[...], outw_ref[l]).astype(BF)


def gelu_parts(h):
    c0 = math.sqrt(2 / math.pi)
    hh = h * h
    t = jnp.tanh(c0 * (h + 0.044715 * (hh * h)))
    half = 0.5 * (1.0 + t)
    return half, t, hh, c0


def collect(j, acc, part):
    @pl.when(j == 0)
    def _():
        acc[...] = part

    @pl.when(j > 0)
    def _():
        acc[...] += part


def ff_forward(last, at_ref, x_ref, own_ref, other_ref, vec_ref, up_ref, upb_ref, dn_ref, xo_ref, h_ref, *refs):
    *p_refs, b_s, acc = refs
    j = pl.program_id(0)

    @pl.when(j == 0)
    def _():
        def first(start, c):
            at = pl.ds(start, RB)
            x = add_branch(x_ref, own_ref, other_ref, vec_ref.at[0], 4, at_ref[1], start, RB)
            xo_ref[at, :] = x
            xhat, _ = normalize(x)
            b_s[at, :] = (xhat * vec_ref[0, 2:3, :] + vec_ref[0, 3:4, :]).astype(BF)
            return c

        row_loop(first)

    h = dot(b_s[...], up_ref[0]) + upb_ref[0]
    h_ref[...] = h
    half, _, _, _ = gelu_parts(h)
    collect(j, acc, dot((h * half).astype(BF), dn_ref[0]))

    @pl.when(j == pl.num_programs(0) - 1)
    def _():
        if not last:
            p_refs[0][...] = acc[...].astype(BF)
        else:
            low, high = acc[:, :C].astype(BF), acc[:, C:].astype(BF)
            own = at_ref[0] == 0
            p_refs[0][...] = jnp.where(own, low, high)
            p_refs[1][...] = jnp.where(own, high, low)


def put_by_core(at_ref, keep_ref, give_ref, at, low, high):
    @pl.when(at_ref[4] == 0)
    def _():
        keep_ref[at] = low
        give_ref[at] = high

    @pl.when(at_ref[4] != 0)
    def _():
        keep_ref[at] = high
        give_ref[at] = low


def ff_backward(joined, *refs):
    at_ref, g_ref = refs[:2]
    refs = refs[2:]
    if joined:
        own_ref, other_ref, xn_ref, nvec_ref = refs[:4]
        refs = refs[4:]
    x_ref, h_ref, vec_ref, up_ref, dn_ref = refs[:5]
    refs = refs[5:]
    if joined:
        go_ref, refs = refs[0], refs[1:]
    keep_ref, give_ref, small_ref, p_ref, dm_s, acc, upb_s = refs
    j = pl.program_id(0)

    @pl.when(j == 0)
    def _():
        def first(start, c):
            at = pl.ds(start, RB)
            g = g_ref[at, :]
            sums, s1, s2 = c
            if joined:
                dn = own_ref[at, :].astype(F32) + other_ref[at, :].astype(F32)
                dx, dg = norm_pull(dn, xn_ref[at, :], nvec_ref[0, 0:1, :])
                g = g + dx
                go_ref[at, :] = g
                s1 = s1 + jnp.sum(dg, 0, keepdims=True)
                s2 = s2 + jnp.sum(dn, 0, keepdims=True)
            dm = (row_mask(start, RB, at_ref[1]) * g).astype(BF)
            dm_s[at, :] = dm
            xhat, _ = normalize(x_ref[at, :])
            b = (xhat * vec_ref[0, 2:3, :] + vec_ref[0, 3:4, :]).astype(BF)
            put_by_core(at_ref, keep_ref, give_ref, (at, pl.ds(0, D)), dm, b)
            return sums + jnp.sum(dm.astype(F32), 0, keepdims=True), s1, s2

        zero = jnp.zeros((1, D), F32)
        sums, s1, s2 = row_loop(first, (zero, zero, zero))
        small_ref[...] = jnp.zeros_like(small_ref)
        for i, row in enumerate((s1, s2, sums)):
            small_ref[i : i + 1, :] = my_lanes(at_ref, row)

    h = h_ref[...]
    half, t, hh, c0 = gelu_parts(h)
    e = (h * half).astype(BF)
    slope = half + 0.5 * c0 * h * (1.0 - t * t) * (1.0 + 3 * 0.044715 * hh)
    dh = (dot_nt(dm_s[...], dn_ref[0]) * slope).astype(BF)
    put_by_core(at_ref, keep_ref, give_ref, (slice(None), pl.ds(pl.multiple_of(D + j * FC, 128), FC)), e, dh)
    upb_s[0:1, pl.ds(pl.multiple_of(j * FC, 128), FC)] = jnp.sum(dh.astype(F32), 0, keepdims=True)
    collect(j, acc, dot_nt(dh, up_ref[0]))

    @pl.when(j == pl.num_programs(0) - 1)
    def _():
        p_ref[...] = acc[...].astype(BF)
        for i in range(4):
            small_ref[3 + i : 4 + i, :] = upb_s[0:1, i * C : (i + 1) * C]


FIRST, SECOND = 5, 6
WIDE = 3 * D


class Swapped:
    def __init__(self, at_ref):
        self.at_ref = at_ref

    def __getitem__(self, i):
        return self.at_ref[{FIRST: SECOND, SECOND: FIRST}.get(i, i)]


def put_pieces(at_ref, ref, value):
    for n in range(4):
        ref[lax.rem(n - at_ref[SECOND] + 4, 4), pl.ds(0, PIECE)] = value[n * PIECE : (n + 1) * PIECE]


def ff_weights(at_ref, mine_ref, got_ref, *outs):
    for k, out_ref in enumerate(outs):
        block = lax.rem(at_ref[FIRST] + k, 4)
        lanes = pl.ds(pl.multiple_of(D + block * 4 * PIECE, 128), 4 * PIECE)
        total = sum(dot_tn(ref[:, lanes], ref[:, pl.ds(0, D)]) for ref in (mine_ref, got_ref))
        put_pieces(at_ref, out_ref, total.astype(BF))


def mixer_backward(
    l, last, at_ref, g_in_ref, own_ref, other_ref, x1_ref, x0_ref, u_ref, qs_ref, g_ref, ks_ref, vec_ref, inw_ref, outw_ref,
    sw_ref, sb_ref, skip_ref, table_ref,
    go_ref, small_ref, dk_ref, p_ref, keep_ref, give_ref, dy_ref, a_ref, z_ref, du_ref, dz_s, dg_s, w1_s, w2_s, dw0_s, rhs_e, rhs_o, se, so, rhs2_e, rhs2_o, inv_s,
):
    small_ref[...] = jnp.zeros_like(small_ref)

    def first(start, c):
        at = pl.ds(start, RB)
        sums, s1, s2 = c
        dn = own_ref[at, :].astype(F32) + other_ref[at, :].astype(F32)
        dx, dg = norm_pull(dn, x1_ref[at, :], vec_ref[l, 2:3, :])
        g = g_in_ref[at, :] + dx
        go_ref[at, :] = g
        dy = (row_mask(start, RB, at_ref[1]) * g).astype(BF)
        dy_ref[at, :] = dy
        xhat, _ = normalize(x0_ref[at, :])
        a_ref[at, :] = (xhat * vec_ref[l, 0:1, :] + vec_ref[l, 1:2, :]).astype(BF)
        return (
            sums + jnp.sum(dy.astype(F32), 0, keepdims=True),
            s1 + jnp.sum(dg, 0, keepdims=True),
            s2 + jnp.sum(dn, 0, keepdims=True),
        )

    zero = jnp.zeros((1, D), F32)
    sums, s1, s2 = row_loop(first, (zero, zero, zero))
    for i, row in enumerate((s1, s2, sums)):
        small_ref[i : i + 1, :] = my_lanes(at_ref, row)
    dz_s[...] = dot_nt(dy_ref[...], outw_ref[l])
    halves = (pl.ds(0, H), pl.ds(H, H))
    for b in range(C // 128):
        at = lanes_of(b)
        w0, w1, w2 = short_conv(u_ref, sw_ref.at[l], sb_ref.at[l], b)
        dskip = 0.0
        for i, (rows, rhs) in enumerate(zip(halves, (rhs_e, rhs_o))):
            dz, g = dz_s[rows, at], g_ref[rows, at]
            z_ref[rows, at] = (g * w0[i]).astype(BF)
            dw0_s[rows, at] = dz * g
            dg = dz * w0[i]
            dg_s[rows, at] = dg
            dskip = dskip + jnp.sum(dg * (w2[i] * w1[i]), 0, keepdims=True)
            w1_s[rows, at] = w1[i]
            w2_s[rows, at] = w2[i]
            put_split(rhs, dg, 0, at)
        small_ref[18:19, at] = dskip
    se[...] = dot(table_ref[FORWARD_EVEN], rhs_e[...])
    so[...] = dot(table_ref[FORWARD_ODD], rhs_o[...])
    for b in range(C // 128):
        at = lanes_of(b)
        spec = butterfly(se, so, at)
        put_inverse(rhs2_e, rhs2_o, spectrum_product(spec, [ks_ref[l, i, :, at] for i in range(4)], True), at)
        put_inverse(
            rhs2_e, rhs2_o, spectrum_product(spec, [qs_ref[i, :, at] for i in range(4)], True), pl.ds(C + b * 128, 128)
        )
    inv_s[pl.ds(0, H), :] = dot(table_ref[INVERSE_EVEN], rhs2_e[...])
    inv_s[pl.ds(H, H), :] = dot(table_ref[INVERSE_ODD], rhs2_o[...])
    dk_ref[...] = inv_s[:, pl.ds(C, C)]
    for b in range(C // 128):
        at = lanes_of(b)
        dw = [[dw0_s[rows, at] for rows in halves], [], []]
        for rows in halves:
            dq = inv_s[rows, at] + skip_ref[l, 0:1, at] * dg_s[rows, at]
            dw[1].append(dq * w2_s[rows, at])
            dw[2].append(dq * w1_s[rows, at])
        for s in range(3):
            to = lanes_of(s * (C // 128) + b)
            ue, uo = u_ref[halves[0], to], u_ref[halves[1], to]
            t0, t1, t2 = (sw_ref[l, j : j + 1, to] for j in range(3))
            de, do = dw[s]
            de_u, do_u = up_one(de), up_one(do)
            due = (t2 * de + t1 * do + t0 * de_u).astype(BF)
            duo = (t2 * do + t1 * de_u + t0 * do_u).astype(BF)
            du_ref[halves[0], to] = due
            du_ref[halves[1], to] = duo
            uo_d = down_one(uo)
            small_ref[3 + s : 4 + s, at] = jnp.sum(due.astype(F32) + duo.astype(F32), 0, keepdims=True)
            taps = de * down_one(ue) + do * uo_d, de * uo_d + do * ue, de * ue + do * uo
            for j, tap in enumerate(taps):
                small_ref[6 + 3 * j + s : 7 + 3 * j + s, at] = jnp.sum(tap, 0, keepdims=True)
            small_ref[15 + s : 16 + s, at] = jnp.sum(de + do, 0, keepdims=True)
    part = dot_nt(du_ref[:, pl.ds(0, C)], inw_ref[l, 0])
    for s in range(1, 3):
        part += dot_nt(du_ref[:, pl.ds(s * C, C)], inw_ref[l, s])
    p_ref[...] = part.astype(BF)

    def spread(start, c):
        rows = pl.ds(start, RB)
        a, dy, z = a_ref[rows, :], dy_ref[rows, :], z_ref[rows, :]
        du = [du_ref[rows, pl.ds(s * C, C)] for s in range(3)]
        lane = 0
        for low, high in ((a, a), (du[0], du[2]), (a, dy), (du[1], z)):
            put_by_core(at_ref, keep_ref, give_ref, (rows, pl.ds(lane, low.shape[1])), low, high)
            lane += low.shape[1]
        return c

    row_loop(spread)
    if last:

        def terms(start, c):
            at = pl.ds(start, RB)
            dn = p_ref[at, :].astype(F32)
            xhat, _ = normalize(x0_ref[at, :])
            return c[0] + jnp.sum(dn * xhat, 0, keepdims=True), c[1] + jnp.sum(dn, 0, keepdims=True)

        s1, s2 = row_loop(terms, (zero, zero))
        for i, row in enumerate((s1, s2)):
            for half in range(2):
                small_ref[20 + 2 * i + half : 21 + 2 * i + half, :] = row[:, half * C : (half + 1) * C]


def put_split_rows(value):
    hi = value.astype(BF).astype(F32)
    return jnp.concatenate([hi, value - hi], 0).astype(BF)


def mixer_weights(packed, at_ref, mine_ref, got_ref, *refs):
    if packed:
        pack_refs, refs = refs[:2], refs[2:]
    for k, out_ref in enumerate(refs):
        block = lax.rem(at_ref[FIRST] + k, 4)
        left = pl.multiple_of(jnp.where(block < 2, block, block + 1) * C, 128)
        right = pl.multiple_of(jnp.where(block < 2, D, 2 * D + C), 128)
        total = sum(dot_tn(ref[:, pl.ds(left, C)], ref[:, pl.ds(right, C)]) for ref in (mine_ref, got_ref))
        put_pieces(at_ref, out_ref, total.astype(BF))
        if packed:
            for n in range(4):
                rows = pl.ds(pl.multiple_of(block * 32 + n * 8, 8), 8)
                value = pack_refs[0][rows, :] + pack_refs[1][rows, :]
                out_ref[lax.rem(n - at_ref[SECOND] + 4, 4), pl.ds(PIECE, 16)] = put_split_rows(value)


def add_parts(count, sides, *refs):
    ins, outs = refs[:count], refs[count:]
    lane = 0
    for side in range(sides):
        some = ins[side * count // sides : (side + 1) * count // sides]
        lanes = slice(lane, lane + some[0].shape[-1])
        lane = lanes.stop
        for i, out in enumerate(outs):
            total = functools.reduce(jnp.add, [(r[i] if len(outs) > 1 else r[...]).astype(F32) for r in some])
            rows = (slice(None),) * (total.ndim - 2)
            out[rows + (slice(0, PIECE), lanes)] = total[rows + (slice(0, PIECE),)].astype(BF)
            if total.shape[-2] > PIECE:
                for n in range(total.shape[0] if total.ndim > 2 else 1):
                    value = total[n] if total.ndim > 2 else total
                    value = value[PIECE : PIECE + 8] + value[PIECE + 8 : PIECE + 16]
                    to = (n, slice(PIECE, PIECE + 16)) if total.ndim > 2 else slice(PIECE, PIECE + 16)
                    out[to] = put_split_rows(value)


def gather_block(at_ref, ref, block, tmp, pack_ref=None, first=0):
    for m in range(4):
        if len(ref.shape) == 5:
            by_x = (at_ref[4] == 0) != isinstance(at_ref, Swapped)
            at = 0, jnp.where(by_x, m, block), jnp.where(by_x, block, m)
        else:
            at = lax.rem(at_ref[FIRST] - block + 4, 4), lax.rem(at_ref[SECOND] - m + 4, 4)
        tmp[pl.ds(m * PIECE, PIECE), :] = ref[at + (slice(0, PIECE),)].astype(tmp.dtype)
        if pack_ref is not None:
            extra = ref[at + (slice(PIECE, PIECE + 16),)].astype(F32)
            pack_ref[pl.ds(pl.multiple_of(first + m * 8, 8), 8), :] = extra[:8] + extra[8:]


def gather_half(at_ref, half, refs, *args):
    own = at_ref[4] == half
    pl.when(own)(lambda: gather_block(at_ref, refs[0], *args))
    pl.when(jnp.logical_not(own))(lambda: gather_block(Swapped(at_ref), refs[1], *args))


def place_ff(at_ref, *refs):
    ins, (gup_ref, gdn_ref, mark_ref, tmp) = refs[:2], refs[-4:]
    mark_ref[...] = jnp.zeros_like(mark_ref)
    block = pl.program_id(0)
    gather_half(at_ref, 0, ins, block, gdn_ref.at[0])
    gather_half(at_ref, 1, ins, block, tmp)
    gup_ref[0] = tmp[...].T.astype(F32)


def place_mixer(packed, at_ref, *refs):
    ins, outs, mark_ref, tmp = refs[:2], refs[2:-2], refs[-2], refs[-1]
    mark_ref[...] = jnp.zeros_like(mark_ref)
    gin_ref, gout_ref = outs[:2]
    pack_ref = outs[2] if packed else None
    step = pl.program_id(0)
    for i in range(2):
        block = lax.rem(step, 2) * 2 + i
        first = step * 64 + i * 32

        @pl.when(step < 3)
        def _():
            to = gin_ref.at[0, 0, pl.ds(i * C, C), :]
            gather_half(at_ref, step // 2, ins, block, to, pack_ref, first)

        @pl.when(step == 3)
        def _():
            gather_half(at_ref, 1, ins, block, tmp, pack_ref, first)
            gout_ref[0, :, pl.ds(i * C, C)] = tmp[...].T.astype(F32)


PACK = 256
SHARED = 72
LAYER_ROWS = 92


def pack_small(at_ref, gnet_ref, gout_ref, *refs):
    keep_ref, give_ref, out_ref = refs[-3:]
    out_ref[...] = jnp.zeros_like(out_ref)
    out_ref[0:NET, :] = gnet_ref[...]
    out_ref[NET : NET + 4, :] = refs[1][20:24, :]
    for l in range(2):
        ff_ref, mixer_ref = refs[2 * l : 2 * l + 2]
        row = SHARED + LAYER_ROWS * l
        if l > 0:
            out_ref[row : row + 2, :] = refs[0][0:2, :]
        out_ref[row + 2 : row + 4, :] = mixer_ref[0:2, :]
        out_ref[row + 4 : row + 5, :] = ff_ref[2:3, :]
        out_ref[row + 5 : row + 6, :] = mixer_ref[2:3, :]
        out_ref[row + 6 : row + 10, :] = ff_ref[3:7, :]
        out_ref[row + 10 : row + 26, :] = mixer_ref[3:19, :]
        out_ref[row + 26 : row + 90, :] = gout_ref[l]
    put_by_core(at_ref, keep_ref, give_ref, slice(None), out_ref[: PACK // 2], out_ref[PACK // 2 :])


def unpack_small(
    at_ref, pack_ref, other_ref, gain_ref, bias_ref, inb_ref, sw_ref, sb_ref, first_ref, inner_ref, fbias_ref, fout_ref,
    skip_ref, outb_ref, upb_ref, dnb_ref, net_s,
):
    net_s[...] = pack_ref[0:SHARED, :] + other_ref[...]
    for l in range(2):
        row = SHARED + LAYER_ROWS * l
        layer = slice(l, l + 1)
        for i, ref in enumerate((gain_ref, bias_ref)):
            low, high = NET + 2 * i, NET + 2 * i + 1
            if l == 0:
                value = jnp.where(at_ref[0] == 0, net_s[low : low + 1, :], net_s[high : high + 1, :])
            else:
                value = pack_ref[row + i : row + i + 1, :]
            ref[l, 0:1, :] = value
            ref[l, 1:2, :] = pack_ref[row + 2 + i : row + 3 + i, :]
        dnb_ref[layer, :] = pack_ref[row + 4 : row + 5, :]
        outb_ref[layer, :] = pack_ref[row + 5 : row + 6, :]
        for i in range(4):
            upb_ref[layer, i * C : (i + 1) * C] = pack_ref[row + 6 + i : row + 7 + i, :]
        for s in range(3):
            inb_ref[s, layer, :] = pack_ref[row + 10 + s : row + 11 + s, :]
            sb_ref[s, layer, :] = pack_ref[row + 22 + s : row + 23 + s, :]
            for j in range(3):
                sw_ref[j, s, layer, :] = pack_ref[row + 13 + 3 * j + s : row + 14 + 3 * j + s, :]
        skip_ref[layer, :] = pack_ref[row + 25 : row + 26, :]
        fout_ref[l] = pack_ref[row + 26 : row + 90, :]
        for i in range(2):
            inner_ref[l, i] = net_s[0:NET, i * 128 + l * NET : i * 128 + (l + 1) * NET]
        lanes = slice(256 + l * NET, 256 + (l + 1) * NET)
        for r in range(EMB):
            first_ref[r, layer, :] = net_s[r : r + 1, lanes]
        for i in range(3):
            fbias_ref[i, layer, :] = net_s[40 + i : 41 + i, lanes]


def sds(shape, dtype=F32):
    return jax.ShapeDtypeStruct(shape, dtype)


def params(us, mib=32):
    return dict(
        compiler_params=pltpu.CompilerParams(vmem_limit_bytes=mib * 2**20),
        cost_estimate=pl.CostEstimate(flops=int(us * 1e9), bytes_accessed=10000, transcendentals=0),
    )


SMEM = pl.BlockSpec(memory_space=pltpu.SMEM)
WHOLE = pl.BlockSpec(memory_space=pltpu.VMEM)
ANY = pl.BlockSpec(memory_space=pl.ANY)
SLOTS = pltpu.VMEM((C // 128, T, 128), F32)


def layer_of(x, l):
    rest = x.ndim - 1
    return pl.BlockSpec((1,) + x.shape[1:], lambda *_: (l,) + (0,) * rest, pipeline_mode=pl.Buffered(1))


def fixed(shape):
    return pl.BlockSpec(shape, lambda *_: (0,) * len(shape))


def spectrum_scratch():
    return [pltpu.VMEM((3 * H, C), BF)] * 2 + [pltpu.VMEM((T, C), F32)] * 2


def run_filter_backward(at, inner, out, sines, cosines, dks):
    return pl.pallas_call(
        filter_backward,
        in_specs=[SMEM] + [WHOLE] * 7,
        out_specs=[WHOLE] * 2,
        out_shape=[sds((2, NET, C)), sds((NET, C))],
        name="filter_backward",
        **params(5, 8),
    )(at, FEATS, inner, out, sines, cosines, *dks)


def run_arrange(at, own, other):
    return pl.pallas_call(
        arrange,
        in_specs=[SMEM, WHOLE, WHOLE],
        out_specs=WHOLE,
        out_shape=sds((T, D)),
        scratch_shapes=[SLOTS],
        name="arrange",
        **params(0.2, 6),
    )(at, own, other)


def run_finish_result(at, x, own, other, vec, l):
    return pl.pallas_call(
        finish_result,
        grid=(1,),
        in_specs=[SMEM, WHOLE, WHOLE, WHOLE, layer_of(vec, l)],
        out_specs=WHOLE,
        out_shape=sds((T, C), BF),
        scratch_shapes=[pltpu.VMEM((T, D), F32), SLOTS],
        name="finish_result",
        **params(2, 8),
    )(at, x, own, other, vec)


def run_finish_grad(at, g, own, other, x, vec, l):
    return pl.pallas_call(
        finish_grad,
        grid=(1,),
        in_specs=[SMEM, WHOLE, WHOLE, WHOLE, WHOLE, layer_of(vec, l)],
        out_specs=WHOLE,
        out_shape=sds((T, C)),
        scratch_shapes=[pltpu.VMEM((T, D), F32), SLOTS],
        name="finish_grad",
        **params(2.6, 8),
    )(at, g, own, other, x, vec)


def first_forward(
    at_ref, own_ref, other_ref, feats_ref, first_ref, inner_ref, bias_ref, out_ref,
    vec_ref, inw_ref, inb_ref, sw_ref, sb_ref, skip_ref, table_ref, outw_ref,
    x_ref, ks_ref, sin_ref, cos_ref, both_ref, wide_ref, u_ref, qs_ref, g_ref, p_ref,
    slots, first_s, bias_s, k_s, *scratch,
):
    rhs_e, rhs_o, se, so = scratch[3:7]
    filter_forward(
        at_ref, feats_ref, first_ref, inner_ref, bias_ref, out_ref, table_ref,
        ks_ref, sin_ref, cos_ref, both_ref, wide_ref, first_s, bias_s, k_s, rhs_e, rhs_o, se, so,
    )
    arrange(at_ref, own_ref, other_ref, x_ref, slots)
    mixer_forward(
        0, False, at_ref, x_ref, vec_ref, inw_ref, inb_ref, sw_ref, sb_ref, ks_ref, skip_ref, table_ref, outw_ref,
        u_ref, qs_ref, g_ref, p_ref, *scratch,
    )


def mixer_forward_scratch():
    return (
        [pltpu.VMEM((T, D), BF), pltpu.VMEM((T, C), F32), pltpu.VMEM((T, C), F32)]
        + spectrum_scratch()
        + [pltpu.VMEM((6 * H, C), BF)] * 2
        + [pltpu.VMEM((T, C), BF)]
    )


def run_first_forward(at, own, other, filters, vec, inw, inb, sw, sb, skip, outw):
    args = [at, own, other, FEATS, *filters, vec, inw, inb, sw, sb, skip, TABLE, outw]
    outs = [
        sds((T, D)), sds((2, 4, H, C)), sds((3, T, 128)), sds((3, T, 128)), sds((2, 128, 128)), sds((2, 128, C)),
        sds((T, 3 * C)), sds((4, H, C)), sds((T, C)), sds((T, D), BF),
    ]
    return pl.pallas_call(
        first_forward,
        in_specs=[SMEM] + [WHOLE] * (len(args) - 1),
        out_specs=[WHOLE] * len(outs),
        out_shape=outs,
        scratch_shapes=[SLOTS, pltpu.VMEM((128, 128), F32), pltpu.VMEM((8, 128), F32), pltpu.VMEM((T, C), F32)]
        + mixer_forward_scratch(),
        name="first_forward",
        **params(13, 14),
    )(*args)


def run_mixer_forward(l, joint, at, x, vec, inw, inb, sw, sb, ks, skip, outw):
    joined = joint is not None
    args = [at, x] + (list(joint) + [vec] if joined else [])
    args += [vec, inw, inb, sw, sb, ks, skip, TABLE, outw]
    outs = ([sds((T, D))] if joined else []) + [sds((T, 3 * C)), sds((4, H, C)), sds((T, C)), sds((T, D), BF)]
    return pl.pallas_call(
        functools.partial(mixer_forward, l, joined),
        in_specs=[SMEM] + [WHOLE] * (len(args) - 1),
        out_specs=[WHOLE] * len(outs),
        out_shape=outs,
        scratch_shapes=mixer_forward_scratch(),
        name="mixer_forward",
        **params(6, 10),
    )(*args)


FC = 512


def up_spec(l):
    return pl.BlockSpec((1, D, FC), lambda j: (l, 0, j))


def down_spec(l):
    return pl.BlockSpec((1, FC, D), lambda j: (l, j, 0))


def hidden_spec(rows, width=FC):
    return pl.BlockSpec((rows, width), lambda j: (0, j))


def run_ff_forward(l, last, at, x, own, other, vec, up, upb, dn, after):
    return pl.pallas_call(
        functools.partial(body_without, functools.partial(ff_forward, last), 8, len(after)),
        grid=(FH // FC,),
        in_specs=[
            SMEM, fixed((T, D)), fixed((T, D)), fixed((T, D)), layer_of(vec, l),
            up_spec(l), pl.BlockSpec((1, 1, FC), lambda j: (l, 0, j)), down_spec(l),
        ] + [ANY] * len(after),
        out_specs=[fixed((T, D)), hidden_spec(T)] + ([fixed((T, C))] * 2 if last else [fixed((T, D))]),
        out_shape=[sds((T, D)), sds((T, FH))] + ([sds((T, C), BF)] * 2 if last else [sds((T, D), BF)]),
        scratch_shapes=[pltpu.VMEM((T, D), BF), pltpu.VMEM((T, D), F32)],
        name="ff_forward",
        **params(6, 16),
    )(at, x, own, other, vec, up, upb, dn, *after)


def run_ff_backward(l, at, g, joint, x, h, vec, up, dn, after):
    joined = joint is not None
    args = [at, g] + (list(joint) + [vec] if joined else []) + [x, h, vec, up, dn]
    specs = [SMEM, fixed((T, D))]
    if joined:
        specs += [fixed((T, D))] * 3 + [layer_of(vec, l + 1)]
    specs += [fixed((T, D)), hidden_spec(T), layer_of(vec, l), up_spec(l), down_spec(l)]
    out_specs = [fixed((T, D))] if joined else []
    outs = [sds((T, D))] if joined else []
    out_specs += [fixed((T, WIDE)), fixed((T, WIDE)), fixed((8, C)), fixed((T, D))]
    outs += [sds((T, WIDE), BF), sds((T, WIDE), BF), sds((8, C)), sds((T, D), BF)]
    return pl.pallas_call(
        functools.partial(body_without, functools.partial(ff_backward, joined), len(args), len(after)),
        grid=(FH // FC,),
        in_specs=specs + [ANY] * len(after),
        out_specs=out_specs,
        out_shape=outs,
        scratch_shapes=[pltpu.VMEM((T, D), BF), pltpu.VMEM((T, D), F32), pltpu.VMEM((8, FH), F32)],
        name="ff_backward",
        **params(8, 20),
    )(*args, *after)


def run_ff_weights(at, mine, got):
    return pl.pallas_call(
        ff_weights,
        in_specs=[SMEM, WHOLE, WHOLE],
        out_specs=[WHOLE] * 4,
        out_shape=[sds((4, PIECE, D), BF)] * 4,
        name="ff_weights",
        **params(3, 12),
    )(at, mine, got)


def run_mixer_backward(l, last, at, g_in, own, other, x1, x0, u, qs, g, ks, vec, inw, outw, sw, sb, skip, after):
    args = [at, g_in, own, other, x1, x0, u, qs, g, ks, vec, inw, outw, sw, sb, skip, TABLE]
    outs = [
        sds((T, D)), sds((24, C)), sds((T, C)), sds((T, D), BF), sds((T, WIDE), BF), sds((T, WIDE), BF),
    ]
    tc = pltpu.VMEM((T, C), F32)
    return pl.pallas_call(
        functools.partial(body_without, functools.partial(mixer_backward, l, last), len(args), len(after)),
        in_specs=[SMEM] + [WHOLE] * (len(args) - 1) + [ANY] * len(after),
        out_specs=[WHOLE] * len(outs),
        out_shape=outs,
        scratch_shapes=[
            pltpu.VMEM((T, D), BF), pltpu.VMEM((T, D), BF), pltpu.VMEM((T, C), BF), pltpu.VMEM((T, 3 * C), BF),
            tc, tc, tc, tc, tc, *spectrum_scratch(),
            pltpu.VMEM((6 * H, 2 * C), BF), pltpu.VMEM((6 * H, 2 * C), BF), pltpu.VMEM((T, 2 * C), F32),
        ],
        name="mixer_backward",
        **params(10, 19),
    )(*args, *after)


def run_mixer_weights(at, mine, got, pack):
    rows = PIECE + (16 if pack else 0)
    return pl.pallas_call(
        functools.partial(mixer_weights, bool(pack)),
        in_specs=[SMEM] + [WHOLE] * (2 + len(pack)),
        out_specs=[WHOLE] * 4,
        out_shape=[sds((4, rows, C), BF)] * 4,
        name="mixer_weights",
        **params(2.4, 12),
    )(at, mine, got, *pack)


def run_add(parts, count, after=(), sides=1):
    shape = parts[0].shape[1:] if count > 1 else parts[0].shape
    width = sum(p.shape[-1] for p in parts[:: len(parts) // sides])
    made = pl.pallas_call(
        functools.partial(body_without, functools.partial(add_parts, len(parts), sides), len(parts), len(after)),
        in_specs=[WHOLE] * len(parts) + [ANY] * len(after),
        out_specs=[WHOLE] * count,
        out_shape=[sds(shape[:-1] + (width,), BF)] * count,
        name="add_parts",
        **params(0.6, 8),
    )(*parts, *after)
    return list(made)


def run_behind(arrays, after, mib=4):
    count = len(arrays)
    return pl.pallas_call(
        lambda *refs: None,
        in_specs=[ANY] * (count + len(after)),
        out_specs=[ANY] * count,
        out_shape=[sds(x.shape, x.dtype) for x in arrays],
        input_output_aliases={i: i for i in range(count)},
        name="behind",
        **params(0.1, mib),
    )(*arrays, *after)


def run_place(body, at, ins, place, into, shapes, out_specs, steps, width, name):
    aliases = {} if into is None else {3: 0, 4: 1}
    into = [] if into is None else list(into)
    return pl.pallas_call(
        functools.partial(body_without, body, 3, len(into)),
        grid=(steps,),
        in_specs=[SMEM] + [lane_block(m.shape, width, place) for m in ins] + [ANY] * len(into),
        out_specs=out_specs + [fixed((8, 128))],
        out_shape=[sds(s) for s in shapes] + [sds((8, 128))],
        scratch_shapes=[pltpu.VMEM((4 * PIECE, width), BF)],
        input_output_aliases=aliases,
        name=name,
        **params(5, 20),
    )(at, *ins, *into)


def lane_block(shape, width, place):
    return pl.BlockSpec(shape[:-1] + (width,), lambda *_: (0,) * (len(shape) - 1) + (place,))


def body_without(body, first, count, *refs):
    body(*refs[:first], *refs[first + count :])


def run_place_ff(l, layers, at, ins, place, into):
    specs = [
        pl.BlockSpec((1, D, 4 * PIECE), lambda p: (l, 0, p)),
        pl.BlockSpec((1, 4 * PIECE, D), lambda p: (l, p, 0)),
    ]
    return run_place(place_ff, at, ins, place, into, [(layers, D, FH), (layers, FH, D)], specs, 4, D, "place_ff")


def run_place_mixer(l, layers, at, ins, place, into):
    packed = ins[0].shape[-2] > PIECE
    specs = [
        pl.BlockSpec((1, 1, D, C), lambda n: (l, jnp.minimum(n, 2), 0, 0)),
        pl.BlockSpec((1, C, D), lambda n: (l, 0, 0)),
    ] + [fixed((PACK, C))] * packed
    shapes = [(layers, 3, D, C), (layers, C, D)] + [(PACK, C)] * packed
    body = functools.partial(place_mixer, packed)
    return run_place(body, at, ins, place, into, shapes, specs, 4, C, "place_mixer")


SWAP = [(0, 1), (1, 0)]


def swap(x, axis):
    return lax.ppermute(x, axis, SWAP)


def shift(x, axis, k):
    pairs = []
    for y, x_at, c in np.ndindex(4, 4, 2):
        along_x = (axis == FIRST) == (c == 0)
        to = (y, (x_at + k) % 4) if along_x else ((y + k) % 4, x_at)
        pairs.append(((y * 4 + x_at) * 2 + c, (to[0] * 4 + to[1]) * 2 + c))
    return lax.ppermute(x, ("y", "x", "c"), pairs)


def send_first(blocks):
    return [blocks[0]] + [shift(blocks[k], FIRST, k) for k in range(1, 4)]


def sum_first(*gradients, after=()):
    return run_add([p for came in gradients for p in came], 4, after, len(gradients))


def send_second(pieces):
    return [pieces[0]] + [shift(pieces[m], SECOND, m) for m in range(1, 4)]


def sum_second(came, after=()):
    return run_add(came, 1, after)[0]


def sum_near(piece, after=()):
    return run_add([piece, swap(piece, "zl")], 1, after)[0]


def gather_second(piece, after):
    came = [shift(piece, SECOND, m) for m in range(1, 4)]
    return jnp.stack([piece] + list(run_behind(came, after)))


def gather_first(row, after):
    came = [shift(row, FIRST, k) for k in range(1, 4)]
    return jnp.stack([row] + list(run_behind(came, after)))


def gather_plane(piece, after):
    mine = lax.all_gather(piece, ("y", "x"), axis=0, tiled=False)
    mine = mine.reshape(1, 4, 4, *piece.shape)
    [mine] = run_behind([mine], after, 56)
    return [mine, swap(mine, "c")]


def run_pack_small(at, gnet, gout, small):
    return pl.pallas_call(
        pack_small,
        in_specs=[SMEM] + [WHOLE] * (2 + len(small)),
        out_specs=[WHOLE] * 2,
        out_shape=[sds((PACK // 2, C))] * 2,
        scratch_shapes=[pltpu.VMEM((PACK, C), F32)],
        name="pack_small",
        **params(0.6, 4),
    )(at, gnet, gout, *small)


def run_unpack_small(at, pack, other):
    shapes = [
        (2, 2, C), (2, 2, C), (3, 2, C), (3, 3, 2, C), (3, 2, C), (EMB, 2, NET), (2, 2, NET, NET), (3, 2, NET),
        (2, NET, C), (2, C), (2, C), (2, FH), (2, C),
    ]
    return pl.pallas_call(
        unpack_small,
        in_specs=[SMEM, WHOLE, WHOLE],
        out_specs=[WHOLE] * len(shapes),
        out_shape=[sds(s) for s in shapes],
        scratch_shapes=[pltpu.VMEM((SHARED, C), F32)],
        name="unpack_small",
        **params(2, 4),
    )(at, pack, other)


def shards(
    tokens, lengths, norm_gain, norm_bias, in_weight, in_bias, short_weight, short_bias, filter_first, filter_inner,
    filter_biases, filter_out, filter_skip, out_weight, out_bias, up_weight, up_bias, down_weight, down_bias, cotangent,
):
    layers = norm_gain.shape[0]
    half_at = lax.axis_index("zh")
    core = lax.axis_index("c")
    x_at, y_at = lax.axis_index("x"), lax.axis_index("y")
    order = jnp.where(core == 0, x_at, y_at), jnp.where(core == 0, y_at, x_at)
    at = jnp.stack([half_at, lengths[0], x_at, y_at, core, *order]).astype(jnp.int32)

    tokens_other = swap(tokens, "zh")
    rows = jnp.stack(
        [norm_gain[:, 0], norm_bias[:, 0], norm_gain[:, 1], norm_bias[:, 1], out_bias, down_bias, out_bias, out_bias], 1
    )
    other = swap(rows, "zh")
    low = half_at == 0
    vec = jnp.concatenate([jnp.where(low, rows, other), jnp.where(low, other, rows)], 2)

    inw = in_weight.transpose(0, 2, 1, 3)
    inb = in_bias.reshape(layers, 1, 3 * C)
    sw = short_weight.reshape(layers, 3, 3 * C)
    sb = short_bias.reshape(layers, 1, 3 * C)
    skip = filter_skip.reshape(layers, 1, C)
    upb = up_bias.reshape(layers, 1, FH)

    cot_other = swap(cotangent, "zh")
    grad = run_arrange(at, cotangent, cot_other)
    saved = []
    joint = None
    for l in range(layers):
        if l == 0:
            filters = filter_first, filter_inner, filter_biases, filter_out
            made = run_first_forward(at, tokens, tokens_other, filters, vec, inw, inb, sw, sb, skip, out_weight)
            x, ks, sines, cosines, inner, fout, *made = made
        else:
            x, *made = run_mixer_forward(l, joint, at, x, vec, inw, inb, sw, sb, ks, skip, out_weight)
        u, qs, g, p = made
        if l == 0:
            [p] = run_behind([p], [cot_other])
        after = [grad] if l == 0 else []
        last = l == layers - 1
        x1, h, *p2 = run_ff_forward(l, last, at, x, p, swap(p, "zh"), vec, up_weight, upb, down_weight, after)
        saved.append((x, u, qs, g, x1, h))
        joint = p2[0], swap(p2[-1], "zh")
        x = x1
    last_branch = joint

    joint = None
    small = [None] * layers
    waits = []
    came = {}
    for l in reversed(range(layers)):
        x0, u, qs, g, x1, h = saved[l]
        made = run_ff_backward(l, at, grad, joint, x1, h, vec, up_weight, down_weight, waits)
        if joint is not None:
            grad, made = made[0], made[1:]
        keep, give, ff_small, p = made
        p, give = run_behind([p, give], [last_branch[1]] if l == layers - 1 else came["mixer", l + 1][1:])
        p_other = swap(p, "zh")
        halves = run_ff_weights(at, keep, swap(give, "c"))
        came["ff", l] = send_first(halves)
        waits = list(halves)
        if l < layers - 1:
            later = send_second(sum_first(came["ff", l + 1], came["mixer", l + 1], after=[p]))
            later = sum_second(later)
            waits.append(later)
            later_other = swap(later, "zl")
        made = run_mixer_backward(
            l, l == 0, at, grad, p, p_other, x1, x0, u, qs, g, ks, vec, inw, out_weight, sw, sb, skip, waits
        )
        grad, mixer_small, dk, p, keep, give = made
        p, give = run_behind([p, give], came["ff", l][1:] + ([later_other] if l < layers - 1 else []))
        joint = (p, swap(p, "zh"), x0) if l else (p, x0)
        small[l] = (ff_small, mixer_small, dk)
        pack = ()
        if l == 0:
            later = run_add([later, later_other], 1, [p])[0]
            ff = sum_second(send_second(sum_first(came["ff", 0], after=[p])))
            gfout, gnet = run_filter_backward(at, inner, fout, sines, cosines, [s[-1] for s in small])
            gfout, gnet = run_behind([gfout, gnet], [ff])
            pack = run_pack_small(at, gnet, gfout, [m for some in small for m in some[:-1]])
            pack = pack[0], swap(pack[1], "c")
            ff = sum_near(ff, pack[1:])
        halves = run_mixer_weights(at, keep, swap(give, "c"), pack)
        came["mixer", l] = send_first(halves)
        waits = list(halves)
        if l == layers - 1:
            result = run_finish_result(at, saved[l][4], *last_branch, vec, l)
            waits.append(result)

    mixer = sum_near(sum_second(send_second(sum_first(came["mixer", 0], after=[ff]))))
    later = gather_plane(later, [mixer])
    p, x0 = joint
    [p] = run_behind([p], [mixer])
    mixer = gather_second(mixer, [])
    *ff_out, mark = run_place_ff(1, layers, at, later, 0, None)
    *mixer_out, other_mark = run_place_mixer(1, layers, at, later, 2, None)
    grad = run_finish_grad(at, grad, p, swap(p, "zh"), x0, vec, 0)
    mixer = gather_first(mixer, [grad, mark, other_mark])
    mixer = [mixer, swap(mixer, "c")]
    *mixer_out, pack, mark = run_place_mixer(0, layers, at, mixer, 0, mixer_out)
    *ff_out, mark = run_place_ff(0, layers, at, gather_plane(ff, [mark]), 0, ff_out)

    gain, shift_, inb, sw, sb, first, inner, fbias, fout, skip, outb, upb, dnb = run_unpack_small(
        at, pack, swap(pack[:SHARED], "zh")
    )
    return (
        result, grad, gain, shift_, mixer_out[0].transpose(0, 2, 1, 3), inb.transpose(1, 0, 2),
        sw.transpose(2, 0, 1, 3), sb.transpose(1, 0, 2), first.transpose(1, 0, 2), inner, fbias.transpose(1, 0, 2),
        fout, skip, mixer_out[1], outb, ff_out[0], upb, ff_out[1], dnb,
    )


def solution(mesh):
    names = ("zl", "y", "x", "c", "zh")
    fine = Mesh(mesh.devices.reshape(2, 4, 4, 2, 2), names)
    dp = ("zl", "y", "x", "c")
    rows = P(dp, "zh")
    third, fourth = P(None, None, "zh"), P(None, None, None, "zh")
    second, middle = P(None, "zh"), P(None, "zh", None)
    placed = (
        rows, P(dp), third, third, fourth, third, fourth, third, P(), P(), P(), third, second, middle, second, third,
        second, middle, second, rows,
    )
    return jax.shard_map(
        shards,
        mesh=fine,
        in_specs=placed,
        out_specs=(
            rows, rows, third, third, fourth, third, fourth, third, P(), P(), P(), third, second, middle, second, third,
            second, middle, second,
        ),
        check_vma=False,
    )
```

```python
import functools
import math

import jax
import jax.numpy as jnp
import ml_dtypes
import numpy as np
from jax import lax
from jax.experimental import pallas as pl
from jax.experimental.pallas import tpu as pltpu
from jax.sharding import Mesh
from jax.sharding import PartitionSpec as P

D = 768
T = 512
H = T // 2
C = 384
FH = 1536
NET = 64
EMB = 33
BANDS = 16
PIECE = 96
EPSILON = 1e-05
HIGH = lax.Precision.HIGHEST
F32 = jnp.float32
BF = jnp.bfloat16

ORDER = np.concatenate([np.arange(0, T, 2), np.arange(1, T, 2)])


def split_table(t):
    hi = t.astype(ml_dtypes.bfloat16)
    lo = (t - hi.astype(np.float64)).astype(ml_dtypes.bfloat16)
    return hi, lo


def wave_tables():
    n = np.arange(H)
    even = 2 * math.pi * (np.outer(n, 2 * n) % (2 * T)) / (2 * T)
    odd = 2 * math.pi * (np.outer(n, 2 * n + 1) % (2 * T)) / (2 * T)
    alt = np.where(n % 2 == 0, 1.0, -1.0)
    out = []
    for ang in (even, odd):
        co, si = np.cos(ang), np.sin(ang)
        si[0] = alt
        hi, lo = split_table(np.concatenate([co, si], 0))
        out.append(np.concatenate([hi, lo, hi], 1))
        hi, lo = split_table(np.concatenate([co.T, si.T], 1))
        out.append(np.concatenate([hi, lo, hi], 1))
    fe, ie, fo, io = out
    return np.concatenate([fe, fo, np.concatenate([ie, io], 0)], 1)


TABLE = wave_tables()
FORWARD_EVEN = slice(None), slice(0, 3 * H)
FORWARD_ODD = slice(None), slice(3 * H, 6 * H)
INVERSE_EVEN = slice(0, H), slice(6 * H, 12 * H)
INVERSE_ODD = slice(H, 2 * H), slice(6 * H, 12 * H)


def slot_features():
    slots = ORDER.astype(np.float64)
    freqs = 0.0001 + (BANDS - 1 - 0.0001) * np.arange(BANDS) / (BANDS - 1)
    angle = 2 * math.pi * slots[:, None] * freqs[None, :] / T
    times = (slots / (T - 1))[:, None]
    feats = np.concatenate([times, np.cos(angle), -np.sin(angle), np.zeros((T, 128 - EMB))], 1)
    return feats.astype(np.float32)


FEATS = slot_features()


def dot(a, b):
    return lax.dot_general(a, b, (((1,), (0,)), ((), ())), preferred_element_type=F32)


def dot_nt(a, b):
    return lax.dot_general(a, b, (((1,), (1,)), ((), ())), preferred_element_type=F32)


def dot_tn(a, b):
    return lax.dot_general(a, b, (((0,), (0,)), ((), ())), preferred_element_type=F32)


def normalize(x):
    mean = jnp.mean(x, -1, keepdims=True)
    scale = lax.rsqrt(jnp.mean(x * x, -1, keepdims=True) - mean * mean + EPSILON)
    return (x - mean) * scale, scale


def norm_pull(dn, x, gain):
    xhat, scale = normalize(x)
    ds = dn * gain
    first = jnp.mean(ds, -1, keepdims=True)
    second = jnp.mean(ds * xhat, -1, keepdims=True)
    return scale * (ds - first - xhat * second), dn * xhat


def row_mask(start, rows, length):
    r = start + lax.broadcasted_iota(jnp.int32, (rows, 1), 0)
    slot = jnp.where(r < H, 2 * r, 2 * (r - H) + 1)
    return (slot < length).astype(F32)


def down_one(x):
    r = lax.broadcasted_iota(jnp.int32, x.shape, 0)
    return jnp.where(r == 0, 0.0, pltpu.roll(x, 1, 0))


def up_one(x):
    r = lax.broadcasted_iota(jnp.int32, x.shape, 0)
    return jnp.where(r == x.shape[0] - 1, 0.0, pltpu.roll(x, x.shape[0] - 1, 0))


def put_split(ref, value, rows, lanes):
    hi = value.astype(BF)
    lo = (value - hi.astype(F32)).astype(BF)
    step = ref.shape[0] // 3
    ref[pl.ds(rows, value.shape[0]), lanes] = hi
    ref[pl.ds(step + rows, value.shape[0]), lanes] = hi
    ref[pl.ds(2 * step + rows, value.shape[0]), lanes] = lo


def top_row(shape):
    return lax.broadcasted_iota(jnp.int32, shape, 0) == 0


def butterfly(even, odd, lanes):
    ce, se = even[pl.ds(0, H), lanes], even[pl.ds(H, H), lanes]
    co, so = odd[pl.ds(0, H), lanes], odd[pl.ds(H, H), lanes]
    top = top_row(ce.shape)
    return ce + co, ce - co, jnp.where(top, se, se + so), jnp.where(top, so, se - so)


def spectrum_product(a, k, conj):
    a1, a2, b1, b2 = a
    k1, k2, l1, l2 = k
    top = top_row(a1.shape)
    aa, bb, cc, dd = a1 * k1, b1 * l1, a2 * k2, b2 * l2
    if conj:
        y1 = jnp.where(top, aa, aa + bb)
        y2 = jnp.where(top, cc, cc + dd)
        m1 = jnp.where(top, bb + dd, b1 * k1 - a1 * l1)
        m2 = jnp.where(top, b2 * l1 - b1 * l2, b2 * k2 - a2 * l2)
    else:
        y1 = jnp.where(top, aa, aa - bb)
        y2 = jnp.where(top, cc, cc - dd)
        m1 = jnp.where(top, bb - dd, a1 * l1 + b1 * k1)
        m2 = jnp.where(top, b1 * l2 + b2 * l1, a2 * l2 + b2 * k2)
    return y1, y2, m1, m2


def put_inverse(rhs_e, rhs_o, y, lanes):
    y1, y2, m1, m2 = y
    top = top_row(y1.shape)
    unit = 1.0 / T
    w = jnp.where(top, 0.5 * unit, unit)
    put_split(rhs_e, (y1 + y2) * w, 0, lanes)
    put_split(rhs_o, (y1 - y2) * w, 0, lanes)
    put_split(rhs_e, jnp.where(top, m1, m1 + m2) * unit, H, lanes)
    put_split(rhs_o, jnp.where(top, m2, m1 - m2) * unit, H, lanes)


def lanes_of(block):
    return pl.ds(block * 128, 128)


def short_conv(u_ref, sw_ref, sb_ref, block):
    out = []
    for s in range(3):
        at = lanes_of(s * (C // 128) + block)
        ue, uo = u_ref[pl.ds(0, H), at], u_ref[pl.ds(H, H), at]
        t0, t1, t2 = (sw_ref[j : j + 1, at] for j in range(3))
        bias = sb_ref[0:1, at]
        uo_d = down_one(uo)
        we = t2 * ue + t1 * uo_d + t0 * down_one(ue) + bias
        wo = t2 * uo + t1 * ue + t0 * uo_d + bias
        out.append((we, wo))
    return out


def hdot(a, b, dims=(1, 0)):
    return lax.dot_general(
        a, b, (((dims[0],), (dims[1],)), ((), ())), precision=HIGH, preferred_element_type=F32
    )


def decay_of(half_at, feats_ref):
    slow = math.log(0.01) / 1.5
    fast = math.log(0.01) / 0.3
    channel = (half_at * C + lax.broadcasted_iota(jnp.int32, (1, C), 1)).astype(F32)
    rates = jnp.abs(slow + (fast - slow) * channel / (D - 1))
    return jnp.exp(-feats_ref[:, 0:1] * rates) + 0.05


def sin_cos(x):
    k = jnp.floor(x * (2 / math.pi) + 0.5)
    r = ((x - k * 1.5703125) - k * 4.837512969970703125e-4) - k * 7.54978995489188e-8
    rr = r * r
    sine = r + r * rr * (-1.6666654611e-1 + rr * (8.3321608736e-3 + rr * -1.9515295891e-4))
    cosine = 1.0 - 0.5 * rr + rr * rr * (
        4.166664568298827e-2 + rr * (-1.388731625493765e-3 + rr * 2.443315711809948e-5)
    )
    quarter = k - 4.0 * jnp.floor(k * 0.25)
    odd = (quarter == 1.0) | (quarter == 3.0)
    s = jnp.where(odd, cosine, sine)
    c = jnp.where(odd, sine, cosine)
    return jnp.where(quarter >= 2.0, -s, s), jnp.where((quarter == 1.0) | (quarter == 2.0), -c, c)


def filter_forward(
    at_ref, feats_ref, first_ref, inner_ref, bias_ref, out_ref, table_ref,
    ks_ref, sin_ref, cos_ref, both_ref, wide_ref, first_s, bias_s, k_s, rhs_e, rhs_o, se, so,
):
    for ref in (both_ref, wide_ref, first_s, bias_s):
        ref[...] = jnp.zeros_like(ref)
    for l in range(2):
        at = pl.ds(l * NET, NET)
        first_s[0:EMB, at] = first_ref[l]
        bias_s[0:3, at] = bias_ref[l]
        wide_ref[l, at, :] = out_ref[l]
        for i in range(2):
            both_ref[i, at, at] = inner_ref[l, i]
    low = feats_ref[...]
    for i in range(3):
        weight = first_s[...] if i == 0 else both_ref[i - 1]
        low, cosine = sin_cos(hdot(low, weight) + bias_s[i : i + 1, :])
        sin_ref[i] = low
        cos_ref[i] = cosine
    decay = decay_of(at_ref[0], feats_ref)
    for l in range(2):
        k_s[...] = hdot(sin_ref[2], wide_ref[l]) * decay
        for b in range(C // 128):
            at = lanes_of(b)
            put_split(rhs_e, k_s[pl.ds(0, H), at], 0, at)
            put_split(rhs_o, k_s[pl.ds(H, H), at], 0, at)
        se[...] = dot(table_ref[FORWARD_EVEN], rhs_e[...])
        so[...] = dot(table_ref[FORWARD_ODD], rhs_o[...])
        for b in range(C // 128):
            at = lanes_of(b)
            for i, v in enumerate(butterfly(se, so, at)):
                ks_ref[l, i, :, at] = v


def filter_backward(at_ref, feats_ref, inner_ref, out_ref, sin_ref, cos_ref, dk0_ref, dk1_ref, gout_ref, gnet_ref):
    decay = decay_of(at_ref[0], feats_ref)
    ds = jnp.zeros((T, 128), F32)
    for l, dk_ref in enumerate((dk0_ref, dk1_ref)):
        dk = dk_ref[...] * decay
        gout_ref[l] = hdot(sin_ref[2], dk, (0, 0))[l * NET : (l + 1) * NET]
        ds += hdot(dk, out_ref[l], (1, 1))
    lane = lax.broadcasted_iota(jnp.int32, (NET, 128), 1)
    gnet_ref[...] = jnp.zeros_like(gnet_ref)
    for i in (2, 1, 0):
        da = ds * cos_ref[i]
        gnet_ref[40 + i : 41 + i, pl.ds(256, 128)] = jnp.sum(da, 0, keepdims=True)
        if i > 0:
            block = hdot(sin_ref[i - 1], da, (0, 0))
            gnet_ref[:, pl.ds((i - 1) * 128, 128)] = jnp.where(lane < NET, block[:NET], block[NET:])
            ds = hdot(da, inner_ref[i - 1], (1, 1))
        else:
            gnet_ref[0:40, pl.ds(256, 128)] = hdot(feats_ref[...], da, (0, 0))[0:40]


def arrange(at_ref, own_ref, other_ref, out_ref, tmp):
    for half, first in ((0, own_ref), (1, other_ref)):
        for b in range(C // 128):
            tmp[b] = first[:, lanes_of(b)].astype(F32)

        def put(first_lane):
            for b in range(C // 128):
                to = pl.ds(first_lane + b * 128, 128)
                out_ref[pl.ds(0, H), to] = tmp[b, pl.ds(0, H, stride=2), :]
                out_ref[pl.ds(H, H), to] = tmp[b, pl.ds(1, H, stride=2), :]

        pl.when(at_ref[0] == half)(functools.partial(put, 0))
        pl.when(at_ref[0] != half)(functools.partial(put, C))


def my_lanes(at_ref, row):
    return jnp.where(at_ref[0] == 0, row[:, :C], row[:, C:])


def by_slot(at_ref, src_ref, out_ref, tmp):
    def put(first_lane):
        for b in range(C // 128):
            lanes = pl.ds(first_lane + b * 128, 128)
            tmp[b, pl.ds(0, H, stride=2), :] = src_ref[pl.ds(0, H), lanes]
            tmp[b, pl.ds(1, H, stride=2), :] = src_ref[pl.ds(H, H), lanes]

    pl.when(at_ref[0] == 0)(functools.partial(put, 0))
    pl.when(at_ref[0] != 0)(functools.partial(put, C))
    for b in range(C // 128):
        out_ref[:, lanes_of(b)] = tmp[b].astype(out_ref.dtype)


def finish_result(at_ref, x_ref, own_ref, other_ref, vec_ref, out_ref, y_s, tmp):
    def put(first_lane):
        lanes = pl.ds(first_lane, C)

        def body(start, c):
            rows = pl.ds(start, RB)
            y = own_ref[rows, :].astype(F32) + other_ref[rows, :].astype(F32) + vec_ref[0, 5:6, lanes]
            y_s[rows, lanes] = x_ref[rows, lanes] + row_mask(start, RB, at_ref[1]) * y
            return c

        row_loop(body)

    pl.when(at_ref[0] == 0)(functools.partial(put, 0))
    pl.when(at_ref[0] != 0)(functools.partial(put, C))
    by_slot(at_ref, y_s, out_ref, tmp)


def finish_grad(at_ref, g_ref, own_ref, other_ref, x_ref, vec_ref, out_ref, x_s, tmp):
    def body(start, c):
        at = pl.ds(start, RB)
        dn = own_ref[at, :].astype(F32) + other_ref[at, :].astype(F32)
        x_s[at, :] = g_ref[at, :] + norm_pull(dn, x_ref[at, :], vec_ref[0, 0:1, :])[0]
        return c

    row_loop(body)
    by_slot(at_ref, x_s, out_ref, tmp)


def add_branch(x_ref, own_ref, other_ref, vec_ref, row, length, start, rows):
    at = pl.ds(start, rows)
    y = own_ref[at, :].astype(F32) + other_ref[at, :].astype(F32) + vec_ref[row : row + 1, :]
    return x_ref[at, :] + row_mask(start, rows, length) * y


RB = 128


def row_loop(body, init=0):
    def step(i, c):
        return body(pl.multiple_of(i * RB, RB), c)

    return lax.fori_loop(0, T // RB, step, init)


def mixer_forward(l, joined, *refs):
    at_ref, x_ref = refs[:2]
    refs = refs[2:]
    if joined:
        own_ref, other_ref, prev_ref = refs[:3]
        refs = refs[3:]
    (vec_ref, inw_ref, inb_ref, sw_ref, sb_ref, ks_ref, skip_ref, table_ref, outw_ref) = refs[:9]
    refs = refs[9:]
    if joined:
        xo_ref = refs[0]
        refs = refs[1:]
    u_ref, qs_ref, g_ref, p_ref, a_s, w0_s, q_s, rhs_e, rhs_o, se, so, rhs2_e, rhs2_o, z_s = refs

    def first(start, c):
        at = pl.ds(start, RB)
        if joined:
            x = add_branch(x_ref, own_ref, other_ref, prev_ref.at[l - 1], 5, at_ref[1], start, RB)
            xo_ref[at, :] = x
        else:
            x = x_ref[at, :]
        xhat, _ = normalize(x)
        a_s[at, :] = (xhat * vec_ref[l, 0:1, :] + vec_ref[l, 1:2, :]).astype(BF)
        return c

    row_loop(first)
    for s in range(3):
        at = pl.ds(s * C, C)
        u_ref[:, at] = dot(a_s[...], inw_ref[l, s]) + inb_ref[l, 0:1, at]
    for b in range(C // 128):
        at = lanes_of(b)
        (w0e, w0o), (w1e, w1o), (w2e, w2o) = short_conv(u_ref, sw_ref.at[l], sb_ref.at[l], b)
        w0_s[pl.ds(0, H), at] = w0e
        w0_s[pl.ds(H, H), at] = w0o
        qe, qo = w2e * w1e, w2o * w1o
        q_s[pl.ds(0, H), at] = qe
        q_s[pl.ds(H, H), at] = qo
        put_split(rhs_e, qe, 0, at)
        put_split(rhs_o, qo, 0, at)
    se[...] = dot(table_ref[FORWARD_EVEN], rhs_e[...])
    so[...] = dot(table_ref[FORWARD_ODD], rhs_o[...])
    for b in range(C // 128):
        at = lanes_of(b)
        spec = butterfly(se, so, at)
        for i, v in enumerate(spec):
            qs_ref[i, :, at] = v
        y = spectrum_product(spec, [ks_ref[l, i, :, at] for i in range(4)], False)
        put_inverse(rhs2_e, rhs2_o, y, at)
    se[pl.ds(0, H), :] = dot(table_ref[INVERSE_EVEN], rhs2_e[...])
    se[pl.ds(H, H), :] = dot(table_ref[INVERSE_ODD], rhs2_o[...])

    def last(start, c):
        at = pl.ds(start, RB)
        g = se[at, :] + skip_ref[l, 0:1, :] * q_s[at, :]
        g_ref[at, :] = g
        z_s[at, :] = (g * w0_s[at, :]).astype(BF)
        return c

    row_loop(last)
    p_ref[...] = dot(z_s[...], outw_ref[l]).astype(BF)


def gelu_parts(h):
    c0 = math.sqrt(2 / math.pi)
    hh = h * h
    t = jnp.tanh(c0 * (h + 0.044715 * (hh * h)))
    half = 0.5 * (1.0 + t)
    return half, t, hh, c0


def ff_forward(l, last, at_ref, x_ref, own_ref, other_ref, vec_ref, up_ref, upb_ref, dn_ref, xo_ref, h_ref, *refs):
    *p_refs, b_s, acc = refs

    def first(start, c):
        at = pl.ds(start, RB)
        x = add_branch(x_ref, own_ref, other_ref, vec_ref.at[l], 4, at_ref[1], start, RB)
        xo_ref[at, :] = x
        xhat, _ = normalize(x)
        b_s[at, :] = (xhat * vec_ref[l, 2:3, :] + vec_ref[l, 3:4, :]).astype(BF)
        return c

    row_loop(first)
    for j in range(FH // FC):
        part = slice(j * FC, (j + 1) * FC)
        h = dot(b_s[...], up_ref[l, :, part]) + upb_ref[l, :, part]
        h_ref[:, part] = h
        half, _, _, _ = gelu_parts(h)
        total = dot((h * half).astype(BF), dn_ref[l, part, :])
        if j == 0:
            acc[...] = total
        else:
            acc[...] += total
    if not last:
        p_refs[0][...] = acc[...].astype(BF)
    else:
        low, high = acc[:, :C].astype(BF), acc[:, C:].astype(BF)
        own = at_ref[0] == 0
        p_refs[0][...] = jnp.where(own, low, high)
        p_refs[1][...] = jnp.where(own, high, low)


def put_by_core(at_ref, keep_ref, give_ref, at, low, high):
    @pl.when(at_ref[4] == 0)
    def _():
        keep_ref[at] = low
        give_ref[at] = high

    @pl.when(at_ref[4] != 0)
    def _():
        keep_ref[at] = high
        give_ref[at] = low


def ff_backward(l, joined, *refs):
    at_ref, g_ref = refs[:2]
    refs = refs[2:]
    if joined:
        own_ref, other_ref, xn_ref = refs[:3]
        refs = refs[3:]
    vec_ref, x_ref, h_ref, up_ref, dn_ref = refs[:5]
    refs = refs[5:]
    if joined:
        go_ref, refs = refs[0], refs[1:]
    keep_ref, give_ref, small_ref, p_ref, dm_s, acc = refs

    def first(start, c):
        at = pl.ds(start, RB)
        g = g_ref[at, :]
        sums, s1, s2 = c
        if joined:
            dn = own_ref[at, :].astype(F32) + other_ref[at, :].astype(F32)
            dx, dg = norm_pull(dn, xn_ref[at, :], vec_ref[l + 1, 0:1, :])
            g = g + dx
            go_ref[at, :] = g
            s1 = s1 + jnp.sum(dg, 0, keepdims=True)
            s2 = s2 + jnp.sum(dn, 0, keepdims=True)
        dm = (row_mask(start, RB, at_ref[1]) * g).astype(BF)
        dm_s[at, :] = dm
        xhat, _ = normalize(x_ref[at, :])
        b = (xhat * vec_ref[l, 2:3, :] + vec_ref[l, 3:4, :]).astype(BF)
        put_by_core(at_ref, keep_ref, give_ref, (at, pl.ds(0, D)), dm, b)
        return sums + jnp.sum(dm.astype(F32), 0, keepdims=True), s1, s2

    zero = jnp.zeros((1, D), F32)
    sums, s1, s2 = row_loop(first, (zero, zero, zero))
    small_ref[...] = jnp.zeros_like(small_ref)
    for i, row in enumerate((s1, s2, sums)):
        small_ref[i : i + 1, :] = my_lanes(at_ref, row)
    for j in range(FH // FC):
        part = slice(j * FC, (j + 1) * FC)
        h = h_ref[:, part]
        half, t, hh, c0 = gelu_parts(h)
        e = (h * half).astype(BF)
        slope = half + 0.5 * c0 * h * (1.0 - t * t) * (1.0 + 3 * 0.044715 * hh)
        dh = (dot_nt(dm_s[...], dn_ref[l, part, :]) * slope).astype(BF)
        put_by_core(at_ref, keep_ref, give_ref, (slice(None), pl.ds(D + j * FC, FC)), e, dh)
        sums = jnp.sum(dh.astype(F32), 0, keepdims=True)
        for i in range(FC // C):
            small_ref[3 + j * FC // C + i : 4 + j * FC // C + i, :] = sums[:, i * C : (i + 1) * C]
        total = dot_nt(dh, up_ref[l, :, part])
        if j == 0:
            acc[...] = total
        else:
            acc[...] += total
    p_ref[...] = acc[...].astype(BF)


FIRST, SECOND = 5, 6
WIDE = 3 * D


class Swapped:
    def __init__(self, at_ref):
        self.at_ref = at_ref

    def __getitem__(self, i):
        return self.at_ref[{FIRST: SECOND, SECOND: FIRST}.get(i, i)]


def put_pieces(at_ref, ref, value):
    for n in range(4):
        ref[lax.rem(n - at_ref[SECOND] + 4, 4), pl.ds(0, PIECE)] = value[n * PIECE : (n + 1) * PIECE]


def ff_weights(at_ref, mine_ref, got_ref, *outs):
    for k, out_ref in enumerate(outs):
        block = lax.rem(at_ref[FIRST] + k, 4)
        lanes = pl.ds(pl.multiple_of(D + block * 4 * PIECE, 128), 4 * PIECE)
        total = sum(dot_tn(ref[:, lanes], ref[:, pl.ds(0, D)]) for ref in (mine_ref, got_ref))
        put_pieces(at_ref, out_ref, total.astype(BF))


def mixer_backward(
    l, last, at_ref, g_in_ref, own_ref, other_ref, x1_ref, x0_ref, u_ref, qs_ref, g_ref, ks_ref, vec_ref, inw_ref, outw_ref,
    sw_ref, sb_ref, skip_ref, table_ref,
    go_ref, small_ref, dk_ref, p_ref, keep_ref, give_ref, dy_ref, a_ref, z_ref, du_ref, dz_s, dg_s, w1_s, w2_s, dw0_s, rhs_e, rhs_o, se, so, rhs2_e, rhs2_o, inv_s,
):
    small_ref[...] = jnp.zeros_like(small_ref)

    def first(start, c):
        at = pl.ds(start, RB)
        sums, s1, s2 = c
        dn = own_ref[at, :].astype(F32) + other_ref[at, :].astype(F32)
        dx, dg = norm_pull(dn, x1_ref[at, :], vec_ref[l, 2:3, :])
        g = g_in_ref[at, :] + dx
        go_ref[at, :] = g
        dy = (row_mask(start, RB, at_ref[1]) * g).astype(BF)
        dy_ref[at, :] = dy
        xhat, _ = normalize(x0_ref[at, :])
        a_ref[at, :] = (xhat * vec_ref[l, 0:1, :] + vec_ref[l, 1:2, :]).astype(BF)
        return (
            sums + jnp.sum(dy.astype(F32), 0, keepdims=True),
            s1 + jnp.sum(dg, 0, keepdims=True),
            s2 + jnp.sum(dn, 0, keepdims=True),
        )

    zero = jnp.zeros((1, D), F32)
    sums, s1, s2 = row_loop(first, (zero, zero, zero))
    for i, row in enumerate((s1, s2, sums)):
        small_ref[i : i + 1, :] = my_lanes(at_ref, row)
    dz_s[...] = dot_nt(dy_ref[...], outw_ref[l])
    halves = (pl.ds(0, H), pl.ds(H, H))
    for b in range(C // 128):
        at = lanes_of(b)
        w0, w1, w2 = short_conv(u_ref, sw_ref.at[l], sb_ref.at[l], b)
        dskip = 0.0
        for i, (rows, rhs) in enumerate(zip(halves, (rhs_e, rhs_o))):
            dz, g = dz_s[rows, at], g_ref[rows, at]
            z_ref[rows, at] = (g * w0[i]).astype(BF)
            dw0_s[rows, at] = dz * g
            dg = dz * w0[i]
            dg_s[rows, at] = dg
            dskip = dskip + jnp.sum(dg * (w2[i] * w1[i]), 0, keepdims=True)
            w1_s[rows, at] = w1[i]
            w2_s[rows, at] = w2[i]
            put_split(rhs, dg, 0, at)
        small_ref[18:19, at] = dskip
    se[...] = dot(table_ref[FORWARD_EVEN], rhs_e[...])
    so[...] = dot(table_ref[FORWARD_ODD], rhs_o[...])
    for b in range(C // 128):
        at = lanes_of(b)
        spec = butterfly(se, so, at)
        put_inverse(rhs2_e, rhs2_o, spectrum_product(spec, [ks_ref[l, i, :, at] for i in range(4)], True), at)
        put_inverse(
            rhs2_e, rhs2_o, spectrum_product(spec, [qs_ref[i, :, at] for i in range(4)], True), pl.ds(C + b * 128, 128)
        )
    inv_s[pl.ds(0, H), :] = dot(table_ref[INVERSE_EVEN], rhs2_e[...])
    inv_s[pl.ds(H, H), :] = dot(table_ref[INVERSE_ODD], rhs2_o[...])
    dk_ref[...] = inv_s[:, pl.ds(C, C)]
    for b in range(C // 128):
        at = lanes_of(b)
        dw = [[dw0_s[rows, at] for rows in halves], [], []]
        for rows in halves:
            dq = inv_s[rows, at] + skip_ref[l, 0:1, at] * dg_s[rows, at]
            dw[1].append(dq * w2_s[rows, at])
            dw[2].append(dq * w1_s[rows, at])
        for s in range(3):
            to = lanes_of(s * (C // 128) + b)
            ue, uo = u_ref[halves[0], to], u_ref[halves[1], to]
            t0, t1, t2 = (sw_ref[l, j : j + 1, to] for j in range(3))
            de, do = dw[s]
            de_u, do_u = up_one(de), up_one(do)
            due = (t2 * de + t1 * do + t0 * de_u).astype(BF)
            duo = (t2 * do + t1 * de_u + t0 * do_u).astype(BF)
            du_ref[halves[0], to] = due
            du_ref[halves[1], to] = duo
            uo_d = down_one(uo)
            small_ref[3 + s : 4 + s, at] = jnp.sum(due.astype(F32) + duo.astype(F32), 0, keepdims=True)
            taps = de * down_one(ue) + do * uo_d, de * uo_d + do * ue, de * ue + do * uo
            for j, tap in enumerate(taps):
                small_ref[6 + 3 * j + s : 7 + 3 * j + s, at] = jnp.sum(tap, 0, keepdims=True)
            small_ref[15 + s : 16 + s, at] = jnp.sum(de + do, 0, keepdims=True)
    part = dot_nt(du_ref[:, pl.ds(0, C)], inw_ref[l, 0])
    for s in range(1, 3):
        part += dot_nt(du_ref[:, pl.ds(s * C, C)], inw_ref[l, s])
    p_ref[...] = part.astype(BF)

    def spread(start, c):
        rows = pl.ds(start, RB)
        a, dy, z = a_ref[rows, :], dy_ref[rows, :], z_ref[rows, :]
        du = [du_ref[rows, pl.ds(s * C, C)] for s in range(3)]
        lane = 0
        for low, high in ((a, a), (du[0], du[2]), (a, dy), (du[1], z)):
            put_by_core(at_ref, keep_ref, give_ref, (rows, pl.ds(lane, low.shape[1])), low, high)
            lane += low.shape[1]
        return c

    row_loop(spread)
    if last:

        def terms(start, c):
            at = pl.ds(start, RB)
            dn = p_ref[at, :].astype(F32)
            xhat, _ = normalize(x0_ref[at, :])
            return c[0] + jnp.sum(dn * xhat, 0, keepdims=True), c[1] + jnp.sum(dn, 0, keepdims=True)

        s1, s2 = row_loop(terms, (zero, zero))
        for i, row in enumerate((s1, s2)):
            for half in range(2):
                small_ref[20 + 2 * i + half : 21 + 2 * i + half, :] = row[:, half * C : (half + 1) * C]


def put_split_rows(value):
    hi = value.astype(BF).astype(F32)
    return jnp.concatenate([hi, value - hi], 0).astype(BF)


def mixer_weights(packed, at_ref, mine_ref, got_ref, *refs):
    if packed:
        pack_refs, refs = refs[:2], refs[2:]
    for k, out_ref in enumerate(refs):
        block = lax.rem(at_ref[FIRST] + k, 4)
        left = pl.multiple_of(jnp.where(block < 2, block, block + 1) * C, 128)
        right = pl.multiple_of(jnp.where(block < 2, D, 2 * D + C), 128)
        total = sum(dot_tn(ref[:, pl.ds(left, C)], ref[:, pl.ds(right, C)]) for ref in (mine_ref, got_ref))
        put_pieces(at_ref, out_ref, total.astype(BF))
        if packed:
            for n in range(4):
                rows = pl.ds(pl.multiple_of(block * 32 + n * 8, 8), 8)
                value = pack_refs[0][rows, :] + pack_refs[1][rows, :]
                out_ref[lax.rem(n - at_ref[SECOND] + 4, 4), pl.ds(PIECE, 16)] = put_split_rows(value)


def add_parts(count, sides, *refs):
    ins, outs = refs[:count], refs[count:]
    lane = 0
    for side in range(sides):
        some = ins[side * count // sides : (side + 1) * count // sides]
        lanes = slice(lane, lane + some[0].shape[-1])
        lane = lanes.stop
        for i, out in enumerate(outs):
            total = functools.reduce(jnp.add, [(r[i] if len(outs) > 1 else r[...]).astype(F32) for r in some])
            rows = (slice(None),) * (total.ndim - 2)
            out[rows + (slice(0, PIECE), lanes)] = total[rows + (slice(0, PIECE),)].astype(BF)
            if total.shape[-2] > PIECE:
                for n in range(total.shape[0] if total.ndim > 2 else 1):
                    value = total[n] if total.ndim > 2 else total
                    value = value[PIECE : PIECE + 8] + value[PIECE + 8 : PIECE + 16]
                    to = (n, slice(PIECE, PIECE + 16)) if total.ndim > 2 else slice(PIECE, PIECE + 16)
                    out[to] = put_split_rows(value)


def gather_block(at_ref, ref, block, tmp, pack_ref=None, first=0):
    for m in range(4):
        if len(ref.shape) == 5:
            by_x = (at_ref[4] == 0) != isinstance(at_ref, Swapped)
            at = 0, jnp.where(by_x, m, block), jnp.where(by_x, block, m)
        else:
            at = lax.rem(at_ref[FIRST] - block + 4, 4), lax.rem(at_ref[SECOND] - m + 4, 4)
        tmp[pl.ds(m * PIECE, PIECE), :] = ref[at + (slice(0, PIECE),)].astype(tmp.dtype)
        if pack_ref is not None:
            extra = ref[at + (slice(PIECE, PIECE + 16),)].astype(F32)
            pack_ref[pl.ds(pl.multiple_of(first + m * 8, 8), 8), :] = extra[:8] + extra[8:]


def gather_half(at_ref, half, refs, *args):
    own = at_ref[4] == half
    pl.when(own)(lambda: gather_block(at_ref, refs[0], *args))
    pl.when(jnp.logical_not(own))(lambda: gather_block(Swapped(at_ref), refs[1], *args))


def place_ff(at_ref, *refs):
    ins, (gup_ref, gdn_ref, mark_ref, tmp) = refs[:2], refs[-4:]
    mark_ref[...] = jnp.zeros_like(mark_ref)
    block = pl.program_id(0)
    gather_half(at_ref, 0, ins, block, gdn_ref.at[0])
    gather_half(at_ref, 1, ins, block, tmp)
    gup_ref[0] = tmp[...].T.astype(F32)


def place_mixer(packed, at_ref, *refs):
    ins, outs, mark_ref, tmp = refs[:2], refs[2:-2], refs[-2], refs[-1]
    mark_ref[...] = jnp.zeros_like(mark_ref)
    gin_ref, gout_ref = outs[:2]
    pack_ref = outs[2] if packed else None
    step = pl.program_id(0)
    for i in range(2):
        block = lax.rem(step, 2) * 2 + i
        first = step * 64 + i * 32

        @pl.when(step < 3)
        def _():
            to = gin_ref.at[0, 0, pl.ds(i * C, C), :]
            gather_half(at_ref, step // 2, ins, block, to, pack_ref, first)

        @pl.when(step == 3)
        def _():
            gather_half(at_ref, 1, ins, block, tmp, pack_ref, first)
            gout_ref[0, :, pl.ds(i * C, C)] = tmp[...].T.astype(F32)


PACK = 256
SHARED = 72
LAYER_ROWS = 92


def pack_small(at_ref, gnet_ref, gout_ref, *refs):
    keep_ref, give_ref, out_ref = refs[-3:]
    out_ref[...] = jnp.zeros_like(out_ref)
    out_ref[0:NET, :] = gnet_ref[...]
    out_ref[NET : NET + 4, :] = refs[1][20:24, :]
    for l in range(2):
        ff_ref, mixer_ref = refs[2 * l : 2 * l + 2]
        row = SHARED + LAYER_ROWS * l
        if l > 0:
            out_ref[row : row + 2, :] = refs[0][0:2, :]
        out_ref[row + 2 : row + 4, :] = mixer_ref[0:2, :]
        out_ref[row + 4 : row + 5, :] = ff_ref[2:3, :]
        out_ref[row + 5 : row + 6, :] = mixer_ref[2:3, :]
        out_ref[row + 6 : row + 10, :] = ff_ref[3:7, :]
        out_ref[row + 10 : row + 26, :] = mixer_ref[3:19, :]
        out_ref[row + 26 : row + 90, :] = gout_ref[l]
    put_by_core(at_ref, keep_ref, give_ref, slice(None), out_ref[: PACK // 2], out_ref[PACK // 2 :])


def unpack_small(
    at_ref, pack_ref, other_ref, gain_ref, bias_ref, inb_ref, sw_ref, sb_ref, first_ref, inner_ref, fbias_ref, fout_ref,
    skip_ref, outb_ref, upb_ref, dnb_ref, net_s,
):
    net_s[...] = pack_ref[0:SHARED, :] + other_ref[...]
    for l in range(2):
        row = SHARED + LAYER_ROWS * l
        layer = slice(l, l + 1)
        for i, ref in enumerate((gain_ref, bias_ref)):
            low, high = NET + 2 * i, NET + 2 * i + 1
            if l == 0:
                value = jnp.where(at_ref[0] == 0, net_s[low : low + 1, :], net_s[high : high + 1, :])
            else:
                value = pack_ref[row + i : row + i + 1, :]
            ref[l, 0:1, :] = value
            ref[l, 1:2, :] = pack_ref[row + 2 + i : row + 3 + i, :]
        dnb_ref[layer, :] = pack_ref[row + 4 : row + 5, :]
        outb_ref[layer, :] = pack_ref[row + 5 : row + 6, :]
        for i in range(4):
            upb_ref[layer, i * C : (i + 1) * C] = pack_ref[row + 6 + i : row + 7 + i, :]
        for s in range(3):
            inb_ref[s, layer, :] = pack_ref[row + 10 + s : row + 11 + s, :]
            sb_ref[s, layer, :] = pack_ref[row + 22 + s : row + 23 + s, :]
            for j in range(3):
                sw_ref[j, s, layer, :] = pack_ref[row + 13 + 3 * j + s : row + 14 + 3 * j + s, :]
        skip_ref[layer, :] = pack_ref[row + 25 : row + 26, :]
        fout_ref[l] = pack_ref[row + 26 : row + 90, :]
        for i in range(2):
            inner_ref[l, i] = net_s[0:NET, i * 128 + l * NET : i * 128 + (l + 1) * NET]
        lanes = slice(256 + l * NET, 256 + (l + 1) * NET)
        for r in range(EMB):
            first_ref[r, layer, :] = net_s[r : r + 1, lanes]
        for i in range(3):
            fbias_ref[i, layer, :] = net_s[40 + i : 41 + i, lanes]


def sds(shape, dtype=F32):
    return jax.ShapeDtypeStruct(shape, dtype)


def params(us, mib=32):
    return dict(
        compiler_params=pltpu.CompilerParams(vmem_limit_bytes=mib * 2**20),
        cost_estimate=pl.CostEstimate(flops=int(us * 1e9), bytes_accessed=10000, transcendentals=0),
    )


SMEM = pl.BlockSpec(memory_space=pltpu.SMEM)
WHOLE = pl.BlockSpec(memory_space=pltpu.VMEM)
ANY = pl.BlockSpec(memory_space=pl.ANY)
SLOTS = pltpu.VMEM((C // 128, T, 128), F32)


def layer_of(x, l):
    rest = x.ndim - 1
    return pl.BlockSpec((1,) + x.shape[1:], lambda *_: (l,) + (0,) * rest, pipeline_mode=pl.Buffered(1))


def fixed(shape):
    return pl.BlockSpec(shape, lambda *_: (0,) * len(shape))


def spectrum_scratch():
    return [pltpu.VMEM((3 * H, C), BF)] * 2 + [pltpu.VMEM((T, C), F32)] * 2


def run_filter_backward(at, inner, out, sines, cosines, dks):
    return pl.pallas_call(
        filter_backward,
        in_specs=[SMEM] + [WHOLE] * 7,
        out_specs=[WHOLE] * 2,
        out_shape=[sds((2, NET, C)), sds((NET, C))],
        name="filter_backward",
        **params(5, 8),
    )(at, FEATS, inner, out, sines, cosines, *dks)


def run_arrange(at, own, other):
    return pl.pallas_call(
        arrange,
        in_specs=[SMEM, WHOLE, WHOLE],
        out_specs=WHOLE,
        out_shape=sds((T, D)),
        scratch_shapes=[SLOTS],
        name="arrange",
        **params(0.2, 6),
    )(at, own, other)


def run_finish_result(at, x, own, other, vec, l):
    return pl.pallas_call(
        finish_result,
        grid=(1,),
        in_specs=[SMEM, WHOLE, WHOLE, WHOLE, layer_of(vec, l)],
        out_specs=WHOLE,
        out_shape=sds((T, C), BF),
        scratch_shapes=[pltpu.VMEM((T, D), F32), SLOTS],
        name="finish_result",
        **params(2, 8),
    )(at, x, own, other, vec)


def run_finish_grad(at, g, own, other, x, vec, l):
    return pl.pallas_call(
        finish_grad,
        grid=(1,),
        in_specs=[SMEM, WHOLE, WHOLE, WHOLE, WHOLE, layer_of(vec, l)],
        out_specs=WHOLE,
        out_shape=sds((T, C)),
        scratch_shapes=[pltpu.VMEM((T, D), F32), SLOTS],
        name="finish_grad",
        **params(2.6, 8),
    )(at, g, own, other, x, vec)


def first_forward(
    at_ref, own_ref, other_ref, feats_ref, first_ref, inner_ref, bias_ref, out_ref,
    vec_ref, inw_ref, inb_ref, sw_ref, sb_ref, skip_ref, table_ref, outw_ref,
    x_ref, ks_ref, sin_ref, cos_ref, both_ref, wide_ref, u_ref, qs_ref, g_ref, p_ref,
    slots, first_s, bias_s, k_s, *scratch,
):
    rhs_e, rhs_o, se, so = scratch[3:7]
    filter_forward(
        at_ref, feats_ref, first_ref, inner_ref, bias_ref, out_ref, table_ref,
        ks_ref, sin_ref, cos_ref, both_ref, wide_ref, first_s, bias_s, k_s, rhs_e, rhs_o, se, so,
    )
    arrange(at_ref, own_ref, other_ref, x_ref, slots)
    mixer_forward(
        0, False, at_ref, x_ref, vec_ref, inw_ref, inb_ref, sw_ref, sb_ref, ks_ref, skip_ref, table_ref, outw_ref,
        u_ref, qs_ref, g_ref, p_ref, *scratch,
    )


def mixer_forward_scratch():
    return (
        [pltpu.VMEM((T, D), BF), pltpu.VMEM((T, C), F32), pltpu.VMEM((T, C), F32)]
        + spectrum_scratch()
        + [pltpu.VMEM((6 * H, C), BF)] * 2
        + [pltpu.VMEM((T, C), BF)]
    )


def run_first_forward(at, own, other, filters, vec, inw, inb, sw, sb, skip, outw):
    args = [at, own, other, FEATS, *filters, vec, inw, inb, sw, sb, skip, TABLE, outw]
    outs = [
        sds((T, D)), sds((2, 4, H, C)), sds((3, T, 128)), sds((3, T, 128)), sds((2, 128, 128)), sds((2, 128, C)),
        sds((T, 3 * C)), sds((4, H, C)), sds((T, C)), sds((T, D), BF),
    ]
    return pl.pallas_call(
        first_forward,
        in_specs=[SMEM] + [WHOLE] * (len(args) - 1),
        out_specs=[WHOLE] * len(outs),
        out_shape=outs,
        scratch_shapes=[SLOTS, pltpu.VMEM((128, 128), F32), pltpu.VMEM((8, 128), F32), pltpu.VMEM((T, C), F32)]
        + mixer_forward_scratch(),
        name="first_forward",
        **params(13, 14),
    )(*args)


def run_mixer_forward(l, joint, at, x, vec, inw, inb, sw, sb, ks, skip, outw):
    joined = joint is not None
    args = [at, x] + (list(joint) + [vec] if joined else [])
    args += [vec, inw, inb, sw, sb, ks, skip, TABLE, outw]
    outs = ([sds((T, D))] if joined else []) + [sds((T, 3 * C)), sds((4, H, C)), sds((T, C)), sds((T, D), BF)]
    return pl.pallas_call(
        functools.partial(mixer_forward, l, joined),
        in_specs=[SMEM] + [WHOLE] * (len(args) - 1),
        out_specs=[WHOLE] * len(outs),
        out_shape=outs,
        scratch_shapes=mixer_forward_scratch(),
        name="mixer_forward",
        **params(6, 10),
    )(*args)


FC = 768


def run_ff_forward(l, last, at, x, own, other, vec, up, upb, dn, after):
    return pl.pallas_call(
        functools.partial(body_without, functools.partial(ff_forward, l, last), 8, len(after)),
        in_specs=[SMEM] + [WHOLE] * 7 + [ANY] * len(after),
        out_specs=[WHOLE] * (4 if last else 3),
        out_shape=[sds((T, D)), sds((T, FH))] + ([sds((T, C), BF)] * 2 if last else [sds((T, D), BF)]),
        scratch_shapes=[pltpu.VMEM((T, D), BF), pltpu.VMEM((T, D), F32)],
        name="ff_forward",
        **params(6, 16),
    )(at, x, own, other, vec, up, upb, dn, *after)


def run_ff_backward(l, at, g, joint, x, h, vec, up, dn, after):
    joined = joint is not None
    args = [at, g] + (list(joint) if joined else []) + [vec, x, h, up, dn]
    outs = [sds((T, D))] if joined else []
    outs += [sds((T, WIDE), BF), sds((T, WIDE), BF), sds((8, C)), sds((T, D), BF)]
    return pl.pallas_call(
        functools.partial(body_without, functools.partial(ff_backward, l, joined), len(args), len(after)),
        in_specs=[SMEM] + [WHOLE] * (len(args) - 1) + [ANY] * len(after),
        out_specs=[WHOLE] * len(outs),
        out_shape=outs,
        scratch_shapes=[pltpu.VMEM((T, D), BF), pltpu.VMEM((T, D), F32)],
        name="ff_backward",
        **params(8, 16),
    )(*args, *after)


def run_ff_weights(at, mine, got):
    return pl.pallas_call(
        ff_weights,
        in_specs=[SMEM, WHOLE, WHOLE],
        out_specs=[WHOLE] * 4,
        out_shape=[sds((4, PIECE, D), BF)] * 4,
        name="ff_weights",
        **params(3, 12),
    )(at, mine, got)


def run_mixer_backward(l, last, at, g_in, own, other, x1, x0, u, qs, g, ks, vec, inw, outw, sw, sb, skip, after):
    args = [at, g_in, own, other, x1, x0, u, qs, g, ks, vec, inw, outw, sw, sb, skip, TABLE]
    outs = [
        sds((T, D)), sds((24, C)), sds((T, C)), sds((T, D), BF), sds((T, WIDE), BF), sds((T, WIDE), BF),
    ]
    tc = pltpu.VMEM((T, C), F32)
    return pl.pallas_call(
        functools.partial(body_without, functools.partial(mixer_backward, l, last), len(args), len(after)),
        in_specs=[SMEM] + [WHOLE] * (len(args) - 1) + [ANY] * len(after),
        out_specs=[WHOLE] * len(outs),
        out_shape=outs,
        scratch_shapes=[
            pltpu.VMEM((T, D), BF), pltpu.VMEM((T, D), BF), pltpu.VMEM((T, C), BF), pltpu.VMEM((T, 3 * C), BF),
            tc, tc, tc, tc, tc, *spectrum_scratch(),
            pltpu.VMEM((6 * H, 2 * C), BF), pltpu.VMEM((6 * H, 2 * C), BF), pltpu.VMEM((T, 2 * C), F32),
        ],
        name="mixer_backward",
        **params(10, 19),
    )(*args, *after)


def run_mixer_weights(at, mine, got, pack):
    rows = PIECE + (16 if pack else 0)
    return pl.pallas_call(
        functools.partial(mixer_weights, bool(pack)),
        in_specs=[SMEM] + [WHOLE] * (2 + len(pack)),
        out_specs=[WHOLE] * 4,
        out_shape=[sds((4, rows, C), BF)] * 4,
        name="mixer_weights",
        **params(2.4, 12),
    )(at, mine, got, *pack)


def run_add(parts, count, after=(), sides=1):
    shape = parts[0].shape[1:] if count > 1 else parts[0].shape
    width = sum(p.shape[-1] for p in parts[:: len(parts) // sides])
    made = pl.pallas_call(
        functools.partial(body_without, functools.partial(add_parts, len(parts), sides), len(parts), len(after)),
        in_specs=[WHOLE] * len(parts) + [ANY] * len(after),
        out_specs=[WHOLE] * count,
        out_shape=[sds(shape[:-1] + (width,), BF)] * count,
        name="add_parts",
        **params(0.6, 8),
    )(*parts, *after)
    return list(made)


def run_behind(arrays, after, mib=4, us=0.1):
    count = len(arrays)
    return pl.pallas_call(
        lambda *refs: None,
        in_specs=[ANY] * (count + len(after)),
        out_specs=[ANY] * count,
        out_shape=[sds(x.shape, x.dtype) for x in arrays],
        input_output_aliases={i: i for i in range(count)},
        name="behind",
        **params(us, mib),
    )(*arrays, *after)


def run_place(body, at, ins, place, into, shapes, out_specs, steps, width, name):
    aliases = {} if into is None else {3: 0, 4: 1}
    into = [] if into is None else list(into)
    return pl.pallas_call(
        functools.partial(body_without, body, 3, len(into)),
        grid=(steps,),
        in_specs=[SMEM] + [lane_block(m.shape, width, place) for m in ins] + [ANY] * len(into),
        out_specs=out_specs + [fixed((8, 128))],
        out_shape=[sds(s) for s in shapes] + [sds((8, 128))],
        scratch_shapes=[pltpu.VMEM((4 * PIECE, width), BF)],
        input_output_aliases=aliases,
        name=name,
        **params(5, 20),
    )(at, *ins, *into)


def lane_block(shape, width, place):
    return pl.BlockSpec(shape[:-1] + (width,), lambda *_: (0,) * (len(shape) - 1) + (place,))


def body_without(body, first, count, *refs):
    body(*refs[:first], *refs[first + count :])


def run_place_ff(l, layers, at, ins, place, into):
    specs = [
        pl.BlockSpec((1, D, 4 * PIECE), lambda p: (l, 0, p)),
        pl.BlockSpec((1, 4 * PIECE, D), lambda p: (l, p, 0)),
    ]
    return run_place(place_ff, at, ins, place, into, [(layers, D, FH), (layers, FH, D)], specs, 4, D, "place_ff")


def run_place_mixer(l, layers, at, ins, place, into):
    packed = ins[0].shape[-2] > PIECE
    specs = [
        pl.BlockSpec((1, 1, D, C), lambda n: (l, jnp.minimum(n, 2), 0, 0)),
        pl.BlockSpec((1, C, D), lambda n: (l, 0, 0)),
    ] + [fixed((PACK, C))] * packed
    shapes = [(layers, 3, D, C), (layers, C, D)] + [(PACK, C)] * packed
    body = functools.partial(place_mixer, packed)
    return run_place(body, at, ins, place, into, shapes, specs, 4, C, "place_mixer")


SWAP = [(0, 1), (1, 0)]


def swap(x, axis):
    return lax.ppermute(x, axis, SWAP)


def shift(x, axis, k):
    pairs = []
    for y, x_at, c in np.ndindex(4, 4, 2):
        along_x = (axis == FIRST) == (c == 0)
        to = (y, (x_at + k) % 4) if along_x else ((y + k) % 4, x_at)
        pairs.append(((y * 4 + x_at) * 2 + c, (to[0] * 4 + to[1]) * 2 + c))
    return lax.ppermute(x, ("y", "x", "c"), pairs)


def send_first(blocks):
    return [blocks[0]] + [shift(blocks[k], FIRST, k) for k in range(1, 4)]


def sum_first(*gradients, after=()):
    return run_add([p for came in gradients for p in came], 4, after, len(gradients))


def send_second(pieces):
    return [pieces[0]] + [shift(pieces[m], SECOND, m) for m in range(1, 4)]


def sum_second(came, after=()):
    return run_add(came, 1, after)[0]


def sum_near(piece, after=()):
    return run_add([piece, swap(piece, "zl")], 1, after)[0]


def gather_second(piece, after):
    came = [shift(piece, SECOND, m) for m in range(1, 4)]
    return jnp.stack([piece] + list(run_behind(came, after)))


def gather_first(row, after):
    came = [shift(row, FIRST, k) for k in range(1, 4)]
    return jnp.stack([row] + list(run_behind(came, after)))


def gather_plane(piece, after):
    mine = lax.all_gather(piece, ("y", "x"), axis=0, tiled=False)
    mine = mine.reshape(1, 4, 4, *piece.shape)
    [mine] = run_behind([mine], after, 56)
    return [mine, swap(mine, "c")]


def run_pack_small(at, gnet, gout, small):
    return pl.pallas_call(
        pack_small,
        in_specs=[SMEM] + [WHOLE] * (2 + len(small)),
        out_specs=[WHOLE] * 2,
        out_shape=[sds((PACK // 2, C))] * 2,
        scratch_shapes=[pltpu.VMEM((PACK, C), F32)],
        name="pack_small",
        **params(0.6, 4),
    )(at, gnet, gout, *small)


def run_unpack_small(at, pack, other):
    shapes = [
        (2, 2, C), (2, 2, C), (3, 2, C), (3, 3, 2, C), (3, 2, C), (EMB, 2, NET), (2, 2, NET, NET), (3, 2, NET),
        (2, NET, C), (2, C), (2, C), (2, FH), (2, C),
    ]
    return pl.pallas_call(
        unpack_small,
        in_specs=[SMEM, WHOLE, WHOLE],
        out_specs=[WHOLE] * len(shapes),
        out_shape=[sds(s) for s in shapes],
        scratch_shapes=[pltpu.VMEM((SHARED, C), F32)],
        name="unpack_small",
        **params(2, 4),
    )(at, pack, other)


def shards(
    tokens, lengths, norm_gain, norm_bias, in_weight, in_bias, short_weight, short_bias, filter_first, filter_inner,
    filter_biases, filter_out, filter_skip, out_weight, out_bias, up_weight, up_bias, down_weight, down_bias, cotangent,
):
    layers = norm_gain.shape[0]
    half_at = lax.axis_index("zh")
    core = lax.axis_index("c")
    x_at, y_at = lax.axis_index("x"), lax.axis_index("y")
    order = jnp.where(core == 0, x_at, y_at), jnp.where(core == 0, y_at, x_at)
    at = jnp.stack([half_at, lengths[0], x_at, y_at, core, *order]).astype(jnp.int32)

    tokens_other = swap(tokens, "zh")
    rows = jnp.stack(
        [norm_gain[:, 0], norm_bias[:, 0], norm_gain[:, 1], norm_bias[:, 1], out_bias, down_bias, out_bias, out_bias], 1
    )
    inw = in_weight.transpose(0, 2, 1, 3)
    at, rows, cotangent = run_behind([at, rows, cotangent], [], 4, 12)
    other = swap(rows, "zh")
    low = half_at == 0
    vec = jnp.concatenate([jnp.where(low, rows, other), jnp.where(low, other, rows)], 2)

    inb = in_bias.reshape(layers, 1, 3 * C)
    sw = short_weight.reshape(layers, 3, 3 * C)
    sb = short_bias.reshape(layers, 1, 3 * C)
    skip = filter_skip.reshape(layers, 1, C)
    upb = up_bias.reshape(layers, 1, FH)

    cot_other = swap(cotangent, "zh")
    grad = run_arrange(at, cotangent, cot_other)
    saved = []
    joint = None
    for l in range(layers):
        if l == 0:
            filters = filter_first, filter_inner, filter_biases, filter_out
            made = run_first_forward(at, tokens, tokens_other, filters, vec, inw, inb, sw, sb, skip, out_weight)
            x, ks, sines, cosines, inner, fout, *made = made
        else:
            x, *made = run_mixer_forward(l, joint, at, x, vec, inw, inb, sw, sb, ks, skip, out_weight)
        u, qs, g, p = made
        if l == 0:
            [p] = run_behind([p], [cot_other], 4, 5)
        after = [grad] if l == 0 else []
        last = l == layers - 1
        x1, h, *p2 = run_ff_forward(l, last, at, x, p, swap(p, "zh"), vec, up_weight, upb, down_weight, after)
        saved.append((x, u, qs, g, x1, h))
        joint = p2[0], swap(p2[-1], "zh")
        x = x1
    last_branch = joint

    joint = None
    small = [None] * layers
    waits = []
    came = {}
    for l in reversed(range(layers)):
        x0, u, qs, g, x1, h = saved[l]
        made = run_ff_backward(l, at, grad, joint, x1, h, vec, up_weight, down_weight, waits)
        if joint is not None:
            grad, made = made[0], made[1:]
        keep, give, ff_small, p = made
        p, give = run_behind([p, give], [last_branch[1]] if l == layers - 1 else came["mixer", l + 1][1:])
        p_other = swap(p, "zh")
        halves = run_ff_weights(at, keep, swap(give, "c"))
        came["ff", l] = send_first(halves)
        waits = list(halves)
        if l < layers - 1:
            later = send_second(sum_first(came["ff", l + 1], came["mixer", l + 1], after=[p]))
            later = sum_second(later)
            waits.append(later)
            later_other = swap(later, "zl")
        made = run_mixer_backward(
            l, l == 0, at, grad, p, p_other, x1, x0, u, qs, g, ks, vec, inw, out_weight, sw, sb, skip, waits
        )
        grad, mixer_small, dk, p, keep, give = made
        p, give = run_behind([p, give], came["ff", l][1:] + ([later_other] if l < layers - 1 else []))
        joint = (p, swap(p, "zh"), x0) if l else (p, x0)
        small[l] = (ff_small, mixer_small, dk)
        pack = ()
        if l == 0:
            later = run_add([later, later_other], 1, [p])[0]
            ff = sum_second(send_second(sum_first(came["ff", 0], after=[p])))
            gfout, gnet = run_filter_backward(at, inner, fout, sines, cosines, [s[-1] for s in small])
            gfout, gnet = run_behind([gfout, gnet], [ff])
            pack = run_pack_small(at, gnet, gfout, [m for some in small for m in some[:-1]])
            pack = pack[0], swap(pack[1], "c")
            ff = sum_near(ff, pack[1:])
        halves = run_mixer_weights(at, keep, swap(give, "c"), pack)
        came["mixer", l] = send_first(halves)
        waits = list(halves)
        if l == layers - 1:
            result = run_finish_result(at, saved[l][4], *last_branch, vec, l)
            waits.append(result)

    mixer = sum_near(sum_second(send_second(sum_first(came["mixer", 0], after=[ff]))))
    later = gather_plane(later, [mixer])
    p, x0 = joint
    [p] = run_behind([p], [mixer])
    last = jnp.concatenate([jnp.pad(ff, ((0, mixer.shape[0] - PIECE), (0, 0))), mixer], 1)
    last = gather_second(last, [])
    *ff_out, mark = run_place_ff(1, layers, at, later, 0, None)
    *mixer_out, other_mark = run_place_mixer(1, layers, at, later, 2, None)
    grad = run_finish_grad(at, grad, p, swap(p, "zh"), x0, vec, 0)
    last = gather_first(last, [grad, mark, other_mark])
    last = [last, swap(last, "c")]
    *mixer_out, pack, mark = run_place_mixer(0, layers, at, last, 2, mixer_out)
    *ff_out, mark = run_place_ff(0, layers, at, last, 0, ff_out)

    gain, shift_, inb, sw, sb, first, inner, fbias, fout, skip, outb, upb, dnb = run_unpack_small(
        at, pack, swap(pack[:SHARED], "zh")
    )
    return (
        result, grad, gain, shift_, mixer_out[0].transpose(0, 2, 1, 3), inb.transpose(1, 0, 2),
        sw.transpose(2, 0, 1, 3), sb.transpose(1, 0, 2), first.transpose(1, 0, 2), inner, fbias.transpose(1, 0, 2),
        fout, skip, mixer_out[1], outb, ff_out[0], upb, ff_out[1], dnb,
    )


def solution(mesh):
    names = ("zl", "y", "x", "c", "zh")
    fine = Mesh(mesh.devices.reshape(2, 4, 4, 2, 2), names)
    dp = ("zl", "y", "x", "c")
    rows = P(dp, "zh")
    third, fourth = P(None, None, "zh"), P(None, None, None, "zh")
    second, middle = P(None, "zh"), P(None, "zh", None)
    placed = (
        rows, P(dp), third, third, fourth, third, fourth, third, P(), P(), P(), third, second, middle, second, third,
        second, middle, second, rows,
    )
    return jax.shard_map(
        shards,
        mesh=fine,
        in_specs=placed,
        out_specs=(
            rows, rows, third, third, fourth, third, fourth, third, P(), P(), P(), third, second, middle, second, third,
            second, middle, second,
        ),
        check_vma=False,
    )
```

```python
import functools
import math

import jax
import jax.numpy as jnp
import ml_dtypes
import numpy as np
from jax import lax
from jax.experimental import pallas as pl
from jax.experimental.pallas import tpu as pltpu
from jax.sharding import Mesh
from jax.sharding import PartitionSpec as P

D = 768
T = 512
H = T // 2
C = 384
FH = 1536
NET = 64
EMB = 33
BANDS = 16
PIECE = 96
EPSILON = 1e-05
HIGH = lax.Precision.HIGHEST
F32 = jnp.float32
BF = jnp.bfloat16

ORDER = np.concatenate([np.arange(0, T, 2), np.arange(1, T, 2)])


def split_table(t):
    hi = t.astype(ml_dtypes.bfloat16)
    lo = (t - hi.astype(np.float64)).astype(ml_dtypes.bfloat16)
    return hi, lo


def wave_tables():
    n = np.arange(H)
    even = 2 * math.pi * (np.outer(n, 2 * n) % (2 * T)) / (2 * T)
    odd = 2 * math.pi * (np.outer(n, 2 * n + 1) % (2 * T)) / (2 * T)
    alt = np.where(n % 2 == 0, 1.0, -1.0)
    out = []
    for ang in (even, odd):
        co, si = np.cos(ang), np.sin(ang)
        si[0] = alt
        hi, lo = split_table(np.concatenate([co, si], 0))
        out.append(np.concatenate([hi, lo, hi], 1))
        hi, lo = split_table(np.concatenate([co.T, si.T], 1))
        out.append(np.concatenate([hi, lo, hi], 1))
    fe, ie, fo, io = out
    return np.concatenate([fe, fo, np.concatenate([ie, io], 0)], 1)


TABLE = wave_tables()
FORWARD_EVEN = slice(None), slice(0, 3 * H)
FORWARD_ODD = slice(None), slice(3 * H, 6 * H)
INVERSE_EVEN = slice(0, H), slice(6 * H, 12 * H)
INVERSE_ODD = slice(H, 2 * H), slice(6 * H, 12 * H)


def slot_features():
    slots = ORDER.astype(np.float64)
    freqs = 0.0001 + (BANDS - 1 - 0.0001) * np.arange(BANDS) / (BANDS - 1)
    angle = 2 * math.pi * slots[:, None] * freqs[None, :] / T
    times = (slots / (T - 1))[:, None]
    feats = np.concatenate([times, np.cos(angle), -np.sin(angle), np.zeros((T, 128 - EMB))], 1)
    return feats.astype(np.float32)


FEATS = slot_features()


def dot(a, b):
    return lax.dot_general(a, b, (((1,), (0,)), ((), ())), preferred_element_type=F32)


def dot_nt(a, b):
    return lax.dot_general(a, b, (((1,), (1,)), ((), ())), preferred_element_type=F32)


def dot_tn(a, b):
    return lax.dot_general(a, b, (((0,), (0,)), ((), ())), preferred_element_type=F32)


def normalize(x):
    mean = jnp.mean(x, -1, keepdims=True)
    scale = lax.rsqrt(jnp.mean(x * x, -1, keepdims=True) - mean * mean + EPSILON)
    return (x - mean) * scale, scale


def norm_pull(dn, x, gain):
    xhat, scale = normalize(x)
    ds = dn * gain
    first = jnp.mean(ds, -1, keepdims=True)
    second = jnp.mean(ds * xhat, -1, keepdims=True)
    return scale * (ds - first - xhat * second), dn * xhat


def row_mask(start, rows, length):
    r = start + lax.broadcasted_iota(jnp.int32, (rows, 1), 0)
    slot = jnp.where(r < H, 2 * r, 2 * (r - H) + 1)
    return (slot < length).astype(F32)


def down_one(x):
    r = lax.broadcasted_iota(jnp.int32, x.shape, 0)
    return jnp.where(r == 0, 0.0, pltpu.roll(x, 1, 0))


def up_one(x):
    r = lax.broadcasted_iota(jnp.int32, x.shape, 0)
    return jnp.where(r == x.shape[0] - 1, 0.0, pltpu.roll(x, x.shape[0] - 1, 0))


def put_split(ref, value, rows, lanes):
    hi = value.astype(BF)
    lo = (value - hi.astype(F32)).astype(BF)
    step = ref.shape[0] // 3
    ref[pl.ds(rows, value.shape[0]), lanes] = hi
    ref[pl.ds(step + rows, value.shape[0]), lanes] = hi
    ref[pl.ds(2 * step + rows, value.shape[0]), lanes] = lo


def top_row(shape):
    return lax.broadcasted_iota(jnp.int32, shape, 0) == 0


def butterfly(even, odd, lanes):
    ce, se = even[pl.ds(0, H), lanes], even[pl.ds(H, H), lanes]
    co, so = odd[pl.ds(0, H), lanes], odd[pl.ds(H, H), lanes]
    top = top_row(ce.shape)
    return ce + co, ce - co, jnp.where(top, se, se + so), jnp.where(top, so, se - so)


def spectrum_product(a, k, conj):
    a1, a2, b1, b2 = a
    k1, k2, l1, l2 = k
    top = top_row(a1.shape)
    aa, bb, cc, dd = a1 * k1, b1 * l1, a2 * k2, b2 * l2
    if conj:
        y1 = jnp.where(top, aa, aa + bb)
        y2 = jnp.where(top, cc, cc + dd)
        m1 = jnp.where(top, bb + dd, b1 * k1 - a1 * l1)
        m2 = jnp.where(top, b2 * l1 - b1 * l2, b2 * k2 - a2 * l2)
    else:
        y1 = jnp.where(top, aa, aa - bb)
        y2 = jnp.where(top, cc, cc - dd)
        m1 = jnp.where(top, bb - dd, a1 * l1 + b1 * k1)
        m2 = jnp.where(top, b1 * l2 + b2 * l1, a2 * l2 + b2 * k2)
    return y1, y2, m1, m2


def put_inverse(rhs_e, rhs_o, y, lanes):
    y1, y2, m1, m2 = y
    top = top_row(y1.shape)
    unit = 1.0 / T
    w = jnp.where(top, 0.5 * unit, unit)
    put_split(rhs_e, (y1 + y2) * w, 0, lanes)
    put_split(rhs_o, (y1 - y2) * w, 0, lanes)
    put_split(rhs_e, jnp.where(top, m1, m1 + m2) * unit, H, lanes)
    put_split(rhs_o, jnp.where(top, m2, m1 - m2) * unit, H, lanes)


def lanes_of(block):
    return pl.ds(block * 128, 128)


def short_conv(u_ref, sw_ref, sb_ref, block):
    out = []
    for s in range(3):
        at = lanes_of(s * (C // 128) + block)
        ue, uo = u_ref[pl.ds(0, H), at], u_ref[pl.ds(H, H), at]
        t0, t1, t2 = (sw_ref[j : j + 1, at] for j in range(3))
        bias = sb_ref[0:1, at]
        uo_d = down_one(uo)
        we = t2 * ue + t1 * uo_d + t0 * down_one(ue) + bias
        wo = t2 * uo + t1 * ue + t0 * uo_d + bias
        out.append((we, wo))
    return out


def hdot(a, b, dims=(1, 0)):
    return lax.dot_general(
        a, b, (((dims[0],), (dims[1],)), ((), ())), precision=HIGH, preferred_element_type=F32
    )


def decay_of(half_at, feats_ref):
    slow = math.log(0.01) / 1.5
    fast = math.log(0.01) / 0.3
    channel = (half_at * C + lax.broadcasted_iota(jnp.int32, (1, C), 1)).astype(F32)
    rates = jnp.abs(slow + (fast - slow) * channel / (D - 1))
    return jnp.exp(-feats_ref[:, 0:1] * rates) + 0.05


def sin_cos(x):
    k = jnp.floor(x * (2 / math.pi) + 0.5)
    r = ((x - k * 1.5703125) - k * 4.837512969970703125e-4) - k * 7.54978995489188e-8
    rr = r * r
    sine = r + r * rr * (-1.6666654611e-1 + rr * (8.3321608736e-3 + rr * -1.9515295891e-4))
    cosine = 1.0 - 0.5 * rr + rr * rr * (
        4.166664568298827e-2 + rr * (-1.388731625493765e-3 + rr * 2.443315711809948e-5)
    )
    quarter = k - 4.0 * jnp.floor(k * 0.25)
    odd = (quarter == 1.0) | (quarter == 3.0)
    s = jnp.where(odd, cosine, sine)
    c = jnp.where(odd, sine, cosine)
    return jnp.where(quarter >= 2.0, -s, s), jnp.where((quarter == 1.0) | (quarter == 2.0), -c, c)


def filter_forward(
    at_ref, feats_ref, first_ref, inner_ref, bias_ref, out_ref, table_ref,
    ks_ref, sin_ref, cos_ref, both_ref, wide_ref, first_s, bias_s, k_s, rhs_e, rhs_o, se, so,
):
    for ref in (both_ref, wide_ref, first_s, bias_s):
        ref[...] = jnp.zeros_like(ref)
    for l in range(2):
        at = pl.ds(l * NET, NET)
        first_s[0:EMB, at] = first_ref[l]
        bias_s[0:3, at] = bias_ref[l]
        wide_ref[l, at, :] = out_ref[l]
        for i in range(2):
            both_ref[i, at, at] = inner_ref[l, i]
    low = feats_ref[...]
    for i in range(3):
        weight = first_s[...] if i == 0 else both_ref[i - 1]
        low, cosine = sin_cos(hdot(low, weight) + bias_s[i : i + 1, :])
        sin_ref[i] = low
        cos_ref[i] = cosine
    decay = decay_of(at_ref[0], feats_ref)
    for l in range(2):
        k_s[...] = hdot(sin_ref[2], wide_ref[l]) * decay
        for b in range(C // 128):
            at = lanes_of(b)
            put_split(rhs_e, k_s[pl.ds(0, H), at], 0, at)
            put_split(rhs_o, k_s[pl.ds(H, H), at], 0, at)
        se[...] = dot(table_ref[FORWARD_EVEN], rhs_e[...])
        so[...] = dot(table_ref[FORWARD_ODD], rhs_o[...])
        for b in range(C // 128):
            at = lanes_of(b)
            for i, v in enumerate(butterfly(se, so, at)):
                ks_ref[l, i, :, at] = v


def filter_backward(at_ref, feats_ref, inner_ref, out_ref, sin_ref, cos_ref, dk0_ref, dk1_ref, gout_ref, gnet_ref):
    decay = decay_of(at_ref[0], feats_ref)
    ds = jnp.zeros((T, 128), F32)
    for l, dk_ref in enumerate((dk0_ref, dk1_ref)):
        dk = dk_ref[...] * decay
        gout_ref[l] = hdot(sin_ref[2], dk, (0, 0))[l * NET : (l + 1) * NET]
        ds += hdot(dk, out_ref[l], (1, 1))
    lane = lax.broadcasted_iota(jnp.int32, (NET, 128), 1)
    gnet_ref[...] = jnp.zeros_like(gnet_ref)
    for i in (2, 1, 0):
        da = ds * cos_ref[i]
        gnet_ref[40 + i : 41 + i, pl.ds(256, 128)] = jnp.sum(da, 0, keepdims=True)
        if i > 0:
            block = hdot(sin_ref[i - 1], da, (0, 0))
            gnet_ref[:, pl.ds((i - 1) * 128, 128)] = jnp.where(lane < NET, block[:NET], block[NET:])
            ds = hdot(da, inner_ref[i - 1], (1, 1))
        else:
            gnet_ref[0:40, pl.ds(256, 128)] = hdot(feats_ref[...], da, (0, 0))[0:40]


def arrange(at_ref, own_ref, other_ref, out_ref, tmp):
    for half, first in ((0, own_ref), (1, other_ref)):
        for b in range(C // 128):
            tmp[b] = first[:, lanes_of(b)].astype(F32)

        def put(first_lane):
            for b in range(C // 128):
                to = pl.ds(first_lane + b * 128, 128)
                out_ref[pl.ds(0, H), to] = tmp[b, pl.ds(0, H, stride=2), :]
                out_ref[pl.ds(H, H), to] = tmp[b, pl.ds(1, H, stride=2), :]

        pl.when(at_ref[0] == half)(functools.partial(put, 0))
        pl.when(at_ref[0] != half)(functools.partial(put, C))


def my_lanes(at_ref, row):
    return jnp.where(at_ref[0] == 0, row[:, :C], row[:, C:])


def by_slot(at_ref, src_ref, out_ref, tmp):
    def put(first_lane):
        for b in range(C // 128):
            lanes = pl.ds(first_lane + b * 128, 128)
            tmp[b, pl.ds(0, H, stride=2), :] = src_ref[pl.ds(0, H), lanes]
            tmp[b, pl.ds(1, H, stride=2), :] = src_ref[pl.ds(H, H), lanes]

    pl.when(at_ref[0] == 0)(functools.partial(put, 0))
    pl.when(at_ref[0] != 0)(functools.partial(put, C))
    for b in range(C // 128):
        out_ref[:, lanes_of(b)] = tmp[b].astype(out_ref.dtype)


def finish_result(at_ref, x_ref, own_ref, other_ref, vec_ref, out_ref, y_s, tmp):
    def put(first_lane):
        lanes = pl.ds(first_lane, C)

        def body(start, c):
            rows = pl.ds(start, RB)
            y = own_ref[rows, :].astype(F32) + other_ref[rows, :].astype(F32) + vec_ref[0, 5:6, lanes]
            y_s[rows, lanes] = x_ref[rows, lanes] + row_mask(start, RB, at_ref[1]) * y
            return c

        row_loop(body)

    pl.when(at_ref[0] == 0)(functools.partial(put, 0))
    pl.when(at_ref[0] != 0)(functools.partial(put, C))
    by_slot(at_ref, y_s, out_ref, tmp)


def finish_grad(at_ref, g_ref, own_ref, other_ref, x_ref, vec_ref, out_ref, x_s, tmp):
    def body(start, c):
        at = pl.ds(start, RB)
        dn = own_ref[at, :].astype(F32) + other_ref[at, :].astype(F32)
        x_s[at, :] = g_ref[at, :] + norm_pull(dn, x_ref[at, :], vec_ref[0, 0:1, :])[0]
        return c

    row_loop(body)
    by_slot(at_ref, x_s, out_ref, tmp)


def add_branch(x_ref, own_ref, other_ref, vec_ref, row, length, start, rows):
    at = pl.ds(start, rows)
    y = own_ref[at, :].astype(F32) + other_ref[at, :].astype(F32) + vec_ref[row : row + 1, :]
    return x_ref[at, :] + row_mask(start, rows, length) * y


RB = 128


def row_loop(body, init=0):
    def step(i, c):
        return body(pl.multiple_of(i * RB, RB), c)

    return lax.fori_loop(0, T // RB, step, init)


def mixer_forward(l, joined, *refs):
    at_ref, x_ref = refs[:2]
    refs = refs[2:]
    if joined:
        own_ref, other_ref, prev_ref = refs[:3]
        refs = refs[3:]
    (vec_ref, inw_ref, inb_ref, sw_ref, sb_ref, ks_ref, skip_ref, table_ref, outw_ref) = refs[:9]
    refs = refs[9:]
    if joined:
        xo_ref = refs[0]
        refs = refs[1:]
    u_ref, qs_ref, g_ref, p_ref, a_s, w0_s, q_s, rhs_e, rhs_o, se, so, rhs2_e, rhs2_o, z_s = refs

    def first(start, c):
        at = pl.ds(start, RB)
        if joined:
            x = add_branch(x_ref, own_ref, other_ref, prev_ref.at[l - 1], 5, at_ref[1], start, RB)
            xo_ref[at, :] = x
        else:
            x = x_ref[at, :]
        xhat, _ = normalize(x)
        a_s[at, :] = (xhat * vec_ref[l, 0:1, :] + vec_ref[l, 1:2, :]).astype(BF)
        return c

    row_loop(first)
    for s in range(3):
        at = pl.ds(s * C, C)
        u_ref[:, at] = dot(a_s[...], inw_ref[l, s]) + inb_ref[l, 0:1, at]
    for b in range(C // 128):
        at = lanes_of(b)
        (w0e, w0o), (w1e, w1o), (w2e, w2o) = short_conv(u_ref, sw_ref.at[l], sb_ref.at[l], b)
        w0_s[pl.ds(0, H), at] = w0e
        w0_s[pl.ds(H, H), at] = w0o
        qe, qo = w2e * w1e, w2o * w1o
        q_s[pl.ds(0, H), at] = qe
        q_s[pl.ds(H, H), at] = qo
        put_split(rhs_e, qe, 0, at)
        put_split(rhs_o, qo, 0, at)
    se[...] = dot(table_ref[FORWARD_EVEN], rhs_e[...])
    so[...] = dot(table_ref[FORWARD_ODD], rhs_o[...])
    for b in range(C // 128):
        at = lanes_of(b)
        spec = butterfly(se, so, at)
        for i, v in enumerate(spec):
            qs_ref[i, :, at] = v
        y = spectrum_product(spec, [ks_ref[l, i, :, at] for i in range(4)], False)
        put_inverse(rhs2_e, rhs2_o, y, at)
    se[pl.ds(0, H), :] = dot(table_ref[INVERSE_EVEN], rhs2_e[...])
    se[pl.ds(H, H), :] = dot(table_ref[INVERSE_ODD], rhs2_o[...])

    def last(start, c):
        at = pl.ds(start, RB)
        g = se[at, :] + skip_ref[l, 0:1, :] * q_s[at, :]
        g_ref[at, :] = g
        z_s[at, :] = (g * w0_s[at, :]).astype(BF)
        return c

    row_loop(last)
    p_ref[...] = dot(z_s[...], outw_ref[l]).astype(BF)


def gelu_parts(h):
    c0 = math.sqrt(2 / math.pi)
    hh = h * h
    t = jnp.tanh(c0 * (h + 0.044715 * (hh * h)))
    half = 0.5 * (1.0 + t)
    return half, t, hh, c0


def ff_forward(l, last, at_ref, x_ref, own_ref, other_ref, vec_ref, up_ref, upb_ref, dn_ref, xo_ref, h_ref, *refs):
    *p_refs, b_s, acc = refs

    def first(start, c):
        at = pl.ds(start, RB)
        x = add_branch(x_ref, own_ref, other_ref, vec_ref.at[l], 4, at_ref[1], start, RB)
        xo_ref[at, :] = x
        xhat, _ = normalize(x)
        b_s[at, :] = (xhat * vec_ref[l, 2:3, :] + vec_ref[l, 3:4, :]).astype(BF)
        return c

    row_loop(first)
    for j in range(FH // FC):
        part = slice(j * FC, (j + 1) * FC)
        h = dot(b_s[...], up_ref[l, :, part]) + upb_ref[l, :, part]
        h_ref[:, part] = h
        half, _, _, _ = gelu_parts(h)
        total = dot((h * half).astype(BF), dn_ref[l, part, :])
        if j == 0:
            acc[...] = total
        else:
            acc[...] += total
    if not last:
        p_refs[0][...] = acc[...].astype(BF)
    else:
        low, high = acc[:, :C].astype(BF), acc[:, C:].astype(BF)
        own = at_ref[0] == 0
        p_refs[0][...] = jnp.where(own, low, high)
        p_refs[1][...] = jnp.where(own, high, low)


def put_by_core(at_ref, keep_ref, give_ref, at, low, high):
    @pl.when(at_ref[4] == 0)
    def _():
        keep_ref[at] = low
        give_ref[at] = high

    @pl.when(at_ref[4] != 0)
    def _():
        keep_ref[at] = high
        give_ref[at] = low


def ff_backward(l, joined, *refs):
    at_ref, g_ref = refs[:2]
    refs = refs[2:]
    if joined:
        own_ref, other_ref, xn_ref = refs[:3]
        refs = refs[3:]
    vec_ref, x_ref, h_ref, up_ref, dn_ref = refs[:5]
    refs = refs[5:]
    if joined:
        go_ref, refs = refs[0], refs[1:]
    keep_ref, give_ref, small_ref, p_ref, dm_s, acc = refs

    def first(start, c):
        at = pl.ds(start, RB)
        g = g_ref[at, :]
        sums, s1, s2 = c
        if joined:
            dn = own_ref[at, :].astype(F32) + other_ref[at, :].astype(F32)
            dx, dg = norm_pull(dn, xn_ref[at, :], vec_ref[l + 1, 0:1, :])
            g = g + dx
            go_ref[at, :] = g
            s1 = s1 + jnp.sum(dg, 0, keepdims=True)
            s2 = s2 + jnp.sum(dn, 0, keepdims=True)
        dm = (row_mask(start, RB, at_ref[1]) * g).astype(BF)
        dm_s[at, :] = dm
        xhat, _ = normalize(x_ref[at, :])
        b = (xhat * vec_ref[l, 2:3, :] + vec_ref[l, 3:4, :]).astype(BF)
        put_by_core(at_ref, keep_ref, give_ref, (at, pl.ds(0, D)), dm, b)
        return sums + jnp.sum(dm.astype(F32), 0, keepdims=True), s1, s2

    zero = jnp.zeros((1, D), F32)
    sums, s1, s2 = row_loop(first, (zero, zero, zero))
    small_ref[...] = jnp.zeros_like(small_ref)
    for i, row in enumerate((s1, s2, sums)):
        small_ref[i : i + 1, :] = my_lanes(at_ref, row)
    for j in range(FH // FC):
        part = slice(j * FC, (j + 1) * FC)
        h = h_ref[:, part]
        half, t, hh, c0 = gelu_parts(h)
        e = (h * half).astype(BF)
        slope = half + 0.5 * c0 * h * (1.0 - t * t) * (1.0 + 3 * 0.044715 * hh)
        dh = (dot_nt(dm_s[...], dn_ref[l, part, :]) * slope).astype(BF)
        put_by_core(at_ref, keep_ref, give_ref, (slice(None), pl.ds(D + j * FC, FC)), e, dh)
        sums = jnp.sum(dh.astype(F32), 0, keepdims=True)
        for i in range(FC // C):
            small_ref[3 + j * FC // C + i : 4 + j * FC // C + i, :] = sums[:, i * C : (i + 1) * C]
        total = dot_nt(dh, up_ref[l, :, part])
        if j == 0:
            acc[...] = total
        else:
            acc[...] += total
    p_ref[...] = acc[...].astype(BF)


FIRST, SECOND = 5, 6
WIDE = 3 * D


class Swapped:
    def __init__(self, at_ref):
        self.at_ref = at_ref

    def __getitem__(self, i):
        return self.at_ref[{FIRST: SECOND, SECOND: FIRST}.get(i, i)]


def put_pieces(at_ref, ref, value):
    for n in range(4):
        ref[lax.rem(n - at_ref[SECOND] + 4, 4), pl.ds(0, PIECE)] = value[n * PIECE : (n + 1) * PIECE]


def ff_weights(at_ref, mine_ref, got_ref, *outs):
    for k, out_ref in enumerate(outs):
        block = lax.rem(at_ref[FIRST] + k, 4)
        lanes = pl.ds(pl.multiple_of(D + block * 4 * PIECE, 128), 4 * PIECE)
        total = sum(dot_tn(ref[:, lanes], ref[:, pl.ds(0, D)]) for ref in (mine_ref, got_ref))
        put_pieces(at_ref, out_ref, total.astype(BF))


def mixer_backward(
    l, last, at_ref, g_in_ref, own_ref, other_ref, x1_ref, x0_ref, u_ref, qs_ref, g_ref, ks_ref, vec_ref, inw_ref, outw_ref,
    sw_ref, sb_ref, skip_ref, table_ref,
    go_ref, small_ref, dk_ref, p_ref, keep_ref, give_ref, dy_ref, a_ref, z_ref, du_ref, dz_s, dg_s, w1_s, w2_s, dw0_s, rhs_e, rhs_o, se, so, rhs2_e, rhs2_o, inv_s,
):
    small_ref[...] = jnp.zeros_like(small_ref)

    def first(start, c):
        at = pl.ds(start, RB)
        sums, s1, s2 = c
        dn = own_ref[at, :].astype(F32) + other_ref[at, :].astype(F32)
        dx, dg = norm_pull(dn, x1_ref[at, :], vec_ref[l, 2:3, :])
        g = g_in_ref[at, :] + dx
        go_ref[at, :] = g
        dy = (row_mask(start, RB, at_ref[1]) * g).astype(BF)
        dy_ref[at, :] = dy
        xhat, _ = normalize(x0_ref[at, :])
        a_ref[at, :] = (xhat * vec_ref[l, 0:1, :] + vec_ref[l, 1:2, :]).astype(BF)
        return (
            sums + jnp.sum(dy.astype(F32), 0, keepdims=True),
            s1 + jnp.sum(dg, 0, keepdims=True),
            s2 + jnp.sum(dn, 0, keepdims=True),
        )

    zero = jnp.zeros((1, D), F32)
    sums, s1, s2 = row_loop(first, (zero, zero, zero))
    for i, row in enumerate((s1, s2, sums)):
        small_ref[i : i + 1, :] = my_lanes(at_ref, row)
    dz_s[...] = dot_nt(dy_ref[...], outw_ref[l])
    halves = (pl.ds(0, H), pl.ds(H, H))
    for b in range(C // 128):
        at = lanes_of(b)
        w0, w1, w2 = short_conv(u_ref, sw_ref.at[l], sb_ref.at[l], b)
        dskip = 0.0
        for i, (rows, rhs) in enumerate(zip(halves, (rhs_e, rhs_o))):
            dz, g = dz_s[rows, at], g_ref[rows, at]
            z_ref[rows, at] = (g * w0[i]).astype(BF)
            dw0_s[rows, at] = dz * g
            dg = dz * w0[i]
            dg_s[rows, at] = dg
            dskip = dskip + jnp.sum(dg * (w2[i] * w1[i]), 0, keepdims=True)
            w1_s[rows, at] = w1[i]
            w2_s[rows, at] = w2[i]
            put_split(rhs, dg, 0, at)
        small_ref[18:19, at] = dskip
    se[...] = dot(table_ref[FORWARD_EVEN], rhs_e[...])
    so[...] = dot(table_ref[FORWARD_ODD], rhs_o[...])
    for b in range(C // 128):
        at = lanes_of(b)
        spec = butterfly(se, so, at)
        put_inverse(rhs2_e, rhs2_o, spectrum_product(spec, [ks_ref[l, i, :, at] for i in range(4)], True), at)
        put_inverse(
            rhs2_e, rhs2_o, spectrum_product(spec, [qs_ref[i, :, at] for i in range(4)], True), pl.ds(C + b * 128, 128)
        )
    inv_s[pl.ds(0, H), :] = dot(table_ref[INVERSE_EVEN], rhs2_e[...])
    inv_s[pl.ds(H, H), :] = dot(table_ref[INVERSE_ODD], rhs2_o[...])
    dk_ref[...] = inv_s[:, pl.ds(C, C)]
    for b in range(C // 128):
        at = lanes_of(b)
        dw = [[dw0_s[rows, at] for rows in halves], [], []]
        for rows in halves:
            dq = inv_s[rows, at] + skip_ref[l, 0:1, at] * dg_s[rows, at]
            dw[1].append(dq * w2_s[rows, at])
            dw[2].append(dq * w1_s[rows, at])
        for s in range(3):
            to = lanes_of(s * (C // 128) + b)
            ue, uo = u_ref[halves[0], to], u_ref[halves[1], to]
            t0, t1, t2 = (sw_ref[l, j : j + 1, to] for j in range(3))
            de, do = dw[s]
            de_u, do_u = up_one(de), up_one(do)
            due = (t2 * de + t1 * do + t0 * de_u).astype(BF)
            duo = (t2 * do + t1 * de_u + t0 * do_u).astype(BF)
            du_ref[halves[0], to] = due
            du_ref[halves[1], to] = duo
            uo_d = down_one(uo)
            small_ref[3 + s : 4 + s, at] = jnp.sum(due.astype(F32) + duo.astype(F32), 0, keepdims=True)
            taps = de * down_one(ue) + do * uo_d, de * uo_d + do * ue, de * ue + do * uo
            for j, tap in enumerate(taps):
                small_ref[6 + 3 * j + s : 7 + 3 * j + s, at] = jnp.sum(tap, 0, keepdims=True)
            small_ref[15 + s : 16 + s, at] = jnp.sum(de + do, 0, keepdims=True)
    part = dot_nt(du_ref[:, pl.ds(0, C)], inw_ref[l, 0])
    for s in range(1, 3):
        part += dot_nt(du_ref[:, pl.ds(s * C, C)], inw_ref[l, s])
    p_ref[...] = part.astype(BF)

    def spread(start, c):
        rows = pl.ds(start, RB)
        a, dy, z = a_ref[rows, :], dy_ref[rows, :], z_ref[rows, :]
        du = [du_ref[rows, pl.ds(s * C, C)] for s in range(3)]
        lane = 0
        for low, high in ((a, a), (du[0], du[2]), (a, dy), (du[1], z)):
            put_by_core(at_ref, keep_ref, give_ref, (rows, pl.ds(lane, low.shape[1])), low, high)
            lane += low.shape[1]
        return c

    row_loop(spread)
    if last:

        def terms(start, c):
            at = pl.ds(start, RB)
            dn = p_ref[at, :].astype(F32)
            xhat, _ = normalize(x0_ref[at, :])
            return c[0] + jnp.sum(dn * xhat, 0, keepdims=True), c[1] + jnp.sum(dn, 0, keepdims=True)

        s1, s2 = row_loop(terms, (zero, zero))
        for i, row in enumerate((s1, s2)):
            for half in range(2):
                small_ref[20 + 2 * i + half : 21 + 2 * i + half, :] = row[:, half * C : (half + 1) * C]


def put_split_rows(value):
    hi = value.astype(BF).astype(F32)
    return jnp.concatenate([hi, value - hi], 0).astype(BF)


def mixer_weights(packed, at_ref, mine_ref, got_ref, *refs):
    if packed:
        pack_refs, refs = refs[:2], refs[2:]
    for k, out_ref in enumerate(refs):
        block = lax.rem(at_ref[FIRST] + k, 4)
        left = pl.multiple_of(jnp.where(block < 2, block, block + 1) * C, 128)
        right = pl.multiple_of(jnp.where(block < 2, D, 2 * D + C), 128)
        total = sum(dot_tn(ref[:, pl.ds(left, C)], ref[:, pl.ds(right, C)]) for ref in (mine_ref, got_ref))
        put_pieces(at_ref, out_ref, total.astype(BF))
        if packed:
            for n in range(4):
                rows = pl.ds(pl.multiple_of(block * 32 + n * 8, 8), 8)
                value = pack_refs[0][rows, :] + pack_refs[1][rows, :]
                out_ref[lax.rem(n - at_ref[SECOND] + 4, 4), pl.ds(PIECE, 16)] = put_split_rows(value)


def add_parts(count, sides, *refs):
    ins, outs = refs[:count], refs[count:]
    lane = 0
    for side in range(sides):
        some = ins[side * count // sides : (side + 1) * count // sides]
        lanes = slice(lane, lane + some[0].shape[-1])
        lane = lanes.stop
        for i, out in enumerate(outs):
            total = functools.reduce(jnp.add, [(r[i] if len(outs) > 1 else r[...]).astype(F32) for r in some])
            rows = (slice(None),) * (total.ndim - 2)
            out[rows + (slice(0, PIECE), lanes)] = total[rows + (slice(0, PIECE),)].astype(BF)
            if total.shape[-2] > PIECE:
                for n in range(total.shape[0] if total.ndim > 2 else 1):
                    value = total[n] if total.ndim > 2 else total
                    value = value[PIECE : PIECE + 8] + value[PIECE + 8 : PIECE + 16]
                    to = (n, slice(PIECE, PIECE + 16)) if total.ndim > 2 else slice(PIECE, PIECE + 16)
                    out[to] = put_split_rows(value)


def gather_block(at_ref, ref, block, tmp, pack_ref=None, first=0):
    for m in range(4):
        if len(ref.shape) == 5:
            by_x = (at_ref[4] == 0) != isinstance(at_ref, Swapped)
            at = 0, jnp.where(by_x, m, block), jnp.where(by_x, block, m)
        else:
            at = lax.rem(at_ref[FIRST] - block + 4, 4), lax.rem(at_ref[SECOND] - m + 4, 4)
        tmp[pl.ds(m * PIECE, PIECE), :] = ref[at + (slice(0, PIECE),)].astype(tmp.dtype)
        if pack_ref is not None:
            extra = ref[at + (slice(PIECE, PIECE + 16),)].astype(F32)
            pack_ref[pl.ds(pl.multiple_of(first + m * 8, 8), 8), :] = extra[:8] + extra[8:]


def gather_half(at_ref, half, refs, *args):
    own = at_ref[4] == half
    pl.when(own)(lambda: gather_block(at_ref, refs[0], *args))
    pl.when(jnp.logical_not(own))(lambda: gather_block(Swapped(at_ref), refs[1], *args))


def place_ff(at_ref, *refs):
    ins, (gup_ref, gdn_ref, mark_ref, tmp) = refs[:2], refs[-4:]
    mark_ref[...] = jnp.zeros_like(mark_ref)
    block = pl.program_id(0)
    gather_half(at_ref, 0, ins, block, gdn_ref.at[0])
    gather_half(at_ref, 1, ins, block, tmp)
    gup_ref[0] = tmp[...].T.astype(F32)


def place_mixer(packed, at_ref, *refs):
    ins, outs, mark_ref, tmp = refs[:2], refs[2:-2], refs[-2], refs[-1]
    mark_ref[...] = jnp.zeros_like(mark_ref)
    gin_ref, gout_ref = outs[:2]
    pack_ref = outs[2] if packed else None
    step = pl.program_id(0)
    for i in range(2):
        block = lax.rem(step, 2) * 2 + i
        first = step * 64 + i * 32

        @pl.when(step < 3)
        def _():
            to = gin_ref.at[0, 0, pl.ds(i * C, C), :]
            gather_half(at_ref, step // 2, ins, block, to, pack_ref, first)

        @pl.when(step == 3)
        def _():
            gather_half(at_ref, 1, ins, block, tmp, pack_ref, first)
            gout_ref[0, :, pl.ds(i * C, C)] = tmp[...].T.astype(F32)


PACK = 256
SHARED = 72
LAYER_ROWS = 92


def pack_small(at_ref, gnet_ref, gout_ref, *refs):
    keep_ref, give_ref, out_ref = refs[-3:]
    out_ref[...] = jnp.zeros_like(out_ref)
    out_ref[0:NET, :] = gnet_ref[...]
    out_ref[NET : NET + 4, :] = refs[1][20:24, :]
    for l in range(2):
        ff_ref, mixer_ref = refs[2 * l : 2 * l + 2]
        row = SHARED + LAYER_ROWS * l
        if l > 0:
            out_ref[row : row + 2, :] = refs[0][0:2, :]
        out_ref[row + 2 : row + 4, :] = mixer_ref[0:2, :]
        out_ref[row + 4 : row + 5, :] = ff_ref[2:3, :]
        out_ref[row + 5 : row + 6, :] = mixer_ref[2:3, :]
        out_ref[row + 6 : row + 10, :] = ff_ref[3:7, :]
        out_ref[row + 10 : row + 26, :] = mixer_ref[3:19, :]
        out_ref[row + 26 : row + 90, :] = gout_ref[l]
    put_by_core(at_ref, keep_ref, give_ref, slice(None), out_ref[: PACK // 2], out_ref[PACK // 2 :])


def unpack_small(
    at_ref, pack_ref, other_ref, gain_ref, bias_ref, inb_ref, sw_ref, sb_ref, first_ref, inner_ref, fbias_ref, fout_ref,
    skip_ref, outb_ref, upb_ref, dnb_ref, net_s,
):
    net_s[...] = pack_ref[0:SHARED, :] + other_ref[...]
    for l in range(2):
        row = SHARED + LAYER_ROWS * l
        layer = slice(l, l + 1)
        for i, ref in enumerate((gain_ref, bias_ref)):
            low, high = NET + 2 * i, NET + 2 * i + 1
            if l == 0:
                value = jnp.where(at_ref[0] == 0, net_s[low : low + 1, :], net_s[high : high + 1, :])
            else:
                value = pack_ref[row + i : row + i + 1, :]
            ref[l, 0:1, :] = value
            ref[l, 1:2, :] = pack_ref[row + 2 + i : row + 3 + i, :]
        dnb_ref[layer, :] = pack_ref[row + 4 : row + 5, :]
        outb_ref[layer, :] = pack_ref[row + 5 : row + 6, :]
        for i in range(4):
            upb_ref[layer, i * C : (i + 1) * C] = pack_ref[row + 6 + i : row + 7 + i, :]
        for s in range(3):
            inb_ref[s, layer, :] = pack_ref[row + 10 + s : row + 11 + s, :]
            sb_ref[s, layer, :] = pack_ref[row + 22 + s : row + 23 + s, :]
            for j in range(3):
                sw_ref[j, s, layer, :] = pack_ref[row + 13 + 3 * j + s : row + 14 + 3 * j + s, :]
        skip_ref[layer, :] = pack_ref[row + 25 : row + 26, :]
        fout_ref[l] = pack_ref[row + 26 : row + 90, :]
        for i in range(2):
            inner_ref[l, i] = net_s[0:NET, i * 128 + l * NET : i * 128 + (l + 1) * NET]
        lanes = slice(256 + l * NET, 256 + (l + 1) * NET)
        for r in range(EMB):
            first_ref[r, layer, :] = net_s[r : r + 1, lanes]
        for i in range(3):
            fbias_ref[i, layer, :] = net_s[40 + i : 41 + i, lanes]


def sds(shape, dtype=F32):
    return jax.ShapeDtypeStruct(shape, dtype)


def params(us, mib=32):
    return dict(
        compiler_params=pltpu.CompilerParams(vmem_limit_bytes=mib * 2**20),
        cost_estimate=pl.CostEstimate(flops=int(us * 1e9), bytes_accessed=10000, transcendentals=0),
    )


SMEM = pl.BlockSpec(memory_space=pltpu.SMEM)
WHOLE = pl.BlockSpec(memory_space=pltpu.VMEM)
ANY = pl.BlockSpec(memory_space=pl.ANY)
SLOTS = pltpu.VMEM((C // 128, T, 128), F32)


def layer_of(x, l):
    rest = x.ndim - 1
    return pl.BlockSpec((1,) + x.shape[1:], lambda *_: (l,) + (0,) * rest, pipeline_mode=pl.Buffered(1))


def fixed(shape):
    return pl.BlockSpec(shape, lambda *_: (0,) * len(shape))


def spectrum_scratch():
    return [pltpu.VMEM((3 * H, C), BF)] * 2 + [pltpu.VMEM((T, C), F32)] * 2


def run_filter_backward(at, inner, out, sines, cosines, dks):
    return pl.pallas_call(
        filter_backward,
        in_specs=[SMEM] + [WHOLE] * 7,
        out_specs=[WHOLE] * 2,
        out_shape=[sds((2, NET, C)), sds((NET, C))],
        name="filter_backward",
        **params(5, 8),
    )(at, FEATS, inner, out, sines, cosines, *dks)


def run_arrange(at, own, other):
    return pl.pallas_call(
        arrange,
        in_specs=[SMEM, WHOLE, WHOLE],
        out_specs=WHOLE,
        out_shape=sds((T, D)),
        scratch_shapes=[SLOTS],
        name="arrange",
        **params(0.2, 6),
    )(at, own, other)


def run_finish_result(at, x, own, other, vec, l):
    return pl.pallas_call(
        finish_result,
        grid=(1,),
        in_specs=[SMEM, WHOLE, WHOLE, WHOLE, layer_of(vec, l)],
        out_specs=WHOLE,
        out_shape=sds((T, C), BF),
        scratch_shapes=[pltpu.VMEM((T, D), F32), SLOTS],
        name="finish_result",
        **params(2, 8),
    )(at, x, own, other, vec)


def run_finish_grad(at, g, own, other, x, vec, l):
    return pl.pallas_call(
        finish_grad,
        grid=(1,),
        in_specs=[SMEM, WHOLE, WHOLE, WHOLE, WHOLE, layer_of(vec, l)],
        out_specs=WHOLE,
        out_shape=sds((T, C)),
        scratch_shapes=[pltpu.VMEM((T, D), F32), SLOTS],
        name="finish_grad",
        **params(2.6, 8),
    )(at, g, own, other, x, vec)


def first_forward(
    at_ref, own_ref, other_ref, feats_ref, first_ref, inner_ref, bias_ref, out_ref,
    vec_ref, inw_ref, inb_ref, sw_ref, sb_ref, skip_ref, table_ref, outw_ref,
    x_ref, ks_ref, sin_ref, cos_ref, both_ref, wide_ref, u_ref, qs_ref, g_ref, p_ref,
    slots, first_s, bias_s, k_s, *scratch,
):
    rhs_e, rhs_o, se, so = scratch[3:7]
    filter_forward(
        at_ref, feats_ref, first_ref, inner_ref, bias_ref, out_ref, table_ref,
        ks_ref, sin_ref, cos_ref, both_ref, wide_ref, first_s, bias_s, k_s, rhs_e, rhs_o, se, so,
    )
    arrange(at_ref, own_ref, other_ref, x_ref, slots)
    mixer_forward(
        0, False, at_ref, x_ref, vec_ref, inw_ref, inb_ref, sw_ref, sb_ref, ks_ref, skip_ref, table_ref, outw_ref,
        u_ref, qs_ref, g_ref, p_ref, *scratch,
    )


def mixer_forward_scratch():
    return (
        [pltpu.VMEM((T, D), BF), pltpu.VMEM((T, C), F32), pltpu.VMEM((T, C), F32)]
        + spectrum_scratch()
        + [pltpu.VMEM((6 * H, C), BF)] * 2
        + [pltpu.VMEM((T, C), BF)]
    )


def run_first_forward(at, own, other, filters, vec, inw, inb, sw, sb, skip, outw):
    args = [at, own, other, FEATS, *filters, vec, inw, inb, sw, sb, skip, TABLE, outw]
    outs = [
        sds((T, D)), sds((2, 4, H, C)), sds((3, T, 128)), sds((3, T, 128)), sds((2, 128, 128)), sds((2, 128, C)),
        sds((T, 3 * C)), sds((4, H, C)), sds((T, C)), sds((T, D), BF),
    ]
    return pl.pallas_call(
        first_forward,
        in_specs=[SMEM] + [WHOLE] * (len(args) - 1),
        out_specs=[WHOLE] * len(outs),
        out_shape=outs,
        scratch_shapes=[SLOTS, pltpu.VMEM((128, 128), F32), pltpu.VMEM((8, 128), F32), pltpu.VMEM((T, C), F32)]
        + mixer_forward_scratch(),
        name="first_forward",
        **params(13, 14),
    )(*args)


def run_mixer_forward(l, joint, at, x, vec, inw, inb, sw, sb, ks, skip, outw):
    joined = joint is not None
    args = [at, x] + (list(joint) + [vec] if joined else [])
    args += [vec, inw, inb, sw, sb, ks, skip, TABLE, outw]
    outs = ([sds((T, D))] if joined else []) + [sds((T, 3 * C)), sds((4, H, C)), sds((T, C)), sds((T, D), BF)]
    return pl.pallas_call(
        functools.partial(mixer_forward, l, joined),
        in_specs=[SMEM] + [WHOLE] * (len(args) - 1),
        out_specs=[WHOLE] * len(outs),
        out_shape=outs,
        scratch_shapes=mixer_forward_scratch(),
        name="mixer_forward",
        **params(6, 10),
    )(*args)


FC = 768


def run_ff_forward(l, last, at, x, own, other, vec, up, upb, dn, after):
    return pl.pallas_call(
        functools.partial(body_without, functools.partial(ff_forward, l, last), 8, len(after)),
        in_specs=[SMEM] + [WHOLE] * 7 + [ANY] * len(after),
        out_specs=[WHOLE] * (4 if last else 3),
        out_shape=[sds((T, D)), sds((T, FH))] + ([sds((T, C), BF)] * 2 if last else [sds((T, D), BF)]),
        scratch_shapes=[pltpu.VMEM((T, D), BF), pltpu.VMEM((T, D), F32)],
        name="ff_forward",
        **params(6, 16),
    )(at, x, own, other, vec, up, upb, dn, *after)


def run_ff_backward(l, at, g, joint, x, h, vec, up, dn, after):
    joined = joint is not None
    args = [at, g] + (list(joint) if joined else []) + [vec, x, h, up, dn]
    outs = [sds((T, D))] if joined else []
    outs += [sds((T, WIDE), BF), sds((T, WIDE), BF), sds((8, C)), sds((T, D), BF)]
    return pl.pallas_call(
        functools.partial(body_without, functools.partial(ff_backward, l, joined), len(args), len(after)),
        in_specs=[SMEM] + [WHOLE] * (len(args) - 1) + [ANY] * len(after),
        out_specs=[WHOLE] * len(outs),
        out_shape=outs,
        scratch_shapes=[pltpu.VMEM((T, D), BF), pltpu.VMEM((T, D), F32)],
        name="ff_backward",
        **params(8, 16),
    )(*args, *after)


def run_ff_weights(at, mine, got):
    return pl.pallas_call(
        ff_weights,
        in_specs=[SMEM, WHOLE, WHOLE],
        out_specs=[WHOLE] * 4,
        out_shape=[sds((4, PIECE, D), BF)] * 4,
        name="ff_weights",
        **params(3, 12),
    )(at, mine, got)


def run_mixer_backward(l, last, at, g_in, own, other, x1, x0, u, qs, g, ks, vec, inw, outw, sw, sb, skip, after):
    args = [at, g_in, own, other, x1, x0, u, qs, g, ks, vec, inw, outw, sw, sb, skip, TABLE]
    outs = [
        sds((T, D)), sds((24, C)), sds((T, C)), sds((T, D), BF), sds((T, WIDE), BF), sds((T, WIDE), BF),
    ]
    tc = pltpu.VMEM((T, C), F32)
    return pl.pallas_call(
        functools.partial(body_without, functools.partial(mixer_backward, l, last), len(args), len(after)),
        in_specs=[SMEM] + [WHOLE] * (len(args) - 1) + [ANY] * len(after),
        out_specs=[WHOLE] * len(outs),
        out_shape=outs,
        scratch_shapes=[
            pltpu.VMEM((T, D), BF), pltpu.VMEM((T, D), BF), pltpu.VMEM((T, C), BF), pltpu.VMEM((T, 3 * C), BF),
            tc, tc, tc, tc, tc, *spectrum_scratch(),
            pltpu.VMEM((6 * H, 2 * C), BF), pltpu.VMEM((6 * H, 2 * C), BF), pltpu.VMEM((T, 2 * C), F32),
        ],
        name="mixer_backward",
        **params(10, 19),
    )(*args, *after)


def run_mixer_weights(at, mine, got, pack):
    rows = PIECE + (16 if pack else 0)
    return pl.pallas_call(
        functools.partial(mixer_weights, bool(pack)),
        in_specs=[SMEM] + [WHOLE] * (2 + len(pack)),
        out_specs=[WHOLE] * 4,
        out_shape=[sds((4, rows, C), BF)] * 4,
        name="mixer_weights",
        **params(2.4, 12),
    )(at, mine, got, *pack)


def run_add(parts, count, after=(), sides=1):
    shape = parts[0].shape[1:] if count > 1 else parts[0].shape
    width = sum(p.shape[-1] for p in parts[:: len(parts) // sides])
    made = pl.pallas_call(
        functools.partial(body_without, functools.partial(add_parts, len(parts), sides), len(parts), len(after)),
        in_specs=[WHOLE] * len(parts) + [ANY] * len(after),
        out_specs=[WHOLE] * count,
        out_shape=[sds(shape[:-1] + (width,), BF)] * count,
        name="add_parts",
        **params(0.6, 8),
    )(*parts, *after)
    return list(made)


def run_behind(arrays, after, mib=4, us=0.1):
    count = len(arrays)
    return pl.pallas_call(
        lambda *refs: None,
        in_specs=[ANY] * (count + len(after)),
        out_specs=[ANY] * count,
        out_shape=[sds(x.shape, x.dtype) for x in arrays],
        input_output_aliases={i: i for i in range(count)},
        name="behind",
        **params(us, mib),
    )(*arrays, *after)


def run_place(body, at, ins, place, into, shapes, out_specs, steps, width, name):
    aliases = {} if into is None else {3: 0, 4: 1}
    into = [] if into is None else list(into)
    return pl.pallas_call(
        functools.partial(body_without, body, 3, len(into)),
        grid=(steps,),
        in_specs=[SMEM] + [lane_block(m.shape, width, place) for m in ins] + [ANY] * len(into),
        out_specs=out_specs + [fixed((8, 128))],
        out_shape=[sds(s) for s in shapes] + [sds((8, 128))],
        scratch_shapes=[pltpu.VMEM((4 * PIECE, width), BF)],
        input_output_aliases=aliases,
        name=name,
        **params(5, 20),
    )(at, *ins, *into)


def lane_block(shape, width, place):
    return pl.BlockSpec(shape[:-1] + (width,), lambda *_: (0,) * (len(shape) - 1) + (place,))


def body_without(body, first, count, *refs):
    body(*refs[:first], *refs[first + count :])


def run_place_ff(l, layers, at, ins, place, into):
    specs = [
        pl.BlockSpec((1, D, 4 * PIECE), lambda p: (l, 0, p)),
        pl.BlockSpec((1, 4 * PIECE, D), lambda p: (l, p, 0)),
    ]
    return run_place(place_ff, at, ins, place, into, [(layers, D, FH), (layers, FH, D)], specs, 4, D, "place_ff")


def run_place_mixer(l, layers, at, ins, place, into):
    packed = ins[0].shape[-2] > PIECE
    specs = [
        pl.BlockSpec((1, 1, D, C), lambda n: (l, jnp.minimum(n, 2), 0, 0)),
        pl.BlockSpec((1, C, D), lambda n: (l, 0, 0)),
    ] + [fixed((PACK, C))] * packed
    shapes = [(layers, 3, D, C), (layers, C, D)] + [(PACK, C)] * packed
    body = functools.partial(place_mixer, packed)
    return run_place(body, at, ins, place, into, shapes, specs, 4, C, "place_mixer")


SWAP = [(0, 1), (1, 0)]


def swap(x, axis):
    return lax.ppermute(x, axis, SWAP)


def shift(x, axis, k):
    pairs = []
    for y, x_at, c in np.ndindex(4, 4, 2):
        along_x = (axis == FIRST) == (c == 0)
        to = (y, (x_at + k) % 4) if along_x else ((y + k) % 4, x_at)
        pairs.append(((y * 4 + x_at) * 2 + c, (to[0] * 4 + to[1]) * 2 + c))
    return lax.ppermute(x, ("y", "x", "c"), pairs)


def send_first(blocks):
    return [blocks[0]] + [shift(blocks[k], FIRST, k) for k in range(1, 4)]


def sum_first(*gradients, after=()):
    return run_add([p for came in gradients for p in came], 4, after, len(gradients))


def send_second(pieces):
    return [pieces[0]] + [shift(pieces[m], SECOND, m) for m in range(1, 4)]


def sum_second(came, after=()):
    return run_add(came, 1, after)[0]


def sum_near(piece, after=()):
    return run_add([piece, swap(piece, "zl")], 1, after)[0]


def gather_second(piece, after):
    came = [shift(piece, SECOND, m) for m in range(1, 4)]
    return jnp.stack([piece] + list(run_behind(came, after)))


def gather_first(row, after):
    came = [shift(row, FIRST, k) for k in range(1, 4)]
    return jnp.stack([row] + list(run_behind(came, after)))


def gather_plane(piece, after):
    mine = lax.all_gather(piece, ("y", "x"), axis=0, tiled=False)
    mine = mine.reshape(1, 4, 4, *piece.shape)
    [mine] = run_behind([mine], after, 56)
    return [mine, swap(mine, "c")]


def run_pack_small(at, gnet, gout, small):
    return pl.pallas_call(
        pack_small,
        in_specs=[SMEM] + [WHOLE] * (2 + len(small)),
        out_specs=[WHOLE] * 2,
        out_shape=[sds((PACK // 2, C))] * 2,
        scratch_shapes=[pltpu.VMEM((PACK, C), F32)],
        name="pack_small",
        **params(0.6, 4),
    )(at, gnet, gout, *small)


def run_unpack_small(at, pack, other):
    shapes = [
        (2, 2, C), (2, 2, C), (3, 2, C), (3, 3, 2, C), (3, 2, C), (EMB, 2, NET), (2, 2, NET, NET), (3, 2, NET),
        (2, NET, C), (2, C), (2, C), (2, FH), (2, C),
    ]
    return pl.pallas_call(
        unpack_small,
        in_specs=[SMEM, WHOLE, WHOLE],
        out_specs=[WHOLE] * len(shapes),
        out_shape=[sds(s) for s in shapes],
        scratch_shapes=[pltpu.VMEM((SHARED, C), F32)],
        name="unpack_small",
        **params(2, 4),
    )(at, pack, other)


def shards(
    tokens, lengths, norm_gain, norm_bias, in_weight, in_bias, short_weight, short_bias, filter_first, filter_inner,
    filter_biases, filter_out, filter_skip, out_weight, out_bias, up_weight, up_bias, down_weight, down_bias, cotangent,
):
    layers = norm_gain.shape[0]
    half_at = lax.axis_index("zh")
    core = lax.axis_index("c")
    x_at, y_at = lax.axis_index("x"), lax.axis_index("y")
    order = jnp.where(core == 0, x_at, y_at), jnp.where(core == 0, y_at, x_at)
    at = jnp.stack([half_at, lengths[0], x_at, y_at, core, *order]).astype(jnp.int32)

    tokens_other = swap(tokens, "zh")
    rows = jnp.stack(
        [norm_gain[:, 0], norm_bias[:, 0], norm_gain[:, 1], norm_bias[:, 1], out_bias, down_bias, out_bias, out_bias], 1
    )
    inw = in_weight.transpose(0, 2, 1, 3)
    at, rows, cotangent = run_behind([at, rows, cotangent], [], 4, 12)
    other = swap(rows, "zh")
    low = half_at == 0
    vec = jnp.concatenate([jnp.where(low, rows, other), jnp.where(low, other, rows)], 2)

    inb = in_bias.reshape(layers, 1, 3 * C)
    sw = short_weight.reshape(layers, 3, 3 * C)
    sb = short_bias.reshape(layers, 1, 3 * C)
    skip = filter_skip.reshape(layers, 1, C)
    upb = up_bias.reshape(layers, 1, FH)

    cot_other = swap(cotangent, "zh")
    grad = run_arrange(at, cotangent, cot_other)
    saved = []
    joint = None
    for l in range(layers):
        if l == 0:
            filters = filter_first, filter_inner, filter_biases, filter_out
            made = run_first_forward(at, tokens, tokens_other, filters, vec, inw, inb, sw, sb, skip, out_weight)
            x, ks, sines, cosines, inner, fout, *made = made
        else:
            x, *made = run_mixer_forward(l, joint, at, x, vec, inw, inb, sw, sb, ks, skip, out_weight)
        u, qs, g, p = made
        if l == 0:
            [p] = run_behind([p], [cot_other], 4, 5)
        after = [grad] if l == 0 else []
        last = l == layers - 1
        x1, h, *p2 = run_ff_forward(l, last, at, x, p, swap(p, "zh"), vec, up_weight, upb, down_weight, after)
        saved.append((x, u, qs, g, x1, h))
        joint = p2[0], swap(p2[-1], "zh")
        x = x1
    last_branch = joint

    joint = None
    small = [None] * layers
    waits = []
    came = {}
    for l in reversed(range(layers)):
        x0, u, qs, g, x1, h = saved[l]
        made = run_ff_backward(l, at, grad, joint, x1, h, vec, up_weight, down_weight, waits)
        if joint is not None:
            grad, made = made[0], made[1:]
        keep, give, ff_small, p = made
        p, give = run_behind([p, give], [last_branch[1]] if l == layers - 1 else came["mixer", l + 1][1:], 4, 6)
        p_other = swap(p, "zh")
        halves = run_ff_weights(at, keep, swap(give, "c"))
        came["ff", l] = send_first(halves)
        waits = list(halves)
        if l < layers - 1:
            later = send_second(sum_first(came["ff", l + 1], came["mixer", l + 1], after=[p]))
            later = sum_second(later)
            waits.append(later)
            later_other = swap(later, "zl")
        made = run_mixer_backward(
            l, l == 0, at, grad, p, p_other, x1, x0, u, qs, g, ks, vec, inw, out_weight, sw, sb, skip, waits
        )
        grad, mixer_small, dk, p, keep, give = made
        p, give = run_behind([p, give], came["ff", l][1:] + ([later_other] if l < layers - 1 else []))
        joint = (p, swap(p, "zh"), x0) if l else (p, x0)
        small[l] = (ff_small, mixer_small, dk)
        pack = ()
        if l == 0:
            later = run_add([later, later_other], 1, [p])[0]
            ff = sum_second(send_second(sum_first(came["ff", 0], after=[p])))
            gfout, gnet = run_filter_backward(at, inner, fout, sines, cosines, [s[-1] for s in small])
            gfout, gnet = run_behind([gfout, gnet], [ff])
            pack = run_pack_small(at, gnet, gfout, [m for some in small for m in some[:-1]])
            pack = pack[0], swap(pack[1], "c")
            ff = sum_near(ff, pack[1:])
        halves = run_mixer_weights(at, keep, swap(give, "c"), pack)
        came["mixer", l] = send_first(halves)
        waits = list(halves)
        if l == layers - 1:
            result = run_finish_result(at, saved[l][4], *last_branch, vec, l)
            waits.append(result)

    mixer = sum_near(sum_second(send_second(sum_first(came["mixer", 0], after=[ff]))))
    later = gather_plane(later, [mixer])
    p, x0 = joint
    [p] = run_behind([p], [mixer])
    last = jnp.concatenate([jnp.pad(ff, ((0, mixer.shape[0] - PIECE), (0, 0))), mixer], 1)
    last = gather_second(last, [])
    *ff_out, mark = run_place_ff(1, layers, at, later, 0, None)
    *mixer_out, other_mark = run_place_mixer(1, layers, at, later, 2, None)
    grad = run_finish_grad(at, grad, p, swap(p, "zh"), x0, vec, 0)
    last = gather_first(last, [grad, mark, other_mark])
    last = [last, swap(last, "c")]
    *mixer_out, pack, mark = run_place_mixer(0, layers, at, last, 2, mixer_out)
    *ff_out, mark = run_place_ff(0, layers, at, last, 0, ff_out)

    gain, shift_, inb, sw, sb, first, inner, fbias, fout, skip, outb, upb, dnb = run_unpack_small(
        at, pack, swap(pack[:SHARED], "zh")
    )
    return (
        result, grad, gain, shift_, mixer_out[0].transpose(0, 2, 1, 3), inb.transpose(1, 0, 2),
        sw.transpose(2, 0, 1, 3), sb.transpose(1, 0, 2), first.transpose(1, 0, 2), inner, fbias.transpose(1, 0, 2),
        fout, skip, mixer_out[1], outb, ff_out[0], upb, ff_out[1], dnb,
    )


def solution(mesh):
    names = ("zl", "y", "x", "c", "zh")
    fine = Mesh(mesh.devices.reshape(2, 4, 4, 2, 2), names)
    dp = ("zl", "y", "x", "c")
    rows = P(dp, "zh")
    third, fourth = P(None, None, "zh"), P(None, None, None, "zh")
    second, middle = P(None, "zh"), P(None, "zh", None)
    placed = (
        rows, P(dp), third, third, fourth, third, fourth, third, P(), P(), P(), third, second, middle, second, third,
        second, middle, second, rows,
    )
    return jax.shard_map(
        shards,
        mesh=fine,
        in_specs=placed,
        out_specs=(
            rows, rows, third, third, fourth, third, fourth, third, P(), P(), P(), third, second, middle, second, third,
            second, middle, second,
        ),
        check_vma=False,
    )
```
